128 devices in a mesh: ctx: 16 (over y, x), tp: 8 (over z, core).
Axes of the slice: x: 4, y: 4, z: 4, core: 2. Of those that a mesh axis runs over, the one named last changes fastest.
Arguments:
- query_heads: bfloat16 [8192, 4096], P('ctx', 'tp'), may hold values from -6 to 6
- key_heads: bfloat16 [8192, 2048], P('ctx', 'tp'), may hold values from -6 to 6
- value_heads: bfloat16 [8192, 2048], P('ctx', 'tp'), may hold values from -6 to 6
- doc_ids: int32 [8192], replicated, may hold values from 0 to 7, never falling along the last dimension, each value on 1 to 4096 neighbouring positions
- out_weight: bfloat16 [4096, 5376], P('tp'), may hold values from -0.75 to 0.75
- residual: bfloat16 [8192, 5376], P('ctx', 'tp'), may hold values from -32 to 32
- post_gain: float32 [5376], P('tp'), may hold values from 0.25 to 1.75
- pre_gain: float32 [5376], P('tp'), may hold values from 0.25 to 1.75
- gate_weight: bfloat16 [5376, 10752], P('ctx', 'tp'), may hold values from -0.078125 to 0.078125
- up_weight: bfloat16 [5376, 10752], P('ctx', 'tp'), may hold values from -0.078125 to 0.078125
Outputs:
- new_residual: bfloat16 [8192, 5376], P('ctx', 'tp')
- activated: bfloat16 [8192, 10752], P('ctx', 'tp')
The draws below stay inside these ranges and needn't reach their ends.
Inputs may be any that keep to these rules, and one draw needn't show every extreme that they name: doc_ids never fall along the span; a document is a run of equal ids.
All inputs are finite; a program needn't handle non-finite values.
Results may differ from the reference program's by a relative error of at most 0.03.
Values may be sent and summed in bfloat16 or wider, within the bound.
No kernel may reach another device: no remote copies, remote signals or barrier semaphores. Data moves between devices by JAX's collectives and lax.ppermute only.
A program may use at most 128 MiB of HBM per device.

```python
import math
import jax
import jax.numpy as jnp
import numpy as np
from jax import lax

D = 5376
H = 32
KV = 16
HD = 128
WINDOW = 1024
FF = 10752
TOK_DEV = 512
TOKENS = 8192
DOCS = 8
N_TP = 8


def draw_query_heads(key, part):
    base_key = jax.random.fold_in(key, 1)
    return jnp.clip(jax.random.normal(base_key, (TOKENS, H * HD), jnp.float32), -5.0, 5.0).astype(jnp.bfloat16)


def draw_key_heads(key, part):
    base_key = jax.random.fold_in(key, 3)
    return jnp.clip(jax.random.normal(base_key, (TOKENS, KV * HD), jnp.float32), -5.0, 5.0).astype(jnp.bfloat16)


def draw_residual(key, part):
    base_key = jax.random.fold_in(key, 5)
    row_key = jax.random.fold_in(key, 6)
    col_key = jax.random.fold_in(key, 7)
    base = jnp.clip(jax.random.normal(base_key, (TOKENS, D), jnp.float32), -4.0, 4.0)
    row_scale = jnp.exp(jax.random.uniform(row_key, (TOKENS, 1), jnp.float32, math.log(0.3), math.log(3.0)))
    column = jnp.arange(D).astype(jnp.float32) / D
    col_scale = 0.6 * jnp.exp(math.log(3.0) * column) * jnp.exp(jax.random.uniform(col_key, (D,), jnp.float32, -0.35, 0.35))
    return (base * row_scale * col_scale[None, :]).astype(jnp.bfloat16)


def column_ramp(key, rise):
    column = jnp.arange(D).astype(jnp.float32) / D
    jitter = jnp.exp(jax.random.uniform(key, (D,), jnp.float32, -0.3, 0.3))
    return jnp.exp(math.log(rise) * column) * jitter


def draw_out_weight(key, part):
    key = jax.random.fold_in(key, 21)
    base_key = jax.random.fold_in(key, 1)
    col_key = jax.random.fold_in(key, 2)
    fan_scale = float(H * HD) ** (-0.5)
    base = jnp.clip(jax.random.normal(base_key, (H * HD, D), jnp.float32), -4.0, 4.0)
    ramp = column_ramp(col_key, 4.0)
    return (base * fan_scale * ramp[None, :]).astype(jnp.bfloat16)


def block_scale(rng, shape, split, least, high):
    gain, own = 1.0, jax.random.fold_in(rng, 6)
    for axis_at, blocks in split:
        draws = jnp.exp(jax.random.uniform(jax.random.fold_in(own, axis_at), (blocks,), jnp.float32, least / len(split), high / len(split)))
        gain = gain * jnp.repeat(draws, shape[axis_at] // blocks).reshape([-1 if axis == axis_at else 1 for axis in range(len(shape))])
    return gain


def profile(amount, total, bound, lean):
    weights = [(1 << 20) // math.isqrt(grade ** lean) + 1 for grade in range(2, amount + 1)]
    surplus, given = total - bound - (amount - 1), [1] * (amount - 1)
    while surplus > 0:
        movable = [i for i in range(amount - 1) if given[i] < bound]
        pool, left = sum([weights[i] for i in movable]), surplus
        for i in movable:
            extra = min(bound - given[i], max(1, left * weights[i] // pool), surplus)
            given[i] = given[i] + extra
            surplus = surplus - extra
    return np.array([bound] + given)


def uneven(stream_key, number_of, total, bound, slope):
    if number_of == 2:
        one = jax.random.randint(stream_key, (), max(1, total - bound), min(bound, total - 1) + 1)
        return jnp.stack([one, total - one])
    tallies = jnp.asarray(profile(number_of, total, bound, slope), jnp.int32)
    pairs = (number_of - 1) // 2
    donor, taker = tallies[1:1 + 2 * pairs:2], tallies[2:2 + 2 * pairs:2]
    slack = jnp.minimum(donor - 1, bound - taker)
    shifted = jax.random.randint(jax.random.fold_in(stream_key, 1), (pairs,), 0, 1 << 20) % (slack + 1)
    tallies = tallies.at[1:1 + 2 * pairs:2].set(donor - shifted).at[2:2 + 2 * pairs:2].set(taker + shifted)
    return tallies[jax.random.permutation(jax.random.fold_in(stream_key, 2), number_of)]


def bell_draw(rng, dims, spread, limit, cuts=(), held_as=jnp.bfloat16):
    drawn = spread * jax.random.normal(rng, dims, jnp.float32)
    if cuts:
        drawn = drawn * block_scale(rng, dims, cuts, -0.22, 0.18)
    return jnp.clip(drawn, -limit, limit).astype(held_as)


def setup_inputs(seed: int = 0) -> dict:
    streams_of = jax.random.split(jax.random.key(seed), 11)
    query_heads = draw_query_heads(jax.random.fold_in(streams_of[10], 71), 0)
    key_heads = draw_key_heads(jax.random.fold_in(streams_of[10], 71), 0)
    value_heads = bell_draw(streams_of[2], (TOKENS, KV * HD), 1.0, 6.0, ((0, 16), (1, 8)))
    doc_ids = jnp.searchsorted(jnp.cumsum(uneven(streams_of[3], DOCS, TOKENS, TOKENS // 2, 2)), jnp.arange(TOKENS), side="right").astype(jnp.int32)
    out_weight = draw_out_weight(jax.random.fold_in(streams_of[10], 71), 0)
    residual = draw_residual(jax.random.fold_in(streams_of[10], 71), 0)
    post_gain = jnp.clip(1.0 + 0.15 * jax.random.normal(streams_of[6], (D,), jnp.float32), 0.25, 1.75)
    pre_gain = jnp.clip(1.0 + 0.15 * jax.random.normal(streams_of[7], (D,), jnp.float32), 0.25, 1.75)
    gate_weight = bell_draw(streams_of[8], (D, FF), D ** -0.5, 0.078125, ((0, 16), (1, 8)))
    up_weight = bell_draw(streams_of[9], (D, FF), D ** -0.5, 0.078125, ((0, 16), (1, 8)))
    return dict(query_heads=query_heads, key_heads=key_heads, value_heads=value_heads, doc_ids=doc_ids, out_weight=out_weight, residual=residual, post_gain=post_gain, pre_gain=pre_gain, gate_weight=gate_weight, up_weight=up_weight)


epsilon = 1e-06

def reference(query_heads, key_heads, value_heads, doc_ids, out_weight, residual, post_gain, pre_gain, gate_weight, up_weight):
    group_size = H // KV
    score_scale = float(D // H) ** (-0.5)
    key_pad = jnp.concatenate([jnp.zeros((WINDOW, KV * HD), jnp.bfloat16), key_heads], axis=0).astype(jnp.float32)
    value_pad = jnp.concatenate([jnp.zeros((WINDOW, KV * HD), jnp.bfloat16), value_heads], axis=0).astype(jnp.float32)
    id_pad = jnp.concatenate([jnp.full((WINDOW,), -1, jnp.int32), doc_ids.astype(jnp.int32)])

    def attend(block_index):
        offset = (block_index * TOK_DEV).astype(jnp.int32)
        queries = lax.dynamic_slice_in_dim(query_heads, offset, TOK_DEV, 0).astype(jnp.float32)
        queries = queries.reshape(TOK_DEV, KV, group_size, HD)
        key_rows = lax.dynamic_slice_in_dim(key_pad, offset, WINDOW + TOK_DEV, 0).reshape(WINDOW + TOK_DEV, KV, HD)
        value_rows = lax.dynamic_slice_in_dim(value_pad, offset, WINDOW + TOK_DEV, 0).reshape(WINDOW + TOK_DEV, KV, HD)
        query_ids = lax.dynamic_slice_in_dim(doc_ids.astype(jnp.int32), offset, TOK_DEV, 0)
        key_ids = lax.dynamic_slice_in_dim(id_pad, offset, WINDOW + TOK_DEV, 0)
        query_pos = offset + jnp.arange(TOK_DEV, dtype=jnp.int32)
        key_pos = offset - WINDOW + jnp.arange(WINDOW + TOK_DEV, dtype=jnp.int32)
        allowed = (query_ids[:, None] == key_ids[None, :]) & (key_pos[None, :] <= query_pos[:, None]) & (key_pos[None, :] > query_pos[:, None] - WINDOW)
        scores = jnp.einsum('qhgd,khd->hgqk', queries, key_rows) * score_scale
        scores = jnp.where(allowed[None, None], scores, -1e+30)
        row_max = lax.optimization_barrier(jnp.max(scores, axis=-1, keepdims=True))
        weights = jnp.exp(scores - row_max)
        row_total = lax.optimization_barrier(jnp.sum(weights, axis=-1, keepdims=True))
        attn_probs = lax.optimization_barrier((weights / row_total).astype(jnp.bfloat16)).astype(jnp.float32)
        mixture = jnp.einsum('hgqk,khd->qhgd', attn_probs, value_rows)
        return mixture.astype(jnp.bfloat16).reshape(TOK_DEV, H * HD)
    attended = lax.map(attend, jnp.arange(TOKENS // TOK_DEV, dtype=jnp.int32)).reshape(TOKENS, H * HD)
    group_cols = H * HD // N_TP
    projected = jnp.zeros((TOKENS, D), jnp.float32)
    for group_index in range(N_TP):
        low = group_index * group_cols
        piece = jnp.dot(attended[:, low:low + group_cols], out_weight[low:low + group_cols], preferred_element_type=jnp.float32)
        rounded = lax.optimization_barrier(piece.astype(jnp.bfloat16))
        projected = projected + rounded.astype(jnp.float32)
    factor = lax.rsqrt(lax.optimization_barrier(jnp.mean(projected * projected, axis=1)) + epsilon)
    branch = projected * factor[:, None] * post_gain[None, :]
    new_residual = (residual.astype(jnp.float32) + branch).astype(jnp.bfloat16)
    stream = new_residual.astype(jnp.float32)
    second = lax.rsqrt(lax.optimization_barrier(jnp.mean(stream * stream, axis=1)) + epsilon)
    normed = (stream * second[:, None] * pre_gain[None, :]).astype(jnp.bfloat16)
    gate = jnp.dot(normed, gate_weight, preferred_element_type=jnp.float32)
    up_sums = jnp.dot(normed, up_weight, preferred_element_type=jnp.float32)
    activated = (jax.nn.gelu(gate, approximate=True) * up_sums).astype(jnp.bfloat16)
    return (new_residual, activated)
```

```python
import jax
import jax.numpy as jnp
from jax import lax
from jax.experimental import pallas as pl
from jax.experimental.pallas import tpu as pltpu
from jax.sharding import Mesh, PartitionSpec as P

D = 5376
HD = 128
WINDOW = 1024
EPS = 1e-06
LOG2E = 1.4426950408889634
SCALE = float(168) ** -0.5
TOK = 512
PER = 64
BF = jnp.bfloat16
F32 = jnp.float32
VM = pl.BlockSpec(memory_space=pltpu.VMEM)
SM = pl.BlockSpec(memory_space=pltpu.SMEM)
HB = pl.BlockSpec(memory_space=pl.ANY)
MB = 1 << 20


def params(mb):
    return pltpu.CompilerParams(vmem_limit_bytes=mb * MB)


def cost(flops, nbytes, trans=0):
    return pl.CostEstimate(flops=int(flops), bytes_accessed=int(nbytes), transcendentals=int(trans))


def shift(value, axis, by):
    n = lax.axis_size(axis)
    return lax.ppermute(value, axis, [(i, (i + by) % n) for i in range(n)])


def behind(value):
    n = 16
    return lax.ppermute(value, ("y", "x"), [(i, i + 1) for i in range(n - 1)])


def pack_kernel(g_ref, u_ref, o_ref):
    g, u = g_ref[...], u_ref[...]
    for j in range(7):
        lo = 192 * j
        o_ref[:, 384 * j:384 * j + 384] = jnp.concatenate(
            [g[:, lo:lo + 128], u[:, lo:lo + 128], g[:, lo + 128:lo + 192], u[:, lo + 128:lo + 192]], axis=1
        )


def pack(gate, up):
    return pl.pallas_call(
        pack_kernel,
        out_shape=jax.ShapeDtypeStruct((336, 2688), BF),
        in_specs=[VM, VM],
        out_specs=VM,
        compiler_params=params(24),
        cost_estimate=cost(0, 4 * 336 * 2688),
        name="pack",
    )(gate, up)


def attend_kernel(at_ref, q_ref, kv2_ref, kv1_ref, kv0_ref, qid_ref, kid_ref, o_ref):
    z, c = at_ref[0], at_ref[1]
    k = jnp.concatenate([kv2_ref[:, :HD], kv1_ref[:, :HD], kv0_ref[:, :HD]], axis=0)
    v = jnp.concatenate([kv2_ref[:, HD:], kv1_ref[:, HD:], kv0_ref[:, HD:]], axis=0)
    for b in range(2):
        lo = 256 * b
        qid = qid_ref[lo:lo + 256, :]
        kid = kid_ref[:, lo:lo + 1280]
        row = lax.broadcasted_iota(jnp.int32, (256, 1280), 0)
        col = lax.broadcasted_iota(jnp.int32, (256, 1280), 1)
        allowed = (qid == kid) & (col > row) & (col <= row + 1024)
        outs = []
        for h in range(2):
            q = q_ref[lo:lo + 256, HD * h:HD * h + HD]
            s = lax.dot_general(q, k[lo:lo + 1280], (((1,), (1,)), ((), ())), preferred_element_type=F32)
            s = jnp.where(allowed, s * (SCALE * LOG2E), -1e30)
            top = jnp.max(s, axis=1, keepdims=True)
            e = jnp.exp2(s - top)
            total = jnp.sum(e, axis=1, keepdims=True)
            mix = jnp.dot(e.astype(BF), v[lo:lo + 1280], preferred_element_type=F32)
            outs.append(mix / total)
        out = jnp.concatenate(outs, axis=1).astype(BF)
        for i in range(4):
            zz, cc = 2 * b + i // 2, i % 2
            o_ref[(cc + c) % 2, (zz - z + 4) % 4] = out[PER * i:PER * i + PER]


def attend(at, q, kv2, kv1, kv0, qid, kid):
    return pl.pallas_call(
        attend_kernel,
        out_shape=jax.ShapeDtypeStruct((2, 4, PER, 256), BF),
        in_specs=[SM] + [VM] * 6,
        out_specs=VM,
        compiler_params=params(32),
        cost_estimate=cost(4 * 1024 * 1280 * 128 * 1.5, 2 * MB, 1024 * 1280),
        name="attend",
    )(at, q, kv2, kv1, kv0, qid, kid)


def project_kernel(a0, a1, s0, s1, w_ref, ws_ref, p0, p1t, p1b, p2t, p2b, p3t, p3b):
    acc = jnp.dot(a0[...], w_ref[:256], preferred_element_type=F32)
    acc += jnp.dot(a1[...], w_ref[256:], preferred_element_type=F32)
    acc += jnp.dot(s0[...], ws_ref[:256], preferred_element_type=F32)
    acc += jnp.dot(s1[...], ws_ref[256:], preferred_element_type=F32)
    out = acc.astype(BF)
    p0[...] = out[:64]
    for i, ref in enumerate((p1t, p1b, p2t, p2b, p3t, p3b)):
        ref[...] = out[64 + 32 * i:96 + 32 * i]


def project(a0, a1, s0, s1, w, ws):
    width = 768
    row = lambda r: pl.BlockSpec((r, width), lambda j: (0, j))
    full = pl.BlockSpec((256, 256), lambda j: (0, 0))
    return pl.pallas_call(
        project_kernel,
        out_shape=[jax.ShapeDtypeStruct((64, D), BF)] + [jax.ShapeDtypeStruct((32, D), BF)] * 6,
        grid=(D // width,),
        in_specs=[full] * 4 + [row(512)] * 2,
        out_specs=[row(64)] + [row(32)] * 6,
        compiler_params=params(24),
        cost_estimate=cost(2 * 256 * 1024 * D, 2 * 1280 * D),
        name="project",
    )(a0, a1, s0, s1, w, ws)


def norm_kernel(p0, at_ref, ab_ref, bt_ref, bb_ref, res_ref, post_ref, pre_ref, new_ref, nrm_ref):
    for half, (a, b) in enumerate(((at_ref, bt_ref), (ab_ref, bb_ref))):
        rows = slice(32 * half, 32 * half + 32)
        owned = p0[rows].astype(F32) + a[...].astype(F32) + b[...].astype(F32)
        factor = lax.rsqrt(jnp.mean(owned * owned, axis=1, keepdims=True) + EPS)
        new = (res_ref[rows].astype(F32) + owned * factor * post_ref[...]).astype(BF)
        new_ref[rows] = new
        stream = new.astype(F32)
        second = lax.rsqrt(jnp.mean(stream * stream, axis=1, keepdims=True) + EPS)
        nrm_ref[rows] = (stream * second * pre_ref[...]).astype(BF)


def norm(*args):
    return pl.pallas_call(
        norm_kernel,
        out_shape=[jax.ShapeDtypeStruct((PER, D), BF)] * 2,
        in_specs=[VM] * 8,
        out_specs=[VM] * 2,
        compiler_params=params(24),
        cost_estimate=cost(20 * PER * D, 8 * PER * D),
        name="norm",
    )(*args)


def gated_kernel(tokens_at, *refs):
    pieces, (w_ref, o_ref, n_ref, sems) = refs[:len(tokens_at)], refs[len(tokens_at):][1:]
    where = refs[len(tokens_at)]

    @pl.when(pl.program_id(0) == 0)
    def _():
        z, c = where[0], where[1]
        copies = []
        for i, (ref, (dz, dc, part)) in enumerate(zip(pieces, tokens_at)):
            base = 64 * (2 * ((z + dz) % 4) + (c + dc) % 2)
            rows = 64
            if part is not None:
                base, rows = base + 32 * part, 32
            copies.append(pltpu.make_async_copy(ref, n_ref.at[pl.ds(pl.multiple_of(base, 32), rows)], sems.at[i]))
            copies[-1].start()
        for copy in copies:
            copy.wait()

    acc = jnp.dot(n_ref[...], w_ref[...], preferred_element_type=F32)
    last = acc[:, 256:]
    g = jnp.concatenate([acc[:, :128], last], axis=1)
    u = jnp.concatenate([acc[:, 128:256], pltpu.roll(last, 64, 1)], axis=1)
    act = 0.5 * g * (1 + jnp.tanh(0.7978845608028654 * (g + 0.044715 * (g * g * g)))) * u
    o_ref[...] = act.T[:192].astype(BF)


def gated(pieces, tokens_at, where, w):
    blocks = w.shape[1] // 384
    n = len(pieces)

    def body(*refs):
        gated_kernel(tokens_at, *refs)

    return pl.pallas_call(
        body,
        out_shape=jax.ShapeDtypeStruct((192 * blocks, TOK), BF),
        grid=(blocks,),
        in_specs=[HB] * n + [SM, pl.BlockSpec((D, 384), lambda j: (0, j))],
        out_specs=pl.BlockSpec((192, TOK), lambda j: (j, 0)),
        scratch_shapes=[pltpu.VMEM((TOK, D), BF), pltpu.SemaphoreType.DMA((n,))],
        compiler_params=params(48),
        cost_estimate=cost(2 * TOK * D * 384 * blocks, 2 * D * 384 * blocks + 2 * TOK * D),
        name="gated",
    )(*pieces, where, w)


def per_device(queries, keys, values, doc_ids, out_weight, residual, post_gain, pre_gain, gate_weight, up_weight):
    y, x, z, c = (lax.axis_index(a) for a in ("y", "x", "z", "c"))
    where = jnp.stack([z, c]).astype(jnp.int32)

    w = pack(gate_weight, up_weight)
    w_first = lax.all_gather(w[:, :1920], ("y", "x"), axis=0, tiled=True)
    w_last = lax.all_gather(w[:, 1920:], ("y", "x"), axis=0, tiled=True)

    start = (4 * y + x) * TOK
    padded = jnp.concatenate([jnp.full((2 * TOK,), -1, jnp.int32), doc_ids])
    kid = lax.dynamic_slice_in_dim(padded, start, 3 * TOK, 0)[None, :]
    qid = lax.dynamic_slice_in_dim(doc_ids, start, TOK, 0)[:, None]

    mixes = []
    for h in range(2):
        cols = slice(HD * h, HD * h + HD)
        kv0 = jnp.concatenate([keys[:, cols], values[:, cols]], axis=1)
        kv1 = behind(kv0)
        kv2 = behind(kv1)
        mixes.append(attend(where, queries[:, 256 * h:256 * h + 256], kv2, kv1, kv0, qid, kid))
    other_weight = shift(out_weight, "c", 1)
    own = [m[0].reshape(256, 256) for m in mixes]
    other = [shift(m[1].reshape(256, 256), "c", 1) for m in mixes]
    p0, p1t, p1b, p2t, p2b, p3t, p3b = project(*own, *other, out_weight, other_weight)

    up_t = shift(p2t, "z", 1)
    dn_b = shift(p2b, "z", -1)
    a_b = shift(p1b, "z", 1)
    b_t = shift(p3t, "z", -1)
    add = lambda p, q: (p.astype(F32) + q.astype(F32)).astype(BF)
    a_t = shift(add(p1t, up_t), "z", 1)
    b_b = shift(add(p3b, dn_b), "z", -1)

    mine = lax.all_to_all(residual, ("z", "c"), 0, 1, tiled=True)
    post = lax.all_gather(post_gain, ("z", "c"), axis=0, tiled=True)[None, :]
    pre = lax.all_gather(pre_gain, ("z", "c"), axis=0, tiled=True)[None, :]
    new, nrm = norm(p0, a_t, a_b, b_t, b_b, mine, post, pre)
    new_residual = lax.all_to_all(new, ("z", "c"), 1, 0, tiled=True)

    top, bottom = nrm[:32], nrm[32:]
    m_t, m_b = shift(top, "z", 1), shift(bottom, "z", 1)
    q_t, q_b = shift(top, "z", -1), shift(bottom, "z", -1)
    f_t, f_b = shift(m_t, "z", 1), shift(q_b, "z", -1)
    pieces = [nrm, m_t, m_b, q_t, q_b, f_t, f_b]
    places = [(0, None), (3, 0), (3, 1), (1, 0), (1, 1), (2, 0), (2, 1)]
    pieces += [shift(p, "c", 1) for p in pieces]
    tokens_at = [(dz, dc, part) for dc in range(2) for dz, part in places]
    act = jnp.concatenate([gated(pieces, tokens_at, where, w_first), gated(pieces, tokens_at, where, w_last)], axis=0)
    return new_residual, act.T


def solution(mesh):
    fine = Mesh(mesh.devices.reshape(4, 4, 4, 2), ("y", "x", "z", "c"))
    t, f = ("y", "x"), ("z", "c")
    in_specs = (P(t, f), P(t, f), P(t, f), P(), P(f, None), P(t, f), P(f), P(f), P(t, f), P(t, f))
    return jax.shard_map(per_device, mesh=fine, in_specs=in_specs, out_specs=(P(t, f), P(t, f)), check_vma=False)
```

```python
import jax
import jax.numpy as jnp
from jax import lax
from jax.experimental import pallas as pl
from jax.experimental.pallas import tpu as pltpu
from jax.sharding import Mesh, PartitionSpec as P

D = 5376
HD = 128
WINDOW = 1024
EPS = 1e-06
LOG2E = 1.4426950408889634
SCALE = float(168) ** -0.5
TOK = 512
PER = 64
BF = jnp.bfloat16
F32 = jnp.float32
VM = pl.BlockSpec(memory_space=pltpu.VMEM)
SM = pl.BlockSpec(memory_space=pltpu.SMEM)
HB = pl.BlockSpec(memory_space=pltpu.HBM)
MB = 1 << 20


def params(mb):
    return pltpu.CompilerParams(vmem_limit_bytes=mb * MB)


def cost(flops, nbytes, trans=0):
    return pl.CostEstimate(flops=int(flops), bytes_accessed=int(nbytes), transcendentals=int(trans))


def shift(value, axis, by):
    n = lax.axis_size(axis)
    return lax.ppermute(value, axis, [(i, (i + by) % n) for i in range(n)])


def behind(value):
    n = 16
    return lax.ppermute(value, ("y", "x"), [(i, i + 1) for i in range(n - 1)])


SPLIT = 8
REST = 2688 - 256 * SPLIT


def pack_kernel(g_ref, u_ref, o_ref, r_ref):
    g, u = g_ref[...], u_ref[...]
    for j in range(10):
        lo = 128 * j
        pair = jnp.concatenate([g[:, lo:lo + 128], u[:, lo:lo + 128]], axis=1)
        if j < SPLIT:
            o_ref[:, 256 * j:256 * j + 256] = pair
        else:
            r_ref[:, 256 * (j - SPLIT):256 * (j - SPLIT) + 256] = pair
    r_ref[:, REST - 128:] = jnp.concatenate([g[:, 1280:], u[:, 1280:]], axis=1)


def pack(gate, up):
    return pl.pallas_call(
        pack_kernel,
        out_shape=[jax.ShapeDtypeStruct((336, 256 * SPLIT), BF), jax.ShapeDtypeStruct((336, REST), BF)],
        in_specs=[VM, VM],
        out_specs=[VM, VM],
        compiler_params=params(16),
        cost_estimate=cost(0, 4 * 336 * 2688),
        name="pack",
    )(gate, up)


def ring(value, by, phase):
    pairs = []
    for y in range(4):
        for x in range(4):
            for z in range(4):
                for c in range(2):
                    along_x = (c == 0) == (phase == 0)
                    yy, xx = (y, (x + by) % 4) if along_x else ((y + by) % 4, x)
                    pairs.append((((y * 4 + x) * 4 + z) * 2 + c, ((yy * 4 + xx) * 4 + z) * 2 + c))
    return lax.ppermute(value, ("y", "x", "z", "c"), pairs)


def ring_gather(own, cut, phase):
    m, p = ring(own, 1, phase), ring(own, -1, phase)
    top, bottom = ring(m[:cut], 1, phase), ring(p[cut:], -1, phase)
    return m, p, top, bottom


def attend_kernel(at_ref, q_ref, kv2_ref, kv1_ref, kv0_ref, qid_ref, kid_ref, o_ref):
    z, c = at_ref[0], at_ref[1]
    k = jnp.concatenate([kv2_ref[:, :HD], kv1_ref[:, :HD], kv0_ref[:, :HD]], axis=0)
    v = jnp.concatenate([kv2_ref[:, HD:], kv1_ref[:, HD:], kv0_ref[:, HD:]], axis=0)
    for b in range(2):
        lo = 256 * b
        qid = qid_ref[lo:lo + 256, :]
        kid = kid_ref[:, lo:lo + 1280]
        row = lax.broadcasted_iota(jnp.int32, (256, 1280), 0)
        col = lax.broadcasted_iota(jnp.int32, (256, 1280), 1)
        allowed = (qid == kid) & (col > row) & (col <= row + 1024)
        outs = []
        for h in range(2):
            q = q_ref[lo:lo + 256, HD * h:HD * h + HD]
            s = lax.dot_general(q, k[lo:lo + 1280], (((1,), (1,)), ((), ())), preferred_element_type=F32)
            s = jnp.where(allowed, s * (SCALE * LOG2E), -1e30)
            top = jnp.max(s, axis=1, keepdims=True)
            e = jnp.exp2(s - top)
            total = jnp.sum(e, axis=1, keepdims=True)
            mix = jnp.dot(e.astype(BF), v[lo:lo + 1280], preferred_element_type=F32)
            outs.append(mix / total)
        out = jnp.concatenate(outs, axis=1).astype(BF)
        for i in range(4):
            zz, cc = 2 * b + i // 2, i % 2
            o_ref[(cc + c) % 2, (zz - z + 4) % 4] = out[PER * i:PER * i + PER]


def attend(at, q, kv2, kv1, kv0, qid, kid):
    return pl.pallas_call(
        attend_kernel,
        out_shape=jax.ShapeDtypeStruct((2, 4, PER, 256), BF),
        in_specs=[SM] + [VM] * 6,
        out_specs=VM,
        compiler_params=params(32),
        cost_estimate=cost(4 * 1024 * 1280 * 128 * 1.5, 2 * MB, 1024 * 1280),
        name="attend",
    )(at, q, kv2, kv1, kv0, qid, kid)


def project_kernel(a0, a1, s0, s1, w_ref, ws_ref, p0, p1t, p1b, p2t, p2b, p3t, p3b):
    acc = jnp.dot(jnp.concatenate([a0[...], a1[...]], axis=1), w_ref[...], preferred_element_type=F32)
    acc += jnp.dot(jnp.concatenate([s0[...], s1[...]], axis=1), ws_ref[...], preferred_element_type=F32)
    out = acc.astype(BF)
    p0[...] = out[:64]
    for i, ref in enumerate((p1t, p1b, p2t, p2b, p3t, p3b)):
        ref[...] = out[64 + 32 * i:96 + 32 * i]


def project(a0, a1, s0, s1, w, ws):
    width = 768
    row = lambda r: pl.BlockSpec((r, width), lambda j: (0, j))
    full = pl.BlockSpec((256, 256), lambda j: (0, 0))
    return pl.pallas_call(
        project_kernel,
        out_shape=[jax.ShapeDtypeStruct((64, D), BF)] + [jax.ShapeDtypeStruct((32, D), BF)] * 6,
        grid=(D // width,),
        in_specs=[full] * 4 + [row(512)] * 2,
        out_specs=[row(64)] + [row(32)] * 6,
        compiler_params=params(24),
        cost_estimate=cost(2 * 256 * 1024 * D, 2 * 1280 * D),
        name="project",
    )(a0, a1, s0, s1, w, ws)


def norm_kernel(p0, at_ref, ab_ref, bt_ref, bb_ref, res_ref, gain_ref, new_ref, nrm_ref):
    post = gain_ref[0:1].astype(F32) + gain_ref[1:2].astype(F32)
    pre = gain_ref[2:3].astype(F32) + gain_ref[3:4].astype(F32)
    for half, (a, b) in enumerate(((at_ref, bt_ref), (ab_ref, bb_ref))):
        rows = slice(32 * half, 32 * half + 32)
        owned = p0[rows].astype(F32) + a[...].astype(F32) + b[...].astype(F32)
        factor = lax.rsqrt(jnp.mean(owned * owned, axis=1, keepdims=True) + EPS)
        new = (res_ref[rows].astype(F32) + owned * factor * post).astype(BF)
        stream = new.astype(F32)
        for j in range(8):
            new_ref[j, rows] = stream[:, 672 * j:672 * j + 672].astype(BF)
        second = lax.rsqrt(jnp.mean(stream * stream, axis=1, keepdims=True) + EPS)
        nrm_ref[rows] = (stream * second * pre).astype(BF)


def norm(*args):
    return pl.pallas_call(
        norm_kernel,
        out_shape=[jax.ShapeDtypeStruct((8, PER, 672), BF), jax.ShapeDtypeStruct((PER, D), BF)],
        in_specs=[VM] * 7,
        out_specs=[VM] * 2,
        compiler_params=params(16),
        cost_estimate=cost(20 * PER * D, 8 * PER * D),
        name="norm",
    )(*args)


def token_copies(where, pieces, tokens_at, n_ref, sems):
    z, c = where[0], where[1]
    copies = []
    for i, (ref, (dz, dc, part)) in enumerate(zip(pieces, tokens_at)):
        base, rows = 64 * (2 * ((z + dz) % 4) + (c + dc) % 2), 64
        if part is not None:
            base, rows = base + 32 * part, 32
        copies.append(pltpu.make_async_copy(ref, n_ref.at[pl.ds(pl.multiple_of(base, 32), rows)], sems.at[i]))
    return copies


def gelu(g):
    return 0.5 * g * (1 + jnp.tanh(0.7978845608028654 * (g + 0.044715 * (g * g * g))))


def gated(pieces, tokens_at, where, w):
    blocks = w.shape[1] // 256
    n = len(pieces)

    def body(*refs):
        place, w_ref, o_ref, n_ref, sems = refs[n:]

        @pl.when(pl.program_id(0) == 0)
        def _():
            copies = token_copies(place, refs[:n], tokens_at, n_ref, sems)
            for copy in copies:
                copy.start()
            for copy in copies:
                copy.wait()

        acc = jnp.dot(n_ref[...], w_ref[...], preferred_element_type=F32)
        o_ref[...] = (gelu(acc[:, :128]) * acc[:, 128:]).T.astype(BF)

    return pl.pallas_call(
        body,
        out_shape=jax.ShapeDtypeStruct((128 * blocks, TOK), BF),
        grid=(blocks,),
        in_specs=[HB] * n + [SM, pl.BlockSpec((D, 256), lambda j: (0, j))],
        out_specs=pl.BlockSpec((128, TOK), lambda j: (j, 0)),
        scratch_shapes=[pltpu.VMEM((TOK, D), BF), pltpu.SemaphoreType.DMA((n,))],
        compiler_params=params(56),
        cost_estimate=cost(2 * TOK * D * 256 * blocks, 2 * D * 256 * blocks + 2 * TOK * D),
        name="gated",
    )(*pieces, where, w)


def gated_rest(pieces, tokens_at, where, groups):
    n, m = len(pieces), len(groups)
    rel = (0, 3, 1, 2)
    parts = [(g, k, 336 * k, rel[k], rel[g]) for g in range(3) for k in range(4)]
    parts += [(3, k, 336 * k, rel[k], 2) for k in range(2)] + [(4, k, 336 * (k - 2), rel[k], 2) for k in (2, 3)]

    def body(*refs):
        place, o_ref, n_ref, w_ref, sems, wsems = refs[n + m:]
        c, y, x = place[1], place[2], place[3]
        copies = token_copies(place, refs[:n], tokens_at, n_ref, sems)
        for i, (g, _, lo, first, then) in enumerate(parts):
            dx = jnp.where(c == 0, first, then)
            dy = jnp.where(c == 0, then, first)
            row = 336 * (4 * ((y + dy) % 4) + (x + dx) % 4)
            src = refs[n + g].at[pl.ds(lo, 336)]
            copies.append(pltpu.make_async_copy(src, w_ref.at[pl.ds(pl.multiple_of(row, 16), 336)], wsems.at[i]))
        for copy in copies:
            copy.start()
        for copy in copies:
            copy.wait()
        for j in range(10 - SPLIT):
            acc = jnp.dot(n_ref[...], w_ref[:, 256 * j:256 * j + 256], preferred_element_type=F32)
            o_ref[128 * j:128 * j + 128] = (gelu(acc[:, :128]) * acc[:, 128:]).T.astype(BF)
        acc = jnp.dot(n_ref[...], w_ref[:, REST - 128:], preferred_element_type=F32)
        act = gelu(acc) * pltpu.roll(acc, 64, 1)
        o_ref[128 * (10 - SPLIT):] = act.T[:64].astype(BF)

    return pl.pallas_call(
        body,
        out_shape=jax.ShapeDtypeStruct((REST // 2, TOK), BF),
        in_specs=[HB] * (n + m) + [SM],
        out_specs=VM,
        scratch_shapes=[
            pltpu.VMEM((TOK, D), BF),
            pltpu.VMEM((D, REST), BF),
            pltpu.SemaphoreType.DMA((n,)),
            pltpu.SemaphoreType.DMA((16,)),
        ],
        compiler_params=params(56),
        cost_estimate=cost(2 * TOK * D * REST, 2 * D * REST + 2 * TOK * D),
        name="gated_rest",
    )(*pieces, *groups, where)


def per_device(queries, keys, values, doc_ids, out_weight, residual, post_gain, pre_gain, gate_weight, up_weight):
    y, x, z, c = (lax.axis_index(a) for a in ("y", "x", "z", "c"))
    where = jnp.stack([z, c, y, x]).astype(jnp.int32)

    w, rest = pack(gate_weight, up_weight)
    w_all = lax.all_gather(w, ("y", "x"), axis=0, tiled=True)
    m, p, top, bottom = ring_gather(rest, 176, 0)
    group = jnp.concatenate([rest, m, p, top, bottom], axis=0)
    queries, group = lax.optimization_barrier((queries, group))
    groups = [group, ring(group, 1, 1), ring(group, -1, 1)]

    gains = jnp.stack([post_gain, pre_gain])
    high = gains.astype(BF)
    low = (gains - high.astype(F32)).astype(BF)
    extra = jnp.stack([high[0], low[0], high[1], low[1]])
    extra = jnp.concatenate([extra, jnp.zeros((12, 672), BF)], axis=0)
    sent = jnp.concatenate([residual.reshape(8, PER, 672), jnp.broadcast_to(extra[None], (8, 16, 672))], axis=1)
    mine = lax.all_to_all(sent, ("z", "c"), 0, 0, tiled=True).transpose(1, 0, 2).reshape(PER + 16, D)

    start = (4 * y + x) * TOK
    padded = jnp.concatenate([jnp.full((2 * TOK,), -1, jnp.int32), doc_ids])
    kid = lax.dynamic_slice_in_dim(padded, start, 3 * TOK, 0)[None, :]
    qid = lax.dynamic_slice_in_dim(doc_ids, start, TOK, 0)[:, None]

    queries, mine = lax.optimization_barrier((queries, mine))
    cols = [slice(HD * h, HD * h + HD) for h in range(2)]
    kv0 = jnp.concatenate([keys[:, cols[0]], values[:, cols[0]], keys[:, cols[1]], values[:, cols[1]]], axis=1)
    kv1 = behind(kv0)
    kv2 = behind(kv1)
    mixes = []
    for h in range(2):
        two = slice(256 * h, 256 * h + 256)
        mixes.append(attend(where, queries[:, two], kv2[:, two], kv1[:, two], kv0[:, two], qid, kid))
    other_weight = shift(out_weight, "c", 1)
    own = [m[0].reshape(256, 256) for m in mixes]
    other = [shift(m[1].reshape(256, 256), "c", 1) for m in mixes]
    p0, p1t, p1b, p2t, p2b, p3t, p3b = project(*own, *other, out_weight, other_weight)

    up_t = shift(p2t, "z", 1)
    dn_b = shift(p2b, "z", -1)
    a_b = shift(p1b, "z", 1)
    b_t = shift(p3t, "z", -1)
    add = lambda p, q: (p.astype(F32) + q.astype(F32)).astype(BF)
    a_t = shift(add(p1t, up_t), "z", 1)
    b_b = shift(add(p3b, dn_b), "z", -1)

    new, nrm = norm(p0, a_t, a_b, b_t, b_b, mine[:PER], mine[PER:PER + 4])

    m, q = shift(nrm, "z", 1), shift(nrm, "z", -1)
    m, q, groups = lax.optimization_barrier((m, q, groups))
    pieces = [nrm, m, q, shift(m[:32], "z", 1), shift(q[32:], "z", -1)]
    places = [(0, None), (3, None), (1, None), (2, 0), (2, 1)]
    pieces += [shift(p, "c", 1) for p in pieces]
    tokens_at = [(dz, dc, part) for dc in range(2) for dz, part in places]
    groups = groups + [ring(groups[1][:672], 1, 1), ring(groups[2][672:], -1, 1)]
    new, pieces = lax.optimization_barrier((new, pieces))
    new_residual = lax.all_to_all(new, ("z", "c"), 0, 0, tiled=True).reshape(TOK, 672)
    act = jnp.concatenate(
        [gated(pieces, tokens_at, where, w_all), gated_rest(pieces, tokens_at, where, groups)], axis=0
    )
    return new_residual, act.T


def solution(mesh):
    fine = Mesh(mesh.devices.reshape(4, 4, 4, 2), ("y", "x", "z", "c"))
    t, f = ("y", "x"), ("z", "c")
    in_specs = (P(t, f), P(t, f), P(t, f), P(), P(f, None), P(t, f), P(f), P(f), P(t, f), P(t, f))
    return jax.shard_map(per_device, mesh=fine, in_specs=in_specs, out_specs=(P(t, f), P(t, f)), check_vma=False)
```

```python
import jax
import jax.numpy as jnp
from jax import lax
from jax.experimental import pallas as pl
from jax.experimental.pallas import tpu as pltpu
from jax.sharding import Mesh, PartitionSpec as P

D = 5376
HD = 128
WINDOW = 1024
EPS = 1e-06
LOG2E = 1.4426950408889634
SCALE = float(168) ** -0.5
TOK = 512
PER = 64
BF = jnp.bfloat16
F32 = jnp.float32
VM = pl.BlockSpec(memory_space=pltpu.VMEM)
SM = pl.BlockSpec(memory_space=pltpu.SMEM)
HB = pl.BlockSpec(memory_space=pltpu.HBM)
MB = 1 << 20


def params(mb):
    return pltpu.CompilerParams(vmem_limit_bytes=mb * MB)


def cost(flops, nbytes, trans=0):
    return pl.CostEstimate(flops=int(flops), bytes_accessed=int(nbytes), transcendentals=int(trans))


def shift(value, axis, by):
    n = lax.axis_size(axis)
    return lax.ppermute(value, axis, [(i, (i + by) % n) for i in range(n)])


def behind(value):
    n = 16
    return lax.ppermute(value, ("y", "x"), [(i, i + 1) for i in range(n - 1)])


def pair_kernel(k_ref, v_ref, kv_ref):
    for h in range(2):
        kv_ref[:, 256 * h:256 * h + 128] = k_ref[:, 128 * h:128 * h + 128]
        kv_ref[:, 256 * h + 128:256 * h + 256] = v_ref[:, 128 * h:128 * h + 128]


def pair(keys, values):
    return pl.pallas_call(
        pair_kernel,
        out_shape=jax.ShapeDtypeStruct((TOK, 512), BF),
        in_specs=[VM] * 2,
        out_specs=VM,
        compiler_params=params(16),
        cost_estimate=cost(0, 1000),
        name="pair",
    )(keys, values)


def pack_kernel(g_ref, u_ref, o_ref):
    g, u = g_ref[...], u_ref[...]
    for j in range(7):
        lo = 192 * j
        o_ref[:, 384 * j:384 * j + 384] = jnp.concatenate(
            [g[:, lo:lo + 128], u[:, lo:lo + 128], g[:, lo + 128:lo + 192], u[:, lo + 128:lo + 192]], axis=1
        )


def pack(gate, up):
    return pl.pallas_call(
        pack_kernel,
        out_shape=jax.ShapeDtypeStruct((336, 2688), BF),
        in_specs=[VM, VM],
        out_specs=VM,
        compiler_params=params(24),
        cost_estimate=cost(0, 1000),
        name="pack",
    )(gate, up)


def ring(value, by, phase):
    pairs = []
    for y in range(4):
        for x in range(4):
            for z in range(4):
                for c in range(2):
                    along_x = (c == 0) == (phase == 0)
                    yy, xx = (y, (x + by) % 4) if along_x else ((y + by) % 4, x)
                    pairs.append((((y * 4 + x) * 4 + z) * 2 + c, ((yy * 4 + xx) * 4 + z) * 2 + c))
    return lax.ppermute(value, ("y", "x", "z", "c"), pairs)


def attend_kernel(at_ref, q_ref, kv2_ref, kv1_ref, kv0_ref, qid_ref, kid_ref, o_ref):
    z, c = at_ref[0], at_ref[1]
    for b in range(2):
        lo = 256 * b
        qid = qid_ref[lo:lo + 256, :]
        kid = kid_ref[:, lo:lo + 1280]
        row = lax.broadcasted_iota(jnp.int32, (256, 1280), 0)
        col = lax.broadcasted_iota(jnp.int32, (256, 1280), 1)
        allowed = (qid == kid) & (col > row) & (col <= row + 1024)
        outs = []
        for h in range(4):
            kc = slice(256 * (h // 2), 256 * (h // 2) + HD)
            vc = slice(256 * (h // 2) + HD, 256 * (h // 2) + 2 * HD)
            near = slice(0, 512 if b else 256)
            k = jnp.concatenate([kv2_ref[lo:, kc], kv1_ref[:, kc], kv0_ref[near, kc]], axis=0)
            v = jnp.concatenate([kv2_ref[lo:, vc], kv1_ref[:, vc], kv0_ref[near, vc]], axis=0)
            q = q_ref[lo:lo + 256, HD * h:HD * h + HD]
            s = lax.dot_general(q, k, (((1,), (1,)), ((), ())), preferred_element_type=F32)
            s = jnp.where(allowed, s * (SCALE * LOG2E), -1e30)
            top = jnp.max(s, axis=1, keepdims=True)
            e = jnp.exp2(s - top)
            total = jnp.sum(e, axis=1, keepdims=True)
            outs.append(jnp.dot(e.astype(BF), v, preferred_element_type=F32) / total)
        out = jnp.concatenate(outs, axis=1).astype(BF)
        for i in range(4):
            zz, cc = 2 * b + i // 2, i % 2
            o_ref[(cc + c) % 2, (zz - z + 4) % 4] = out[PER * i:PER * i + PER]


def attend(at, q, kv2, kv1, kv0, qid, kid):
    return pl.pallas_call(
        attend_kernel,
        out_shape=jax.ShapeDtypeStruct((2, 4, PER, 512), BF),
        in_specs=[SM] + [VM] * 6,
        out_specs=VM,
        compiler_params=params(32),
        cost_estimate=cost(0, 1000),
        name="attend",
    )(at, q, kv2, kv1, kv0, qid, kid)


def project_kernel(a, s, w_ref, ws_ref, p0, p1t, p1b, p2t, p2b, p3t, p3b):
    acc = jnp.dot(a[...], w_ref[...], preferred_element_type=F32)
    acc += jnp.dot(s[...], ws_ref[...], preferred_element_type=F32)
    out = acc.astype(BF)
    p0[...] = out[:64]
    for i, ref in enumerate((p1t, p1b, p2t, p2b, p3t, p3b)):
        ref[...] = out[64 + 32 * i:96 + 32 * i]


def project(a, s, w, ws):
    width = 768
    row = lambda r: pl.BlockSpec((r, width), lambda j: (0, j))
    full = pl.BlockSpec((256, 512), lambda j: (0, 0))
    return pl.pallas_call(
        project_kernel,
        out_shape=[jax.ShapeDtypeStruct((64, D), BF)] + [jax.ShapeDtypeStruct((32, D), BF)] * 6,
        grid=(D // width,),
        in_specs=[full] * 2 + [row(512)] * 2,
        out_specs=[row(64)] + [row(32)] * 6,
        compiler_params=params(24),
        cost_estimate=cost(0, 1000),
        name="project",
    )(a, s, w, ws)


def norm_kernel(p0, at_ref, ab_ref, bt_ref, bb_ref, res_ref, new_ref, nrm_ref):
    gain = jnp.concatenate([res_ref[j, 64:80].astype(F32) for j in range(8)], axis=1)
    post, pre = gain[0:1] + gain[1:2], gain[2:3] + gain[3:4]
    for half, (a, b) in enumerate(((at_ref, bt_ref), (ab_ref, bb_ref))):
        rows = slice(32 * half, 32 * half + 32)
        owned = p0[rows].astype(F32) + a[...].astype(F32) + b[...].astype(F32)
        factor = lax.rsqrt(jnp.mean(owned * owned, axis=1, keepdims=True) + EPS)
        res = jnp.concatenate([res_ref[j, rows].astype(F32) for j in range(8)], axis=1)
        new = (res + owned * factor * post).astype(BF)
        stream = new.astype(F32)
        for j in range(8):
            new_ref[j, rows] = stream[:, 672 * j:672 * j + 672].astype(BF)
        second = lax.rsqrt(jnp.mean(stream * stream, axis=1, keepdims=True) + EPS)
        nrm_ref[rows] = (stream * second * pre).astype(BF)


def norm(*args):
    return pl.pallas_call(
        norm_kernel,
        out_shape=[jax.ShapeDtypeStruct((8, PER, 672), BF), jax.ShapeDtypeStruct((PER, D), BF)],
        in_specs=[VM] * 6,
        out_specs=[VM] * 2,
        compiler_params=params(16),
        cost_estimate=cost(0, 1000),
        name="norm",
    )(*args)


def token_copies(where, pieces, tokens_at, n_ref, sems):
    z, c = where[0], where[1]
    copies = []
    for i, (ref, (dz, dc, part)) in enumerate(zip(pieces, tokens_at)):
        base, rows = 64 * (2 * ((z + dz) % 4) + (c + dc) % 2), 64
        if part is not None:
            base, rows = base + 32 * part, 32
        copies.append(pltpu.make_async_copy(ref, n_ref.at[pl.ds(pl.multiple_of(base, 32), rows)], sems.at[i]))
    return copies


def gelu(g):
    return 0.5 * g * (1 + jnp.tanh(0.7978845608028654 * (g + 0.044715 * (g * g * g))))


REL = (0, 3, 1, 2)


REL = (0, 3, 1, 2)
GROUP = 1408


def order(pieces, tokens_at, where):
    n = len(pieces)

    def body(*refs):
        place, o_ref, n_ref, sems = refs[n:]
        copies = token_copies(place, refs[:n], tokens_at, n_ref, sems)
        for copy in copies:
            copy.start()
        for copy in copies:
            copy.wait()
        c, y, x = place[1], place[2], place[3]

        def put(i, me, value, rows):
            rel = (i - me + 4) % 4
            slot = jnp.where(rel == 0, 0, jnp.where(rel == 3, 1, rel + 1))
            o_ref[rows, pl.ds(pl.multiple_of(GROUP * slot, 128), 1344)] = value

        @pl.loop(0, 8)
        def _(r):
            rows = pl.ds(pl.multiple_of(64 * r, 64), 64)

            @pl.when(c == 0)
            def _():
                for i in range(4):
                    put(i, y, n_ref[rows, 1344 * i:1344 * i + 1344], rows)

            @pl.when(c == 1)
            def _():
                for i in range(4):
                    cols = [1344 * k + 336 * i for k in range(4)]
                    put(i, x, jnp.concatenate([n_ref[rows, lo:lo + 336] for lo in cols], axis=1), rows)

    return pl.pallas_call(
        body,
        out_shape=jax.ShapeDtypeStruct((TOK, 4 * GROUP), BF),
        in_specs=[HB] * n + [SM],
        out_specs=VM,
        scratch_shapes=[pltpu.VMEM((TOK, D), BF), pltpu.SemaphoreType.DMA((n,))],
        compiler_params=params(40),
        cost_estimate=cost(0, 1000),
        name="order",
    )(*pieces, where)


def weight_copies(parts, where, arrays, block, w_ref, sems):
    c, y, x = where[1], where[2], where[3]
    first = jnp.where(c == 0, x, y)
    cols = pl.ds(pl.multiple_of(384 * block, 128), 384)
    copies = []
    for i, (array, slot, rel) in enumerate(parts):
        row = pl.multiple_of(1344 * slot + 336 * ((first + rel) % 4), 16)
        copies.append(
            pltpu.make_async_copy(arrays[array].at[:, cols], w_ref.at[pl.ds(row, 336)], sems.at[i])
        )
    return copies


def fetch_block(parts, place, arrays, w_ref, sems):
    j = pl.program_id(0)
    slot = lax.rem(j, 2)

    @pl.when(j == 0)
    def _():
        for copy in weight_copies(parts, place, arrays, 0, w_ref.at[0], sems.at[0]):
            copy.start()

    @pl.when(j + 1 < 7)
    def _():
        for copy in weight_copies(parts, place, arrays, j + 1, w_ref.at[1 - slot], sems.at[1 - slot]):
            copy.start()

    for copy in weight_copies(parts, place, arrays, j, w_ref.at[slot], sems.at[slot]):
        copy.wait()
    return slot


def near(rows, where, blocks):
    m = len(blocks)
    parts = [(4 * g + k, g, REL[k]) for g in range(3) for k in range(4)]

    def body(*refs):
        place, n_ref, o_ref, w_ref, sems = refs[m:]
        slot = fetch_block(parts, place, refs[:m], w_ref, sems)
        acc = jnp.dot(n_ref[:, :1344], w_ref[slot, :1344], preferred_element_type=F32)
        for g in (1, 2):
            lhs = n_ref[:, GROUP * g:GROUP * g + 1344]
            acc += jnp.dot(lhs, w_ref[slot, 1344 * g:1344 * g + 1344], preferred_element_type=F32)
        o_ref[...] = acc

    return pl.pallas_call(
        body,
        out_shape=jax.ShapeDtypeStruct((TOK, 2688), F32),
        grid=(7,),
        in_specs=[HB] * m + [SM, pl.BlockSpec((TOK, 3 * GROUP), lambda j: (0, 0))],
        out_specs=pl.BlockSpec((TOK, 384), lambda j: (0, j)),
        scratch_shapes=[pltpu.VMEM((2, 3 * 1344, 384), BF), pltpu.SemaphoreType.DMA((2, len(parts)))],
        compiler_params=params(56),
        cost_estimate=cost(2 * TOK * 4032 * 2688, 2 * 4032 * 2688 + 4 * TOK * 2688),
        name="near",
    )(*blocks, where, rows)


def far(rows, where, blocks, sums):
    m = len(blocks)
    parts = [(k, 0, REL[k]) for k in range(4)]

    def body(*refs):
        place, n_ref, s_ref, o_ref, w_ref, sems = refs[m:]
        slot = fetch_block(parts, place, refs[:m], w_ref, sems)
        acc = s_ref[...] + jnp.dot(n_ref[:, :1344], w_ref[slot], preferred_element_type=F32)
        last = acc[:, 256:]
        g = jnp.concatenate([acc[:, :128], last], axis=1)
        u = jnp.concatenate([acc[:, 128:256], pltpu.roll(last, 64, 1)], axis=1)
        o_ref[...] = (gelu(g) * u).T[:192].astype(BF)

    return pl.pallas_call(
        body,
        out_shape=jax.ShapeDtypeStruct((1344, TOK), BF),
        grid=(7,),
        in_specs=[HB] * m
        + [SM, pl.BlockSpec((TOK, GROUP), lambda j: (0, 3)), pl.BlockSpec((TOK, 384), lambda j: (0, j))],
        out_specs=pl.BlockSpec((192, TOK), lambda j: (j, 0)),
        scratch_shapes=[pltpu.VMEM((2, 1344, 384), BF), pltpu.SemaphoreType.DMA((2, len(parts)))],
        compiler_params=params(56),
        cost_estimate=cost(2 * TOK * 1344 * 2688, 2 * 1344 * 2688 + 4 * TOK * 2688),
        name="far",
    )(*blocks, where, rows, sums)


def turn(value, by):
    return lax.dynamic_slice_in_dim(jnp.concatenate([value, value], axis=0), by % 4, 4, 0)


def to_tokens(blocks, z, c):
    blocks = blocks.reshape(4, 2, *blocks.shape[1:])
    keep = jnp.where(c == 0, blocks[:, 0], blocks[:, 1])
    give = jnp.where(c == 0, blocks[:, 1], blocks[:, 0])
    take = shift(give, "c", 1)
    both = turn(jnp.stack([jnp.where(c == 0, keep, take), jnp.where(c == 0, take, keep)], axis=1), z)
    got = jnp.stack([both[0], shift(both[3], "z", 3), shift(both[2], "z", 2), shift(both[1], "z", 1)])
    return turn(got, 4 - z).reshape(8, *got.shape[2:])


def to_features(blocks, z, c):
    both = turn(blocks.reshape(4, 2, *blocks.shape[1:]), z)
    got = jnp.stack([both[0], shift(both[3], "z", 3), shift(both[2], "z", 2), shift(both[1], "z", 1)])
    got = turn(got, 4 - z)
    keep = jnp.where(c == 0, got[:, 0], got[:, 1])
    give = jnp.where(c == 0, got[:, 1], got[:, 0])
    take = shift(give, "c", 1)
    both = jnp.stack([jnp.where(c == 0, keep, take), jnp.where(c == 0, take, keep)], axis=1)
    return both.reshape(8, *got.shape[2:])


def per_device(queries, keys, values, doc_ids, out_weight, residual, post_gain, pre_gain, gate_weight, up_weight):
    y, x, z, c = (lax.axis_index(a) for a in ("y", "x", "z", "c"))
    where = jnp.stack([z, c, y, x]).astype(jnp.int32)

    kv0 = pair(keys, values)
    kv1 = behind(kv0)
    w = pack(gate_weight, up_weight)
    p = ring(w, -1, 0)
    kv1, w_late = lax.optimization_barrier((kv1, w))
    kv2 = behind(kv1)
    m = ring(w_late, 1, 0)
    b = ring(p, -1, 0)
    w_late, kv2 = lax.optimization_barrier((w_late, kv2))
    prev, following = [ring(w_late, 1, 1)], [ring(w_late, -1, 1)]

    gains = jnp.stack([post_gain, pre_gain])
    high = gains.astype(BF)
    low = (gains - high.astype(F32)).astype(BF)
    extra = jnp.stack([high[0], low[0], high[1], low[1]])
    extra = jnp.concatenate([extra, jnp.zeros((12, 672), BF)], axis=0)
    sent = jnp.concatenate([residual.reshape(8, PER, 672), jnp.broadcast_to(extra[None], (8, 16, 672))], axis=1)
    mine = to_tokens(sent, z, c)

    start = (4 * y + x) * TOK
    padded = jnp.concatenate([jnp.full((2 * TOK,), -1, jnp.int32), doc_ids])
    kid = lax.dynamic_slice_in_dim(padded, start, 3 * TOK, 0)[None, :]
    qid = lax.dynamic_slice_in_dim(doc_ids, start, TOK, 0)[:, None]

    queries, mine, p = lax.optimization_barrier((queries, mine, p))
    mix = attend(where, queries, kv2, kv1, kv0, qid, kid)
    other_weight = shift(out_weight, "c", 1)
    own, other = mix[0].reshape(256, 512), shift(mix[1].reshape(256, 512), "c", 1)
    other, m, following[0] = lax.optimization_barrier((other, m, following[0]))
    prev += [ring(v, 1, 1) for v in (m, p)]
    following += [ring(v, -1, 1) for v in (m, p)]
    p0, p1t, p1b, p2t, p2b, p3t, p3b = project(own, other, out_weight, other_weight)

    up_t = shift(p2t, "z", 1)
    dn_b = shift(p2b, "z", -1)
    a_b = shift(p1b, "z", 1)
    b_t = shift(p3t, "z", -1)
    up_t, dn_b, b, prev[0] = lax.optimization_barrier((up_t, dn_b, b, prev[0]))
    prev += [ring(b, 1, 1)]
    following += [ring(b, -1, 1)]
    add = lambda p, q: (p.astype(F32) + q.astype(F32)).astype(BF)
    a_t = shift(add(p1t, up_t), "z", 1)
    b_b = shift(add(p3b, dn_b), "z", -1)
    p0, prev[2], following[2] = lax.optimization_barrier((p0, prev[2], following[2]))
    new, nrm = norm(p0, a_t, a_b, b_t, b_b, mine)

    n_m, n_p = shift(nrm, "z", 1), shift(nrm, "z", -1)
    n_m, n_p, prev[1], following[1] = lax.optimization_barrier((n_m, n_p, prev[1], following[1]))
    pieces = [nrm, n_m, n_p, shift(n_m[:32], "z", 1), shift(n_p[32:], "z", -1)]
    places = [(0, None), (3, None), (1, None), (2, 0), (2, 1)]
    pieces += [shift(piece, "c", 1) for piece in pieces]
    tokens_at = [(dz, dc, part) for dc in range(2) for dz, part in places]
    pieces, prev[3], following[3] = lax.optimization_barrier((pieces, prev[3], following[3]))
    rows = order(pieces, tokens_at, where)

    last = [ring(prev[0], 1, 1), ring(prev[1], 1, 1), ring(following[2], -1, 1), ring(following[3], -1, 1)]
    new, rows = lax.optimization_barrier((new, rows))
    new_residual = to_features(new, z, c).reshape(TOK, 672)
    sums = near(rows, where, [w, m, p, b, *prev, *following])
    act = far(rows, where, last, sums)
    return new_residual, act.T


def solution(mesh):
    fine = Mesh(mesh.devices.reshape(4, 4, 4, 2), ("y", "x", "z", "c"))
    t, f = ("y", "x"), ("z", "c")
    in_specs = (P(t, f), P(t, f), P(t, f), P(), P(f, None), P(t, f), P(f), P(f), P(t, f), P(t, f))
    return jax.shard_map(per_device, mesh=fine, in_specs=in_specs, out_specs=(P(t, f), P(t, f)), check_vma=False)
```

```python
import jax
import jax.numpy as jnp
from jax import lax
from jax.experimental import pallas as pl
from jax.experimental.pallas import tpu as pltpu
from jax.sharding import Mesh, PartitionSpec as P

D = 5376
HD = 128
WINDOW = 1024
EPS = 1e-06
LOG2E = 1.4426950408889634
SCALE = float(168) ** -0.5
TOK = 512
PER = 64
BF = jnp.bfloat16
F32 = jnp.float32
VM = pl.BlockSpec(memory_space=pltpu.VMEM)
SM = pl.BlockSpec(memory_space=pltpu.SMEM)
HB = pl.BlockSpec(memory_space=pltpu.HBM)
MB = 1 << 20


def params(mb):
    return pltpu.CompilerParams(vmem_limit_bytes=mb * MB)


def cost(flops, nbytes, trans=0):
    return pl.CostEstimate(flops=int(flops), bytes_accessed=int(nbytes), transcendentals=int(trans))


def shift(value, axis, by):
    n = lax.axis_size(axis)
    return lax.ppermute(value, axis, [(i, (i + by) % n) for i in range(n)])


def behind(value):
    n = 16
    return lax.ppermute(value, ("y", "x"), [(i, i + 1) for i in range(n - 1)])


def pair_kernel(k_ref, v_ref, kv_ref):
    for h in range(2):
        kv_ref[:, 256 * h:256 * h + 128] = k_ref[:, 128 * h:128 * h + 128]
        kv_ref[:, 256 * h + 128:256 * h + 256] = v_ref[:, 128 * h:128 * h + 128]


def pair(keys, values):
    return pl.pallas_call(
        pair_kernel,
        out_shape=jax.ShapeDtypeStruct((TOK, 512), BF),
        in_specs=[VM] * 2,
        out_specs=VM,
        compiler_params=params(16),
        cost_estimate=cost(0, 1000),
        name="pair",
    )(keys, values)


def pack_kernel(g_ref, u_ref, o_ref):
    g, u = g_ref[...], u_ref[...]
    for j in range(7):
        lo = 192 * j
        o_ref[:, 384 * j:384 * j + 384] = jnp.concatenate(
            [g[:, lo:lo + 128], u[:, lo:lo + 128], g[:, lo + 128:lo + 192], u[:, lo + 128:lo + 192]], axis=1
        )


def pack(gate, up):
    return pl.pallas_call(
        pack_kernel,
        out_shape=jax.ShapeDtypeStruct((336, 2688), BF),
        in_specs=[VM, VM],
        out_specs=VM,
        compiler_params=params(24),
        cost_estimate=cost(0, 1000),
        name="pack",
    )(gate, up)


def ring(value, by, phase):
    pairs = []
    for y in range(4):
        for x in range(4):
            for z in range(4):
                for c in range(2):
                    along_x = (c == 0) == (phase == 0)
                    yy, xx = (y, (x + by) % 4) if along_x else ((y + by) % 4, x)
                    pairs.append((((y * 4 + x) * 4 + z) * 2 + c, ((yy * 4 + xx) * 4 + z) * 2 + c))
    return lax.ppermute(value, ("y", "x", "z", "c"), pairs)


def attend_kernel(at_ref, q_ref, kv2_ref, kv1_ref, kv0_ref, qid_ref, kid_ref, o_ref):
    z, c = at_ref[0], at_ref[1]
    for b in range(2):
        lo = 256 * b
        qid = qid_ref[lo:lo + 256, :]
        kid = kid_ref[:, lo:lo + 1280]
        row = lax.broadcasted_iota(jnp.int32, (256, 1280), 0)
        col = lax.broadcasted_iota(jnp.int32, (256, 1280), 1)
        allowed = (qid == kid) & (col > row) & (col <= row + 1024)
        outs = []
        for h in range(4):
            kc = slice(256 * (h // 2), 256 * (h // 2) + HD)
            vc = slice(256 * (h // 2) + HD, 256 * (h // 2) + 2 * HD)
            near = slice(0, 512 if b else 256)
            k = jnp.concatenate([kv2_ref[lo:, kc], kv1_ref[:, kc], kv0_ref[near, kc]], axis=0)
            v = jnp.concatenate([kv2_ref[lo:, vc], kv1_ref[:, vc], kv0_ref[near, vc]], axis=0)
            q = q_ref[lo:lo + 256, HD * h:HD * h + HD]
            s = lax.dot_general(q, k, (((1,), (1,)), ((), ())), preferred_element_type=F32)
            s = jnp.where(allowed, s * (SCALE * LOG2E), -1e30)
            top = jnp.max(s, axis=1, keepdims=True)
            e = jnp.exp2(s - top)
            total = jnp.sum(e, axis=1, keepdims=True)
            outs.append(jnp.dot(e.astype(BF), v, preferred_element_type=F32) / total)
        out = jnp.concatenate(outs, axis=1).astype(BF)
        for i in range(4):
            zz, cc = 2 * b + i // 2, i % 2
            o_ref[(cc + c) % 2, (zz - z + 4) % 4] = out[PER * i:PER * i + PER]


def attend(at, q, kv2, kv1, kv0, qid, kid):
    return pl.pallas_call(
        attend_kernel,
        out_shape=jax.ShapeDtypeStruct((2, 4, PER, 512), BF),
        in_specs=[SM] + [VM] * 6,
        out_specs=VM,
        compiler_params=params(32),
        cost_estimate=cost(0, 1000),
        name="attend",
    )(at, q, kv2, kv1, kv0, qid, kid)


def project_kernel(a, s, w_ref, ws_ref, p0, p1t, p1b, p2t, p2b, p3t, p3b):
    acc = jnp.dot(a[...], w_ref[...], preferred_element_type=F32)
    acc += jnp.dot(s[...], ws_ref[...], preferred_element_type=F32)
    out = acc.astype(BF)
    p0[...] = out[:64]
    for i, ref in enumerate((p1t, p1b, p2t, p2b, p3t, p3b)):
        ref[...] = out[64 + 32 * i:96 + 32 * i]


def project(a, s, w, ws):
    width = 768
    row = lambda r: pl.BlockSpec((r, width), lambda j: (0, j))
    full = pl.BlockSpec((256, 512), lambda j: (0, 0))
    return pl.pallas_call(
        project_kernel,
        out_shape=[jax.ShapeDtypeStruct((64, D), BF)] + [jax.ShapeDtypeStruct((32, D), BF)] * 6,
        grid=(D // width,),
        in_specs=[full] * 2 + [row(512)] * 2,
        out_specs=[row(64)] + [row(32)] * 6,
        compiler_params=params(24),
        cost_estimate=cost(0, 1000),
        name="project",
    )(a, s, w, ws)


def norm_kernel(p0, at_ref, ab_ref, bt_ref, bb_ref, res_ref, new_ref, nrm_ref):
    gain = jnp.concatenate([res_ref[j, 64:80].astype(F32) for j in range(8)], axis=1)
    post, pre = gain[0:1] + gain[1:2], gain[2:3] + gain[3:4]
    for half, (a, b) in enumerate(((at_ref, bt_ref), (ab_ref, bb_ref))):
        rows = slice(32 * half, 32 * half + 32)
        owned = p0[rows].astype(F32) + a[...].astype(F32) + b[...].astype(F32)
        factor = lax.rsqrt(jnp.mean(owned * owned, axis=1, keepdims=True) + EPS)
        res = jnp.concatenate([res_ref[j, rows].astype(F32) for j in range(8)], axis=1)
        new = (res + owned * factor * post).astype(BF)
        stream = new.astype(F32)
        for j in range(8):
            new_ref[j, rows] = stream[:, 672 * j:672 * j + 672].astype(BF)
        second = lax.rsqrt(jnp.mean(stream * stream, axis=1, keepdims=True) + EPS)
        nrm_ref[rows] = (stream * second * pre).astype(BF)


def norm(*args):
    return pl.pallas_call(
        norm_kernel,
        out_shape=[jax.ShapeDtypeStruct((8, PER, 672), BF), jax.ShapeDtypeStruct((PER, D), BF)],
        in_specs=[VM] * 6,
        out_specs=[VM] * 2,
        compiler_params=params(16),
        cost_estimate=cost(0, 1000),
        name="norm",
    )(*args)


def token_copies(where, pieces, tokens_at, n_ref, sems):
    z, c = where[0], where[1]
    copies = []
    for i, (ref, (dz, dc, part)) in enumerate(zip(pieces, tokens_at)):
        base, rows = 64 * (2 * ((z + dz) % 4) + (c + dc) % 2), 64
        if part is not None:
            base, rows = base + 32 * part, 32
        copies.append(pltpu.make_async_copy(ref, n_ref.at[pl.ds(pl.multiple_of(base, 32), rows)], sems.at[i]))
    return copies


def gelu(g):
    return 0.5 * g * (1 + jnp.tanh(0.7978845608028654 * (g + 0.044715 * (g * g * g))))


REL = (0, 3, 1, 2)


REL = (0, 3, 1, 2)
GROUP = 1408


def order(pieces, tokens_at, where):
    n = len(pieces)

    def body(*refs):
        place, o_ref, n_ref, sems = refs[n:]
        copies = token_copies(place, refs[:n], tokens_at, n_ref, sems)
        for copy in copies:
            copy.start()
        for copy in copies:
            copy.wait()
        c, y, x = place[1], place[2], place[3]

        def put(i, me, value, rows):
            rel = (i - me + 4) % 4
            slot = jnp.where(rel == 0, 0, jnp.where(rel == 3, 1, rel + 1))
            o_ref[rows, pl.ds(pl.multiple_of(GROUP * slot, 128), 1344)] = value

        @pl.loop(0, 8)
        def _(r):
            rows = pl.ds(pl.multiple_of(64 * r, 64), 64)

            @pl.when(c == 0)
            def _():
                for i in range(4):
                    put(i, y, n_ref[rows, 1344 * i:1344 * i + 1344], rows)

            @pl.when(c == 1)
            def _():
                for i in range(4):
                    cols = [1344 * k + 336 * i for k in range(4)]
                    put(i, x, jnp.concatenate([n_ref[rows, lo:lo + 336] for lo in cols], axis=1), rows)

    return pl.pallas_call(
        body,
        out_shape=jax.ShapeDtypeStruct((TOK, 4 * GROUP), BF),
        in_specs=[HB] * n + [SM],
        out_specs=VM,
        scratch_shapes=[pltpu.VMEM((TOK, D), BF), pltpu.SemaphoreType.DMA((n,))],
        compiler_params=params(40),
        cost_estimate=cost(0, 1000),
        name="order",
    )(*pieces, where)


def weight_copies(parts, where, arrays, block, w_ref, sems):
    c, y, x = where[1], where[2], where[3]
    first = jnp.where(c == 0, x, y)
    cols = pl.ds(pl.multiple_of(384 * block, 128), 384)
    copies = []
    for i, (array, slot, rel) in enumerate(parts):
        row = pl.multiple_of(1344 * slot + 336 * ((first + rel) % 4), 16)
        copies.append(
            pltpu.make_async_copy(arrays[array].at[:, cols], w_ref.at[pl.ds(row, 336)], sems.at[i])
        )
    return copies


def fetch_block(parts, place, arrays, w_ref, sems):
    j = pl.program_id(0)
    slot = lax.rem(j, 2)

    @pl.when(j == 0)
    def _():
        for copy in weight_copies(parts, place, arrays, 0, w_ref.at[0], sems.at[0]):
            copy.start()

    @pl.when(j + 1 < 7)
    def _():
        for copy in weight_copies(parts, place, arrays, j + 1, w_ref.at[1 - slot], sems.at[1 - slot]):
            copy.start()

    for copy in weight_copies(parts, place, arrays, j, w_ref.at[slot], sems.at[slot]):
        copy.wait()
    return slot


def near(rows, where, blocks):
    m = len(blocks)
    parts = [(4 * g + k, g, REL[k]) for g in range(3) for k in range(4)]

    def body(*refs):
        place, n_ref, o_ref, w_ref, sems = refs[m:]
        slot = fetch_block(parts, place, refs[:m], w_ref, sems)
        acc = jnp.dot(n_ref[:, :1344], w_ref[slot, :1344], preferred_element_type=F32)
        for g in (1, 2):
            lhs = n_ref[:, GROUP * g:GROUP * g + 1344]
            acc += jnp.dot(lhs, w_ref[slot, 1344 * g:1344 * g + 1344], preferred_element_type=F32)
        o_ref[...] = acc

    return pl.pallas_call(
        body,
        out_shape=jax.ShapeDtypeStruct((TOK, 2688), F32),
        grid=(7,),
        in_specs=[HB] * m + [SM, pl.BlockSpec((TOK, 3 * GROUP), lambda j: (0, 0))],
        out_specs=pl.BlockSpec((TOK, 384), lambda j: (0, j)),
        scratch_shapes=[pltpu.VMEM((2, 3 * 1344, 384), BF), pltpu.SemaphoreType.DMA((2, len(parts)))],
        compiler_params=params(56),
        cost_estimate=cost(0, 1000),
        name="near",
    )(*blocks, where, rows)


def far(rows, where, blocks, sums):
    m = len(blocks)
    parts = [(k, 0, REL[k]) for k in range(4)]

    def body(*refs):
        place, n_ref, s_ref, o_ref, w_ref, acc_ref, sems = refs[m:]
        j = pl.program_id(0)
        slot = lax.rem(j, 2)

        @pl.when(j == 0)
        def _():
            for copy in weight_copies(parts, place, refs[:m], 0, w_ref.at[0], sems.at[0]):
                copy.start()

        @pl.when(j + 1 < 7)
        def _():
            for copy in weight_copies(parts, place, refs[:m], j + 1, w_ref.at[1 - slot], sems.at[1 - slot]):
                copy.start()

        @pl.when(j < 7)
        def _():
            for copy in weight_copies(parts, place, refs[:m], j, w_ref.at[slot], sems.at[slot]):
                copy.wait()

        acc = acc_ref[1 - slot]
        last = acc[:, 256:]
        g = jnp.concatenate([acc[:, :128], last], axis=1)
        u = jnp.concatenate([acc[:, 128:256], pltpu.roll(last, 64, 1)], axis=1)
        o_ref[...] = (gelu(g) * u).T[:192].astype(BF)
        acc_ref[slot] = s_ref[...] + jnp.dot(n_ref[:, :1344], w_ref[slot], preferred_element_type=F32)

    return pl.pallas_call(
        body,
        out_shape=jax.ShapeDtypeStruct((1344, TOK), BF),
        grid=(8,),
        in_specs=[HB] * m
        + [
            SM,
            pl.BlockSpec((TOK, GROUP), lambda j: (0, 3)),
            pl.BlockSpec((TOK, 384), lambda j: (0, jnp.minimum(j, 6))),
        ],
        out_specs=pl.BlockSpec((192, TOK), lambda j: (jnp.maximum(j - 1, 0), 0)),
        scratch_shapes=[
            pltpu.VMEM((2, 1344, 384), BF),
            pltpu.VMEM((2, TOK, 384), F32),
            pltpu.SemaphoreType.DMA((2, len(parts))),
        ],
        compiler_params=params(56),
        cost_estimate=cost(2 * TOK * 1344 * 2688, 2 * 1344 * 2688 + 4 * TOK * 2688),
        name="far",
    )(*blocks, where, rows, sums)


def turn(value, by):
    return lax.dynamic_slice_in_dim(jnp.concatenate([value, value], axis=0), by % 4, 4, 0)


def swap(blocks, z, c):
    blocks = blocks.reshape(4, 2, *blocks.shape[1:])
    keep = jnp.where(c == 0, blocks[:, 0], blocks[:, 1])
    give = jnp.where(c == 0, blocks[:, 1], blocks[:, 0])
    take = shift(give, "c", 1)
    both = turn(jnp.stack([jnp.where(c == 0, keep, take), jnp.where(c == 0, take, keep)], axis=1), z)
    return [both[0], shift(both[3], "z", 3), shift(both[2], "z", 2), shift(both[1], "z", 1)]


def gather(got, z):
    got = jnp.stack(got)
    return turn(got, 4 - z).reshape(8, *got.shape[2:])


def per_device(queries, keys, values, doc_ids, out_weight, residual, post_gain, pre_gain, gate_weight, up_weight):
    y, x, z, c = (lax.axis_index(a) for a in ("y", "x", "z", "c"))
    where = jnp.stack([z, c, y, x]).astype(jnp.int32)

    kv0 = pair(keys, values)
    kv1 = behind(kv0)
    gate_weight, kv0 = lax.optimization_barrier((gate_weight, kv0))
    w = pack(gate_weight, up_weight)
    p = ring(w, -1, 0)
    kv1, w_late, residual, post_gain = lax.optimization_barrier((kv1, w, residual, post_gain))
    kv2 = behind(kv1)
    m = ring(w_late, 1, 0)
    b = ring(p, -1, 0)
    w_late, kv2 = lax.optimization_barrier((w_late, kv2))
    prev, following = [ring(w_late, 1, 1)], [ring(w_late, -1, 1)]

    gains = jnp.stack([post_gain, pre_gain])
    high = gains.astype(BF)
    low = (gains - high.astype(F32)).astype(BF)
    extra = jnp.stack([high[0], low[0], high[1], low[1]])
    extra = jnp.concatenate([extra, jnp.zeros((12, 672), BF)], axis=0)
    sent = jnp.concatenate([residual.reshape(8, PER, 672), jnp.broadcast_to(extra[None], (8, 16, 672))], axis=1)
    mine = gather(swap(sent, z, c), z)

    start = (4 * y + x) * TOK
    padded = jnp.concatenate([jnp.full((2 * TOK,), -1, jnp.int32), doc_ids])
    kid = lax.dynamic_slice_in_dim(padded, start, 3 * TOK, 0)[None, :]
    qid = lax.dynamic_slice_in_dim(doc_ids, start, TOK, 0)[:, None]

    queries, mine, p = lax.optimization_barrier((queries, mine, p))
    mix = attend(where, queries, kv2, kv1, kv0, qid, kid)
    other_weight = shift(out_weight, "c", 1)
    own, other = mix[0].reshape(256, 512), shift(mix[1].reshape(256, 512), "c", 1)
    p0, p1t, p1b, p2t, p2b, p3t, p3b = project(own, other, out_weight, other_weight)

    up_t = shift(p2t, "z", 1)
    dn_b = shift(p2b, "z", -1)
    a_b = shift(p1b, "z", 1)
    b_t = shift(p3t, "z", -1)
    up_t, dn_b, m, following[0] = lax.optimization_barrier((up_t, dn_b, m, following[0]))
    add = lambda p, q: (p.astype(F32) + q.astype(F32)).astype(BF)
    a_t = shift(add(p1t, up_t), "z", 1)
    b_b = shift(add(p3b, dn_b), "z", -1)
    p0, b, prev[0] = lax.optimization_barrier((p0, b, prev[0]))
    prev += [ring(v, 1, 1) for v in (m, p, b)]
    following += [ring(v, -1, 1) for v in (m, p, b)]
    new, nrm = norm(p0, a_t, a_b, b_t, b_b, mine)

    n_m, n_p = shift(nrm, "z", 1), shift(nrm, "z", -1)
    n_m, n_p, prev[2], following[2] = lax.optimization_barrier((n_m, n_p, prev[2], following[2]))
    pieces = [nrm, n_m, n_p, shift(n_m[:32], "z", 1), shift(n_p[32:], "z", -1)]
    places = [(0, None), (3, None), (1, None), (2, 0), (2, 1)]
    pieces += [shift(piece, "c", 1) for piece in pieces]
    tokens_at = [(dz, dc, part) for dc in range(2) for dz, part in places]
    pieces, prev[1], following[1] = lax.optimization_barrier((pieces, prev[1], following[1]))
    rows = order(pieces, tokens_at, where)

    last = [ring(prev[0], 1, 1), ring(prev[1], 1, 1), ring(following[2], -1, 1), ring(following[3], -1, 1)]
    new, rows = lax.optimization_barrier((new, rows))
    sent_back = swap(new, z, c)
    sums = near(rows, where, [w, m, p, b, *prev, *following])
    act = far(rows, where, last, sums)
    sent_back, act = lax.optimization_barrier((sent_back, act))
    new_residual = gather(sent_back, z).reshape(TOK, 672)
    return new_residual, act.T


def solution(mesh):
    fine = Mesh(mesh.devices.reshape(4, 4, 4, 2), ("y", "x", "z", "c"))
    t, f = ("y", "x"), ("z", "c")
    in_specs = (P(t, f), P(t, f), P(t, f), P(), P(f, None), P(t, f), P(f), P(f), P(t, f), P(t, f))
    return jax.shard_map(per_device, mesh=fine, in_specs=in_specs, out_specs=(P(t, f), P(t, f)), check_vma=False)
```

```python
import jax
import jax.numpy as jnp
from jax import lax
from jax.experimental import pallas as pl
from jax.experimental.pallas import tpu as pltpu
from jax.sharding import Mesh, PartitionSpec as P

D = 5376
HD = 128
WINDOW = 1024
EPS = 1e-06
LOG2E = 1.4426950408889634
SCALE = float(168) ** -0.5
TOK = 512
PER = 64
BF = jnp.bfloat16
F32 = jnp.float32
VM = pl.BlockSpec(memory_space=pltpu.VMEM)
SM = pl.BlockSpec(memory_space=pltpu.SMEM)
HB = pl.BlockSpec(memory_space=pltpu.HBM)
MB = 1 << 20


def params(mb):
    return pltpu.CompilerParams(vmem_limit_bytes=mb * MB)


def cost(flops, nbytes, trans=0):
    return pl.CostEstimate(flops=int(flops), bytes_accessed=int(nbytes), transcendentals=int(trans))


def shift(value, axis, by):
    n = lax.axis_size(axis)
    return lax.ppermute(value, axis, [(i, (i + by) % n) for i in range(n)])


def behind(value):
    n = 16
    return lax.ppermute(value, ("y", "x"), [(i, i + 1) for i in range(n - 1)])


def pair_kernel(k_ref, v_ref, kv_ref):
    for h in range(2):
        kv_ref[:, 256 * h:256 * h + 128] = k_ref[:, 128 * h:128 * h + 128]
        kv_ref[:, 256 * h + 128:256 * h + 256] = v_ref[:, 128 * h:128 * h + 128]


def pair(keys, values):
    return pl.pallas_call(
        pair_kernel,
        out_shape=jax.ShapeDtypeStruct((TOK, 512), BF),
        in_specs=[VM] * 2,
        out_specs=VM,
        compiler_params=params(16),
        cost_estimate=cost(0, 1000),
        name="pair",
    )(keys, values)


def pack_kernel(g_ref, u_ref, o_ref):
    g, u = g_ref[...], u_ref[...]
    for j in range(7):
        lo = 192 * j
        o_ref[:, 384 * j:384 * j + 384] = jnp.concatenate(
            [g[:, lo:lo + 128], u[:, lo:lo + 128], g[:, lo + 128:lo + 192], u[:, lo + 128:lo + 192]], axis=1
        )


def pack(gate, up):
    return pl.pallas_call(
        pack_kernel,
        out_shape=jax.ShapeDtypeStruct((336, 2688), BF),
        in_specs=[VM, VM],
        out_specs=VM,
        compiler_params=params(24),
        cost_estimate=cost(0, 1000),
        name="pack",
    )(gate, up)


def ring(value, by, phase):
    pairs = []
    for y in range(4):
        for x in range(4):
            for z in range(4):
                for c in range(2):
                    along_x = (c == 0) == (phase == 0)
                    yy, xx = (y, (x + by) % 4) if along_x else ((y + by) % 4, x)
                    pairs.append((((y * 4 + x) * 4 + z) * 2 + c, ((yy * 4 + xx) * 4 + z) * 2 + c))
    return lax.ppermute(value, ("y", "x", "z", "c"), pairs)


def attend_kernel(at_ref, q_ref, kv2_ref, kv1_ref, kv0_ref, qid_ref, kid_ref, o_ref):
    z, c = at_ref[0], at_ref[1]
    for b in range(2):
        lo = 256 * b
        qid = qid_ref[lo:lo + 256, :]
        kid = kid_ref[:, lo:lo + 1280]
        row = lax.broadcasted_iota(jnp.int32, (256, 1280), 0)
        col = lax.broadcasted_iota(jnp.int32, (256, 1280), 1)
        allowed = (qid == kid) & (col > row) & (col <= row + 1024)
        outs = []
        for h in range(4):
            kc = slice(256 * (h // 2), 256 * (h // 2) + HD)
            vc = slice(256 * (h // 2) + HD, 256 * (h // 2) + 2 * HD)
            near = slice(0, 512 if b else 256)
            k = jnp.concatenate([kv2_ref[lo:, kc], kv1_ref[:, kc], kv0_ref[near, kc]], axis=0)
            v = jnp.concatenate([kv2_ref[lo:, vc], kv1_ref[:, vc], kv0_ref[near, vc]], axis=0)
            q = q_ref[lo:lo + 256, HD * h:HD * h + HD]
            s = lax.dot_general(q, k, (((1,), (1,)), ((), ())), preferred_element_type=F32)
            s = jnp.where(allowed, s * (SCALE * LOG2E), -1e30)
            top = jnp.max(s, axis=1, keepdims=True)
            e = jnp.exp2(s - top)
            total = jnp.sum(e, axis=1, keepdims=True)
            outs.append(jnp.dot(e.astype(BF), v, preferred_element_type=F32) / total)
        out = jnp.concatenate(outs, axis=1).astype(BF)
        for i in range(4):
            zz, cc = 2 * b + i // 2, i % 2
            o_ref[(cc + c) % 2, (zz - z + 4) % 4] = out[PER * i:PER * i + PER]


def attend(at, q, kv2, kv1, kv0, qid, kid):
    return pl.pallas_call(
        attend_kernel,
        out_shape=jax.ShapeDtypeStruct((2, 4, PER, 512), BF),
        in_specs=[SM] + [VM] * 6,
        out_specs=VM,
        compiler_params=params(32),
        cost_estimate=cost(0, 1000),
        name="attend",
    )(at, q, kv2, kv1, kv0, qid, kid)


def project_kernel(a, s, w_ref, ws_ref, p0, p1t, p1b, p2t, p2b, p3t, p3b):
    acc = jnp.dot(a[...], w_ref[...], preferred_element_type=F32)
    acc += jnp.dot(s[...], ws_ref[...], preferred_element_type=F32)
    out = acc.astype(BF)
    p0[...] = out[:64]
    for i, ref in enumerate((p1t, p1b, p2t, p2b, p3t, p3b)):
        ref[...] = out[64 + 32 * i:96 + 32 * i]


def project(a, s, w, ws):
    width = 768
    row = lambda r: pl.BlockSpec((r, width), lambda j: (0, j))
    full = pl.BlockSpec((256, 512), lambda j: (0, 0))
    return pl.pallas_call(
        project_kernel,
        out_shape=[jax.ShapeDtypeStruct((64, D), BF)] + [jax.ShapeDtypeStruct((32, D), BF)] * 6,
        grid=(D // width,),
        in_specs=[full] * 2 + [row(512)] * 2,
        out_specs=[row(64)] + [row(32)] * 6,
        compiler_params=params(24),
        cost_estimate=cost(0, 1000),
        name="project",
    )(a, s, w, ws)


def norm_kernel(p0, at_ref, ab_ref, bt_ref, bb_ref, res_ref, new_ref, nrm_ref):
    gain = jnp.concatenate([res_ref[j, 64:80].astype(F32) for j in range(8)], axis=1)
    post, pre = gain[0:1] + gain[1:2], gain[2:3] + gain[3:4]
    for half, (a, b) in enumerate(((at_ref, bt_ref), (ab_ref, bb_ref))):
        rows = slice(32 * half, 32 * half + 32)
        owned = p0[rows].astype(F32) + a[...].astype(F32) + b[...].astype(F32)
        factor = lax.rsqrt(jnp.mean(owned * owned, axis=1, keepdims=True) + EPS)
        res = jnp.concatenate([res_ref[j, rows].astype(F32) for j in range(8)], axis=1)
        new = (res + owned * factor * post).astype(BF)
        stream = new.astype(F32)
        for j in range(8):
            new_ref[j, rows] = stream[:, 672 * j:672 * j + 672].astype(BF)
        second = lax.rsqrt(jnp.mean(stream * stream, axis=1, keepdims=True) + EPS)
        nrm_ref[rows] = (stream * second * pre).astype(BF)


def norm(*args):
    return pl.pallas_call(
        norm_kernel,
        out_shape=[jax.ShapeDtypeStruct((8, PER, 672), BF), jax.ShapeDtypeStruct((PER, D), BF)],
        in_specs=[VM] * 6,
        out_specs=[VM] * 2,
        compiler_params=params(16),
        cost_estimate=cost(0, 1000),
        name="norm",
    )(*args)


def token_copies(where, pieces, tokens_at, n_ref, sems):
    z, c = where[0], where[1]
    copies = []
    for i, (ref, (dz, dc, part)) in enumerate(zip(pieces, tokens_at)):
        base, rows = 64 * (2 * ((z + dz) % 4) + (c + dc) % 2), 64
        if part is not None:
            base, rows = base + 32 * part, 32
        copies.append(pltpu.make_async_copy(ref, n_ref.at[pl.ds(pl.multiple_of(base, 32), rows)], sems.at[i]))
    return copies


def gelu(g):
    return 0.5 * g * (1 + jnp.tanh(0.7978845608028654 * (g + 0.044715 * (g * g * g))))


REL = (0, 3, 1, 2)


REL = (0, 3, 1, 2)
GROUP = 1408


def order(pieces, tokens_at, where):
    n = len(pieces)

    def body(*refs):
        place, o_ref, n_ref, sems = refs[n:]
        copies = token_copies(place, refs[:n], tokens_at, n_ref, sems)
        for copy in copies:
            copy.start()
        for copy in copies:
            copy.wait()
        c, y, x = place[1], place[2], place[3]

        def put(i, me, value, rows):
            rel = (i - me + 4) % 4
            slot = jnp.where(rel == 0, 0, jnp.where(rel == 3, 1, rel + 1))
            o_ref[rows, pl.ds(pl.multiple_of(GROUP * slot, 128), 1344)] = value

        @pl.loop(0, 8)
        def _(r):
            rows = pl.ds(pl.multiple_of(64 * r, 64), 64)

            @pl.when(c == 0)
            def _():
                for i in range(4):
                    put(i, y, n_ref[rows, 1344 * i:1344 * i + 1344], rows)

            @pl.when(c == 1)
            def _():
                for i in range(4):
                    cols = [1344 * k + 336 * i for k in range(4)]
                    put(i, x, jnp.concatenate([n_ref[rows, lo:lo + 336] for lo in cols], axis=1), rows)

    return pl.pallas_call(
        body,
        out_shape=jax.ShapeDtypeStruct((TOK, 4 * GROUP), BF),
        in_specs=[HB] * n + [SM],
        out_specs=VM,
        scratch_shapes=[pltpu.VMEM((TOK, D), BF), pltpu.SemaphoreType.DMA((n,))],
        compiler_params=params(40),
        cost_estimate=cost(0, 1000),
        name="order",
    )(*pieces, where)


def weight_copies(parts, where, arrays, block, w_ref, sems, width=384):
    c, y, x = where[1], where[2], where[3]
    first = jnp.where(c == 0, x, y)
    cols = pl.ds(pl.multiple_of(width * block, 128), width)
    copies = []
    for i, (array, lo, slot, rel) in enumerate(parts):
        row = pl.multiple_of(1344 * slot + 336 * ((first + rel) % 4), 16)
        copies.append(
            pltpu.make_async_copy(arrays[array].at[pl.ds(lo, 336), cols], w_ref.at[pl.ds(row, 336)], sems.at[i])
        )
    return copies


def fetch_block(parts, place, arrays, w_ref, sems, width):
    j = pl.program_id(0)
    slot = lax.rem(j, 2)

    @pl.when(j == 0)
    def _():
        for copy in weight_copies(parts, place, arrays, 0, w_ref.at[0], sems.at[0], width):
            copy.start()

    @pl.when(j + 1 < 2688 // width)
    def _():
        for copy in weight_copies(parts, place, arrays, j + 1, w_ref.at[1 - slot], sems.at[1 - slot], width):
            copy.start()

    for copy in weight_copies(parts, place, arrays, j, w_ref.at[slot], sems.at[slot], width):
        copy.wait()
    return slot


def near(rows, where, blocks):
    m = len(blocks)
    parts = [(g, 336 * k, g, REL[k]) for g in range(3) for k in range(4)]

    def body(*refs):
        place, n_ref, o_ref, w_ref, sems = refs[m:]
        slot = fetch_block(parts, place, refs[:m], w_ref, sems, 896)
        acc = jnp.dot(n_ref[:, :1344], w_ref[slot, :1344], preferred_element_type=F32)
        for g in (1, 2):
            lhs = n_ref[:, GROUP * g:GROUP * g + 1344]
            acc += jnp.dot(lhs, w_ref[slot, 1344 * g:1344 * g + 1344], preferred_element_type=F32)
        o_ref[...] = acc

    return pl.pallas_call(
        body,
        out_shape=jax.ShapeDtypeStruct((TOK, 2688), F32),
        grid=(3,),
        in_specs=[HB] * m + [SM, pl.BlockSpec((TOK, 3 * GROUP), lambda j: (0, 0))],
        out_specs=pl.BlockSpec((TOK, 896), lambda j: (0, j)),
        scratch_shapes=[pltpu.VMEM((2, 3 * 1344, 896), BF), pltpu.SemaphoreType.DMA((2, len(parts)))],
        compiler_params=params(56),
        cost_estimate=cost(0, 1000),
        name="near",
    )(*blocks, where, rows)


def far(rows, where, blocks, sums):
    m = len(blocks)
    parts = [(k // 2, 336 * (k % 2), 0, REL[k]) for k in range(4)]

    def body(*refs):
        place, n_ref, s_ref, o_ref, w_ref, acc_ref, sems = refs[m:]
        j = pl.program_id(0)
        slot = lax.rem(j, 2)

        @pl.when(j == 0)
        def _():
            for copy in weight_copies(parts, place, refs[:m], 0, w_ref.at[0], sems.at[0]):
                copy.start()

        @pl.when(j + 1 < 7)
        def _():
            for copy in weight_copies(parts, place, refs[:m], j + 1, w_ref.at[1 - slot], sems.at[1 - slot]):
                copy.start()

        @pl.when(j < 7)
        def _():
            for copy in weight_copies(parts, place, refs[:m], j, w_ref.at[slot], sems.at[slot]):
                copy.wait()

        acc = acc_ref[1 - slot]
        last = acc[:, 256:]
        g = jnp.concatenate([acc[:, :128], last], axis=1)
        u = jnp.concatenate([acc[:, 128:256], pltpu.roll(last, 64, 1)], axis=1)
        o_ref[...] = (gelu(g) * u).T[:192].astype(BF)
        acc_ref[slot] = s_ref[...] + jnp.dot(n_ref[:, :1344], w_ref[slot], preferred_element_type=F32)

    return pl.pallas_call(
        body,
        out_shape=jax.ShapeDtypeStruct((1344, TOK), BF),
        grid=(8,),
        in_specs=[HB] * m
        + [
            SM,
            pl.BlockSpec((TOK, GROUP), lambda j: (0, 3)),
            pl.BlockSpec((TOK, 384), lambda j: (0, jnp.minimum(j, 6))),
        ],
        out_specs=pl.BlockSpec((192, TOK), lambda j: (jnp.maximum(j - 1, 0), 0)),
        scratch_shapes=[
            pltpu.VMEM((2, 1344, 384), BF),
            pltpu.VMEM((2, TOK, 384), F32),
            pltpu.SemaphoreType.DMA((2, len(parts))),
        ],
        compiler_params=params(56),
        cost_estimate=cost(2 * TOK * 1344 * 2688, 2 * 1344 * 2688 + 4 * TOK * 2688),
        name="far",
    )(*blocks, where, rows, sums)


def turn(value, by):
    return lax.dynamic_slice_in_dim(jnp.concatenate([value, value], axis=0), by % 4, 4, 0)


def swap(blocks, z, c):
    blocks = blocks.reshape(4, 2, *blocks.shape[1:])
    keep = jnp.where(c == 0, blocks[:, 0], blocks[:, 1])
    give = jnp.where(c == 0, blocks[:, 1], blocks[:, 0])
    take = shift(give, "c", 1)
    both = turn(jnp.stack([jnp.where(c == 0, keep, take), jnp.where(c == 0, take, keep)], axis=1), z)
    return [both[0], shift(both[3], "z", 3), shift(both[2], "z", 2), shift(both[1], "z", 1)]


def gather(got, z):
    got = jnp.stack(got)
    return turn(got, 4 - z).reshape(8, *got.shape[2:])


def per_device(queries, keys, values, doc_ids, out_weight, residual, post_gain, pre_gain, gate_weight, up_weight):
    y, x, z, c = (lax.axis_index(a) for a in ("y", "x", "z", "c"))
    where = jnp.stack([z, c, y, x]).astype(jnp.int32)

    kv0 = pair(keys, values)
    kv1 = behind(kv0)
    gate_weight, kv0 = lax.optimization_barrier((gate_weight, kv0))
    w = pack(gate_weight, up_weight)
    p = ring(w, -1, 0)
    kv2 = behind(kv1)
    kv2, w_late = lax.optimization_barrier((kv2, w))
    m = ring(w_late, 1, 0)
    b = ring(p, -1, 0)
    kv2, residual, post_gain = lax.optimization_barrier((kv2, residual, post_gain))
    group = jnp.concatenate([w, m, p, b], axis=0)
    prev, following = ring(group, 1, 1), ring(group, -1, 1)

    gains = jnp.stack([post_gain, pre_gain])
    high = gains.astype(BF)
    low = (gains - high.astype(F32)).astype(BF)
    extra = jnp.stack([high[0], low[0], high[1], low[1]])
    extra = jnp.concatenate([extra, jnp.zeros((12, 672), BF)], axis=0)
    sent = jnp.concatenate([residual.reshape(8, PER, 672), jnp.broadcast_to(extra[None], (8, 16, 672))], axis=1)
    mine = gather(swap(sent, z, c), z)

    start = (4 * y + x) * TOK
    padded = jnp.concatenate([jnp.full((2 * TOK,), -1, jnp.int32), doc_ids])
    kid = lax.dynamic_slice_in_dim(padded, start, 3 * TOK, 0)[None, :]
    qid = lax.dynamic_slice_in_dim(doc_ids, start, TOK, 0)[:, None]

    mix = attend(where, queries, kv2, kv1, kv0, qid, kid)
    other_weight = shift(out_weight, "c", 1)
    own, other = mix[0].reshape(256, 512), shift(mix[1].reshape(256, 512), "c", 1)
    other, mine = lax.optimization_barrier((other, mine))
    p0, p1t, p1b, p2t, p2b, p3t, p3b = project(own, other, out_weight, other_weight)

    up_t = shift(p2t, "z", 1)
    dn_b = shift(p2b, "z", -1)
    a_b = shift(p1b, "z", 1)
    b_t = shift(p3t, "z", -1)
    add = lambda p, q: (p.astype(F32) + q.astype(F32)).astype(BF)
    a_t = shift(add(p1t, up_t), "z", 1)
    b_b = shift(add(p3b, dn_b), "z", -1)
    new, nrm = norm(p0, a_t, a_b, b_t, b_b, mine)

    n_m, n_p = shift(nrm, "z", 1), shift(nrm, "z", -1)
    pieces = [nrm, n_m, n_p, shift(n_m[:32], "z", 1), shift(n_p[32:], "z", -1)]
    places = [(0, None), (3, None), (1, None), (2, 0), (2, 1)]
    pieces += [shift(piece, "c", 1) for piece in pieces]
    tokens_at = [(dz, dc, part) for dc in range(2) for dz, part in places]
    rows = order(pieces, tokens_at, where)

    prev, following, rows = lax.optimization_barrier((prev, following, rows))
    last = [ring(prev[:672], 1, 1), ring(following[672:], -1, 1)]
    new, rows = lax.optimization_barrier((new, rows))
    sent_back = swap(new, z, c)
    sums = near(rows, where, [group, prev, following])
    act = far(rows, where, last, sums)
    sent_back, act = lax.optimization_barrier((sent_back, act))
    new_residual = gather(sent_back, z).reshape(TOK, 672)
    return new_residual, act.T


def solution(mesh):
    fine = Mesh(mesh.devices.reshape(4, 4, 4, 2), ("y", "x", "z", "c"))
    t, f = ("y", "x"), ("z", "c")
    in_specs = (P(t, f), P(t, f), P(t, f), P(), P(f, None), P(t, f), P(f), P(f), P(t, f), P(t, f))
    return jax.shard_map(per_device, mesh=fine, in_specs=in_specs, out_specs=(P(t, f), P(t, f)), check_vma=False)
```

```python
import jax
import jax.numpy as jnp
from jax import lax
from jax.experimental import pallas as pl
from jax.experimental.pallas import tpu as pltpu
from jax.sharding import Mesh, PartitionSpec as P

D = 5376
HD = 128
WINDOW = 1024
EPS = 1e-06
LOG2E = 1.4426950408889634
SCALE = float(168) ** -0.5
TOK = 512
PER = 64
BF = jnp.bfloat16
F32 = jnp.float32
VM = pl.BlockSpec(memory_space=pltpu.VMEM)
SM = pl.BlockSpec(memory_space=pltpu.SMEM)
HB = pl.BlockSpec(memory_space=pltpu.HBM)
MB = 1 << 20


def params(mb):
    return pltpu.CompilerParams(vmem_limit_bytes=mb * MB)


def cost(flops, nbytes, trans=0):
    return pl.CostEstimate(flops=int(flops), bytes_accessed=int(nbytes), transcendentals=int(trans))


def shift(value, axis, by):
    n = lax.axis_size(axis)
    return lax.ppermute(value, axis, [(i, (i + by) % n) for i in range(n)])


def behind(value):
    n = 16
    return lax.ppermute(value, ("y", "x"), [(i, i + 1) for i in range(n - 1)])


def pair_kernel(k_ref, v_ref, kv_ref):
    for h in range(2):
        kv_ref[:, 256 * h:256 * h + 128] = k_ref[:, 128 * h:128 * h + 128]
        kv_ref[:, 256 * h + 128:256 * h + 256] = v_ref[:, 128 * h:128 * h + 128]


def pair(keys, values):
    return pl.pallas_call(
        pair_kernel,
        out_shape=jax.ShapeDtypeStruct((TOK, 512), BF),
        in_specs=[VM] * 2,
        out_specs=VM,
        compiler_params=params(16),
        cost_estimate=cost(0, 1000),
        name="pair",
    )(keys, values)


def pack_kernel(g_ref, u_ref, o_ref):
    g, u = g_ref[...], u_ref[...]
    for j in range(7):
        lo = 192 * j
        o_ref[:, 384 * j:384 * j + 384] = jnp.concatenate(
            [g[:, lo:lo + 128], u[:, lo:lo + 128], g[:, lo + 128:lo + 192], u[:, lo + 128:lo + 192]], axis=1
        )


def pack(gate, up):
    return pl.pallas_call(
        pack_kernel,
        out_shape=jax.ShapeDtypeStruct((336, 2688), BF),
        in_specs=[VM, VM],
        out_specs=VM,
        compiler_params=params(24),
        cost_estimate=cost(0, 1000),
        name="pack",
    )(gate, up)


def ring(value, by, phase):
    pairs = []
    for y in range(4):
        for x in range(4):
            for z in range(4):
                for c in range(2):
                    along_x = (c == 0) == (phase == 0)
                    yy, xx = (y, (x + by) % 4) if along_x else ((y + by) % 4, x)
                    pairs.append((((y * 4 + x) * 4 + z) * 2 + c, ((yy * 4 + xx) * 4 + z) * 2 + c))
    return lax.ppermute(value, ("y", "x", "z", "c"), pairs)


def attend_kernel(at_ref, q_ref, kv2_ref, kv1_ref, kv0_ref, qid_ref, kid_ref, o_ref):
    z, c = at_ref[0], at_ref[1]
    for b in range(2):
        lo = 256 * b
        qid = qid_ref[lo:lo + 256, :]
        kid = kid_ref[:, lo:lo + 1280]
        row = lax.broadcasted_iota(jnp.int32, (256, 1280), 0)
        col = lax.broadcasted_iota(jnp.int32, (256, 1280), 1)
        allowed = (qid == kid) & (col > row) & (col <= row + 1024)
        outs = []
        for h in range(4):
            kc = slice(256 * (h // 2), 256 * (h // 2) + HD)
            vc = slice(256 * (h // 2) + HD, 256 * (h // 2) + 2 * HD)
            near = slice(0, 512 if b else 256)
            k = jnp.concatenate([kv2_ref[lo:, kc], kv1_ref[:, kc], kv0_ref[near, kc]], axis=0)
            v = jnp.concatenate([kv2_ref[lo:, vc], kv1_ref[:, vc], kv0_ref[near, vc]], axis=0)
            q = q_ref[lo:lo + 256, HD * h:HD * h + HD]
            s = lax.dot_general(q, k, (((1,), (1,)), ((), ())), preferred_element_type=F32)
            s = jnp.where(allowed, s * (SCALE * LOG2E), -1e30)
            top = jnp.max(s, axis=1, keepdims=True)
            e = jnp.exp2(s - top)
            total = jnp.sum(e, axis=1, keepdims=True)
            outs.append(jnp.dot(e.astype(BF), v, preferred_element_type=F32) / total)
        out = jnp.concatenate(outs, axis=1).astype(BF)
        for i in range(4):
            zz, cc = 2 * b + i // 2, i % 2
            o_ref[(cc + c) % 2, (zz - z + 4) % 4] = out[PER * i:PER * i + PER]


def attend(at, q, kv2, kv1, kv0, qid, kid):
    return pl.pallas_call(
        attend_kernel,
        out_shape=jax.ShapeDtypeStruct((2, 4, PER, 512), BF),
        in_specs=[SM] + [VM] * 6,
        out_specs=VM,
        compiler_params=params(32),
        cost_estimate=cost(0, 1000),
        name="attend",
    )(at, q, kv2, kv1, kv0, qid, kid)


def project_kernel(a, s, w_ref, ws_ref, p0, p1t, p1b, p2t, p2b, p3t, p3b):
    acc = jnp.dot(a[...], w_ref[...], preferred_element_type=F32)
    acc += jnp.dot(s[...], ws_ref[...], preferred_element_type=F32)
    out = acc.astype(BF)
    p0[...] = out[:64]
    for i, ref in enumerate((p1t, p1b, p2t, p2b, p3t, p3b)):
        ref[...] = out[64 + 32 * i:96 + 32 * i]


def project(a, s, w, ws):
    width = 768
    row = lambda r: pl.BlockSpec((r, width), lambda j: (0, j))
    full = pl.BlockSpec((256, 512), lambda j: (0, 0))
    return pl.pallas_call(
        project_kernel,
        out_shape=[jax.ShapeDtypeStruct((64, D), BF)] + [jax.ShapeDtypeStruct((32, D), BF)] * 6,
        grid=(D // width,),
        in_specs=[full] * 2 + [row(512)] * 2,
        out_specs=[row(64)] + [row(32)] * 6,
        compiler_params=params(24),
        cost_estimate=cost(0, 1000),
        name="project",
    )(a, s, w, ws)


def norm_kernel(p0, at_ref, ab_ref, bt_ref, bb_ref, res_ref, new_ref, nrm_ref):
    gain = jnp.concatenate([res_ref[j, 64:80].astype(F32) for j in range(8)], axis=1)
    post, pre = gain[0:1] + gain[1:2], gain[2:3] + gain[3:4]
    for half, (a, b) in enumerate(((at_ref, bt_ref), (ab_ref, bb_ref))):
        rows = slice(32 * half, 32 * half + 32)
        owned = p0[rows].astype(F32) + a[...].astype(F32) + b[...].astype(F32)
        factor = lax.rsqrt(jnp.mean(owned * owned, axis=1, keepdims=True) + EPS)
        res = jnp.concatenate([res_ref[j, rows].astype(F32) for j in range(8)], axis=1)
        new = (res + owned * factor * post).astype(BF)
        stream = new.astype(F32)
        for j in range(8):
            new_ref[j, rows] = stream[:, 672 * j:672 * j + 672].astype(BF)
        second = lax.rsqrt(jnp.mean(stream * stream, axis=1, keepdims=True) + EPS)
        nrm_ref[rows] = (stream * second * pre).astype(BF)


def norm(*args):
    return pl.pallas_call(
        norm_kernel,
        out_shape=[jax.ShapeDtypeStruct((8, PER, 672), BF), jax.ShapeDtypeStruct((PER, D), BF)],
        in_specs=[VM] * 6,
        out_specs=[VM] * 2,
        compiler_params=params(16),
        cost_estimate=cost(0, 1000),
        name="norm",
    )(*args)


def token_copies(where, pieces, tokens_at, n_ref, sems):
    z, c = where[0], where[1]
    copies = []
    for i, (ref, (dz, dc, part)) in enumerate(zip(pieces, tokens_at)):
        base, rows = 64 * (2 * ((z + dz) % 4) + (c + dc) % 2), 64
        if part is not None:
            base, rows = base + 32 * part, 32
        copies.append(pltpu.make_async_copy(ref, n_ref.at[pl.ds(pl.multiple_of(base, 32), rows)], sems.at[i]))
    return copies


def gelu(g):
    return 0.5 * g * (1 + jnp.tanh(0.7978845608028654 * (g + 0.044715 * (g * g * g))))


REL = (0, 3, 1, 2)


REL = (0, 3, 1, 2)
GROUP = 1408


def order(pieces, tokens_at, where):
    n = len(pieces)

    def body(*refs):
        place, o_ref, n_ref, sems = refs[n:]
        copies = token_copies(place, refs[:n], tokens_at, n_ref, sems)
        for copy in copies:
            copy.start()
        for copy in copies:
            copy.wait()
        c, y, x = place[1], place[2], place[3]

        def put(i, me, value, rows):
            rel = (i - me + 4) % 4
            slot = jnp.where(rel == 0, 0, jnp.where(rel == 3, 1, rel + 1))
            o_ref[rows, pl.ds(pl.multiple_of(GROUP * slot, 128), 1344)] = value

        @pl.loop(0, 8)
        def _(r):
            rows = pl.ds(pl.multiple_of(64 * r, 64), 64)

            @pl.when(c == 0)
            def _():
                for i in range(4):
                    put(i, y, n_ref[rows, 1344 * i:1344 * i + 1344], rows)

            @pl.when(c == 1)
            def _():
                for i in range(4):
                    cols = [1344 * k + 336 * i for k in range(4)]
                    put(i, x, jnp.concatenate([n_ref[rows, lo:lo + 336] for lo in cols], axis=1), rows)

    return pl.pallas_call(
        body,
        out_shape=jax.ShapeDtypeStruct((TOK, 4 * GROUP), BF),
        in_specs=[HB] * n + [SM],
        out_specs=VM,
        scratch_shapes=[pltpu.VMEM((TOK, D), BF), pltpu.SemaphoreType.DMA((n,))],
        compiler_params=params(40),
        cost_estimate=cost(0, 1000),
        name="order",
    )(*pieces, where)


def weight_copies(parts, where, arrays, block, w_ref, sems, width=384):
    c, y, x = where[1], where[2], where[3]
    first = jnp.where(c == 0, x, y)
    cols = pl.ds(pl.multiple_of(width * block, 128), width)
    copies = []
    for i, (array, slot, rel) in enumerate(parts):
        row = pl.multiple_of(1344 * slot + 336 * ((first + rel) % 4), 16)
        copies.append(
            pltpu.make_async_copy(arrays[array].at[:, cols], w_ref.at[pl.ds(row, 336)], sems.at[i])
        )
    return copies


def fetch_block(parts, place, arrays, w_ref, sems, width):
    j = pl.program_id(0)
    slot = lax.rem(j, 2)

    @pl.when(j == 0)
    def _():
        for copy in weight_copies(parts, place, arrays, 0, w_ref.at[0], sems.at[0], width):
            copy.start()

    @pl.when(j + 1 < 2688 // width)
    def _():
        for copy in weight_copies(parts, place, arrays, j + 1, w_ref.at[1 - slot], sems.at[1 - slot], width):
            copy.start()

    for copy in weight_copies(parts, place, arrays, j, w_ref.at[slot], sems.at[slot], width):
        copy.wait()
    return slot


def near(rows, where, blocks):
    m = len(blocks)
    parts = [(4 * g + k, g, REL[k]) for g in range(3) for k in range(4)]

    def body(*refs):
        place, n_ref, o_ref, w_ref, sems = refs[m:]
        slot = fetch_block(parts, place, refs[:m], w_ref, sems, 896)
        acc = jnp.dot(n_ref[:, :1344], w_ref[slot, :1344], preferred_element_type=F32)
        for g in (1, 2):
            lhs = n_ref[:, GROUP * g:GROUP * g + 1344]
            acc += jnp.dot(lhs, w_ref[slot, 1344 * g:1344 * g + 1344], preferred_element_type=F32)
        o_ref[...] = acc

    return pl.pallas_call(
        body,
        out_shape=jax.ShapeDtypeStruct((TOK, 2688), F32),
        grid=(3,),
        in_specs=[HB] * m + [SM, pl.BlockSpec((TOK, 3 * GROUP), lambda j: (0, 0))],
        out_specs=pl.BlockSpec((TOK, 896), lambda j: (0, j)),
        scratch_shapes=[pltpu.VMEM((2, 3 * 1344, 896), BF), pltpu.SemaphoreType.DMA((2, len(parts)))],
        compiler_params=params(56),
        cost_estimate=cost(0, 1000),
        name="near",
    )(*blocks, where, rows)


def far(rows, where, blocks, sums):
    m = len(blocks)
    parts = [(k, 0, REL[k]) for k in range(4)]

    def body(*refs):
        place, n_ref, s_ref, o_ref, w_ref, acc_ref, sems = refs[m:]
        j = pl.program_id(0)
        slot = lax.rem(j, 2)

        @pl.when(j == 0)
        def _():
            for copy in weight_copies(parts, place, refs[:m], 0, w_ref.at[0], sems.at[0]):
                copy.start()

        @pl.when(j + 1 < 7)
        def _():
            for copy in weight_copies(parts, place, refs[:m], j + 1, w_ref.at[1 - slot], sems.at[1 - slot]):
                copy.start()

        @pl.when(j < 7)
        def _():
            for copy in weight_copies(parts, place, refs[:m], j, w_ref.at[slot], sems.at[slot]):
                copy.wait()

        acc = acc_ref[1 - slot]
        last = acc[:, 256:]
        g = jnp.concatenate([acc[:, :128], last], axis=1)
        u = jnp.concatenate([acc[:, 128:256], pltpu.roll(last, 64, 1)], axis=1)
        o_ref[...] = (gelu(g) * u).T[:192].astype(BF)
        acc_ref[slot] = s_ref[...] + jnp.dot(n_ref[:, :1344], w_ref[slot], preferred_element_type=F32)

    return pl.pallas_call(
        body,
        out_shape=jax.ShapeDtypeStruct((1344, TOK), BF),
        grid=(8,),
        in_specs=[HB] * m
        + [
            SM,
            pl.BlockSpec((TOK, GROUP), lambda j: (0, 3)),
            pl.BlockSpec((TOK, 384), lambda j: (0, jnp.minimum(j, 6))),
        ],
        out_specs=pl.BlockSpec((192, TOK), lambda j: (jnp.maximum(j - 1, 0), 0)),
        scratch_shapes=[
            pltpu.VMEM((2, 1344, 384), BF),
            pltpu.VMEM((2, TOK, 384), F32),
            pltpu.SemaphoreType.DMA((2, len(parts))),
        ],
        compiler_params=params(56),
        cost_estimate=cost(2 * TOK * 1344 * 2688, 2 * 1344 * 2688 + 4 * TOK * 2688),
        name="far",
    )(*blocks, where, rows, sums)


def turn(value, by):
    return lax.dynamic_slice_in_dim(jnp.concatenate([value, value], axis=0), by % 4, 4, 0)


def swap(blocks, z, c):
    blocks = blocks.reshape(4, 2, *blocks.shape[1:])
    keep = jnp.where(c == 0, blocks[:, 0], blocks[:, 1])
    give = jnp.where(c == 0, blocks[:, 1], blocks[:, 0])
    take = shift(give, "c", 1)
    both = turn(jnp.stack([jnp.where(c == 0, keep, take), jnp.where(c == 0, take, keep)], axis=1), z)
    return [both[0], shift(both[3], "z", 3), shift(both[2], "z", 2), shift(both[1], "z", 1)]


def gather(got, z):
    got = jnp.stack(got)
    return turn(got, 4 - z).reshape(8, *got.shape[2:])


def per_device(queries, keys, values, doc_ids, out_weight, residual, post_gain, pre_gain, gate_weight, up_weight):
    y, x, z, c = (lax.axis_index(a) for a in ("y", "x", "z", "c"))
    where = jnp.stack([z, c, y, x]).astype(jnp.int32)

    kv0 = pair(keys, values)
    kv1 = behind(kv0)
    gate_weight, kv0 = lax.optimization_barrier((gate_weight, kv0))
    w = pack(gate_weight, up_weight)
    p = ring(w, -1, 0)
    kv1, w = lax.optimization_barrier((kv1, w))
    kv2 = behind(kv1)
    kv2, w_late, p = lax.optimization_barrier((kv2, w, p))
    m = ring(w_late, 1, 0)
    b = ring(p, -1, 0)
    kv2, residual, post_gain = lax.optimization_barrier((kv2, residual, post_gain))
    prev, following = [ring(w_late, 1, 1)], [ring(w, -1, 1)]

    gains = jnp.stack([post_gain, pre_gain])
    high = gains.astype(BF)
    low = (gains - high.astype(F32)).astype(BF)
    extra = jnp.stack([high[0], low[0], high[1], low[1]])
    extra = jnp.concatenate([extra, jnp.zeros((12, 672), BF)], axis=0)
    sent = jnp.concatenate([residual.reshape(8, PER, 672), jnp.broadcast_to(extra[None], (8, 16, 672))], axis=1)
    mine = gather(swap(sent, z, c), z)

    start = (4 * y + x) * TOK
    padded = jnp.concatenate([jnp.full((2 * TOK,), -1, jnp.int32), doc_ids])
    kid = lax.dynamic_slice_in_dim(padded, start, 3 * TOK, 0)[None, :]
    qid = lax.dynamic_slice_in_dim(doc_ids, start, TOK, 0)[:, None]

    queries, p, following[0] = lax.optimization_barrier((queries, p, following[0]))
    mix = attend(where, queries, kv2, kv1, kv0, qid, kid)
    other_weight = shift(out_weight, "c", 1)
    own, other = mix[0].reshape(256, 512), shift(mix[1].reshape(256, 512), "c", 1)
    other, m = lax.optimization_barrier((other, m))
    p0, p1t, p1b, p2t, p2b, p3t, p3b = project(own, other, out_weight, other_weight)

    up_t = shift(p2t, "z", 1)
    dn_b = shift(p2b, "z", -1)
    a_b = shift(p1b, "z", 1)
    b_t = shift(p3t, "z", -1)
    up_t, dn_b, mine, m, b, prev, following = lax.optimization_barrier((up_t, dn_b, mine, m, b, prev, following))
    prev += [ring(v, 1, 1) for v in (m, p, b)]
    following += [ring(v, -1, 1) for v in (m, p, b)]
    add = lambda p, q: (p.astype(F32) + q.astype(F32)).astype(BF)
    a_t = shift(add(p1t, up_t), "z", 1)
    b_b = shift(add(p3b, dn_b), "z", -1)
    p0, prev[2], following[2] = lax.optimization_barrier((p0, prev[2], following[2]))
    new, nrm = norm(p0, a_t, a_b, b_t, b_b, mine)

    n_m, n_p = shift(nrm, "z", 1), shift(nrm, "z", -1)
    n_m, n_p, prev[1], following[1] = lax.optimization_barrier((n_m, n_p, prev[1], following[1]))
    pieces = [nrm, n_m, n_p, shift(n_m[:32], "z", 1), shift(n_p[32:], "z", -1)]
    places = [(0, None), (3, None), (1, None), (2, 0), (2, 1)]
    pieces += [shift(piece, "c", 1) for piece in pieces]
    tokens_at = [(dz, dc, part) for dc in range(2) for dz, part in places]
    pieces, prev[3], following[3] = lax.optimization_barrier((pieces, prev[3], following[3]))
    rows = order(pieces, tokens_at, where)

    last = [ring(prev[0], 1, 1), ring(prev[1], 1, 1), ring(following[2], -1, 1), ring(following[3], -1, 1)]
    new, rows = lax.optimization_barrier((new, rows))
    sent_back = swap(new, z, c)
    sums = near(rows, where, [w, m, p, b, *prev, *following])
    act = far(rows, where, last, sums)
    sent_back, act = lax.optimization_barrier((sent_back, act))
    new_residual = gather(sent_back, z).reshape(TOK, 672)
    return new_residual, act.T


def solution(mesh):
    fine = Mesh(mesh.devices.reshape(4, 4, 4, 2), ("y", "x", "z", "c"))
    t, f = ("y", "x"), ("z", "c")
    in_specs = (P(t, f), P(t, f), P(t, f), P(), P(f, None), P(t, f), P(f), P(f), P(t, f), P(t, f))
    return jax.shard_map(per_device, mesh=fine, in_specs=in_specs, out_specs=(P(t, f), P(t, f)), check_vma=False)
```

```python
import jax
import jax.numpy as jnp
from jax import lax
from jax.experimental import pallas as pl
from jax.experimental.pallas import tpu as pltpu
from jax.sharding import Mesh, PartitionSpec as P

D = 5376
HD = 128
WINDOW = 1024
EPS = 1e-06
LOG2E = 1.4426950408889634
SCALE = float(168) ** -0.5
TOK = 512
PER = 64
BF = jnp.bfloat16
F32 = jnp.float32
VM = pl.BlockSpec(memory_space=pltpu.VMEM)
SM = pl.BlockSpec(memory_space=pltpu.SMEM)
HB = pl.BlockSpec(memory_space=pltpu.HBM)
MB = 1 << 20


def params(mb):
    return pltpu.CompilerParams(vmem_limit_bytes=mb * MB)


def cost(flops, nbytes, trans=0):
    return pl.CostEstimate(flops=int(flops), bytes_accessed=int(nbytes), transcendentals=int(trans))


def shift(value, axis, by):
    n = lax.axis_size(axis)
    return lax.ppermute(value, axis, [(i, (i + by) % n) for i in range(n)])


def behind(value):
    n = 16
    return lax.ppermute(value, ("y", "x"), [(i, i + 1) for i in range(n - 1)])


def pair_kernel(k_ref, v_ref, kv_ref):
    for h in range(2):
        kv_ref[:, 256 * h:256 * h + 128] = k_ref[:, 128 * h:128 * h + 128]
        kv_ref[:, 256 * h + 128:256 * h + 256] = v_ref[:, 128 * h:128 * h + 128]


def pair(keys, values):
    return pl.pallas_call(
        pair_kernel,
        out_shape=jax.ShapeDtypeStruct((TOK, 512), BF),
        in_specs=[VM] * 2,
        out_specs=VM,
        compiler_params=params(16),
        cost_estimate=cost(0, 1000),
        name="pair",
    )(keys, values)


def pack_kernel(g_ref, u_ref, o_ref):
    g, u = g_ref[...], u_ref[...]
    for j in range(7):
        lo = 192 * j
        o_ref[:, 384 * j:384 * j + 384] = jnp.concatenate(
            [g[:, lo:lo + 128], u[:, lo:lo + 128], g[:, lo + 128:lo + 192], u[:, lo + 128:lo + 192]], axis=1
        )


def pack(gate, up):
    return pl.pallas_call(
        pack_kernel,
        out_shape=jax.ShapeDtypeStruct((336, 2688), BF),
        in_specs=[VM, VM],
        out_specs=VM,
        compiler_params=params(24),
        cost_estimate=cost(0, 1000),
        name="pack",
    )(gate, up)


def ring(value, by, phase):
    pairs = []
    for y in range(4):
        for x in range(4):
            for z in range(4):
                for c in range(2):
                    along_x = (c == 0) == (phase == 0)
                    yy, xx = (y, (x + by) % 4) if along_x else ((y + by) % 4, x)
                    pairs.append((((y * 4 + x) * 4 + z) * 2 + c, ((yy * 4 + xx) * 4 + z) * 2 + c))
    return lax.ppermute(value, ("y", "x", "z", "c"), pairs)


def attend_kernel(at_ref, q_ref, kv2_ref, kv1_ref, kv0_ref, qid_ref, kid_ref, o_ref):
    z, c = at_ref[0], at_ref[1]
    for b in range(2):
        lo = 256 * b
        qid = qid_ref[lo:lo + 256, :]
        kid = kid_ref[:, lo:lo + 1280]
        row = lax.broadcasted_iota(jnp.int32, (256, 1280), 0)
        col = lax.broadcasted_iota(jnp.int32, (256, 1280), 1)
        allowed = (qid == kid) & (col > row) & (col <= row + 1024)
        outs = []
        for h in range(4):
            kc = slice(256 * (h // 2), 256 * (h // 2) + HD)
            vc = slice(256 * (h // 2) + HD, 256 * (h // 2) + 2 * HD)
            near = slice(0, 512 if b else 256)
            k = jnp.concatenate([kv2_ref[lo:, kc], kv1_ref[:, kc], kv0_ref[near, kc]], axis=0)
            v = jnp.concatenate([kv2_ref[lo:, vc], kv1_ref[:, vc], kv0_ref[near, vc]], axis=0)
            q = q_ref[lo:lo + 256, HD * h:HD * h + HD]
            s = lax.dot_general(q, k, (((1,), (1,)), ((), ())), preferred_element_type=F32)
            s = jnp.where(allowed, s * (SCALE * LOG2E), -1e30)
            top = jnp.max(s, axis=1, keepdims=True)
            e = jnp.exp2(s - top)
            total = jnp.sum(e, axis=1, keepdims=True)
            outs.append(jnp.dot(e.astype(BF), v, preferred_element_type=F32) / total)
        out = jnp.concatenate(outs, axis=1).astype(BF)
        for i in range(4):
            zz, cc = 2 * b + i // 2, i % 2
            o_ref[(cc + c) % 2, (zz - z + 4) % 4] = out[PER * i:PER * i + PER]


def attend(at, q, kv2, kv1, kv0, qid, kid):
    return pl.pallas_call(
        attend_kernel,
        out_shape=jax.ShapeDtypeStruct((2, 4, PER, 512), BF),
        in_specs=[SM] + [VM] * 6,
        out_specs=VM,
        compiler_params=params(32),
        cost_estimate=cost(0, 1000),
        name="attend",
    )(at, q, kv2, kv1, kv0, qid, kid)


def project_kernel(a, s, w_ref, ws_ref, p0, p1t, p1b, p2t, p2b, p3t, p3b):
    acc = jnp.dot(a[...], w_ref[...], preferred_element_type=F32)
    acc += jnp.dot(s[...], ws_ref[...], preferred_element_type=F32)
    out = acc.astype(BF)
    p0[...] = out[:64]
    for i, ref in enumerate((p1t, p1b, p2t, p2b, p3t, p3b)):
        ref[...] = out[64 + 32 * i:96 + 32 * i]


def project(a, s, w, ws):
    width = 768
    row = lambda r: pl.BlockSpec((r, width), lambda j: (0, j))
    full = pl.BlockSpec((256, 512), lambda j: (0, 0))
    return pl.pallas_call(
        project_kernel,
        out_shape=[jax.ShapeDtypeStruct((64, D), BF)] + [jax.ShapeDtypeStruct((32, D), BF)] * 6,
        grid=(D // width,),
        in_specs=[full] * 2 + [row(512)] * 2,
        out_specs=[row(64)] + [row(32)] * 6,
        compiler_params=params(24),
        cost_estimate=cost(0, 1000),
        name="project",
    )(a, s, w, ws)


def norm_kernel(p0, at_ref, ab_ref, bt_ref, bb_ref, res_ref, new_ref, nrm_ref):
    gain = jnp.concatenate([res_ref[j, 64:80].astype(F32) for j in range(8)], axis=1)
    post, pre = gain[0:1] + gain[1:2], gain[2:3] + gain[3:4]
    for half, (a, b) in enumerate(((at_ref, bt_ref), (ab_ref, bb_ref))):
        rows = slice(32 * half, 32 * half + 32)
        owned = p0[rows].astype(F32) + a[...].astype(F32) + b[...].astype(F32)
        factor = lax.rsqrt(jnp.mean(owned * owned, axis=1, keepdims=True) + EPS)
        res = jnp.concatenate([res_ref[j, rows].astype(F32) for j in range(8)], axis=1)
        new = (res + owned * factor * post).astype(BF)
        stream = new.astype(F32)
        for j in range(8):
            new_ref[j, rows] = stream[:, 672 * j:672 * j + 672].astype(BF)
        second = lax.rsqrt(jnp.mean(stream * stream, axis=1, keepdims=True) + EPS)
        nrm_ref[rows] = (stream * second * pre).astype(BF)


def norm(*args):
    return pl.pallas_call(
        norm_kernel,
        out_shape=[jax.ShapeDtypeStruct((8, PER, 672), BF), jax.ShapeDtypeStruct((PER, D), BF)],
        in_specs=[VM] * 6,
        out_specs=[VM] * 2,
        compiler_params=params(16),
        cost_estimate=cost(0, 1000),
        name="norm",
    )(*args)


def token_copies(where, pieces, tokens_at, n_ref, sems):
    z, c = where[0], where[1]
    copies = []
    for i, (ref, (dz, dc, part)) in enumerate(zip(pieces, tokens_at)):
        base, rows = 64 * (2 * ((z + dz) % 4) + (c + dc) % 2), 64
        if part is not None:
            base, rows = base + 32 * part, 32
        copies.append(pltpu.make_async_copy(ref, n_ref.at[pl.ds(pl.multiple_of(base, 32), rows)], sems.at[i]))
    return copies


def gelu(g):
    return 0.5 * g * (1 + jnp.tanh(0.7978845608028654 * (g + 0.044715 * (g * g * g))))


REL = (0, 3, 1, 2)


REL = (0, 3, 1, 2)
GROUP = 1408


def order(pieces, tokens_at, where):
    n = len(pieces)

    def body(*refs):
        place, o_ref, n_ref, sems = refs[n:]
        copies = token_copies(place, refs[:n], tokens_at, n_ref, sems)
        for copy in copies:
            copy.start()
        for copy in copies:
            copy.wait()
        c, y, x = place[1], place[2], place[3]

        def put(i, me, value, rows):
            rel = (i - me + 4) % 4
            slot = jnp.where(rel == 0, 0, jnp.where(rel == 3, 1, rel + 1))
            o_ref[rows, pl.ds(pl.multiple_of(GROUP * slot, 128), 1344)] = value

        @pl.loop(0, 8)
        def _(r):
            rows = pl.ds(pl.multiple_of(64 * r, 64), 64)

            @pl.when(c == 0)
            def _():
                for i in range(4):
                    put(i, y, n_ref[rows, 1344 * i:1344 * i + 1344], rows)

            @pl.when(c == 1)
            def _():
                for i in range(4):
                    cols = [1344 * k + 336 * i for k in range(4)]
                    put(i, x, jnp.concatenate([n_ref[rows, lo:lo + 336] for lo in cols], axis=1), rows)

    return pl.pallas_call(
        body,
        out_shape=jax.ShapeDtypeStruct((TOK, 4 * GROUP), BF),
        in_specs=[HB] * n + [SM],
        out_specs=VM,
        scratch_shapes=[pltpu.VMEM((TOK, D), BF), pltpu.SemaphoreType.DMA((n,))],
        compiler_params=params(40),
        cost_estimate=cost(0, 1000),
        name="order",
    )(*pieces, where)


def weight_copies(parts, where, arrays, block, w_ref, sems, width=384):
    c, y, x = where[1], where[2], where[3]
    first = jnp.where(c == 0, x, y)
    cols = pl.ds(pl.multiple_of(width * block, 128), width)
    copies = []
    for i, (array, slot, rel) in enumerate(parts):
        row = pl.multiple_of(1344 * slot + 336 * ((first + rel) % 4), 16)
        copies.append(
            pltpu.make_async_copy(arrays[array].at[:, cols], w_ref.at[pl.ds(row, 336)], sems.at[i])
        )
    return copies


def fetch_block(parts, place, arrays, w_ref, sems, width):
    j = pl.program_id(0)
    slot = lax.rem(j, 2)

    @pl.when(j == 0)
    def _():
        for copy in weight_copies(parts, place, arrays, 0, w_ref.at[0], sems.at[0], width):
            copy.start()

    @pl.when(j + 1 < 2688 // width)
    def _():
        for copy in weight_copies(parts, place, arrays, j + 1, w_ref.at[1 - slot], sems.at[1 - slot], width):
            copy.start()

    for copy in weight_copies(parts, place, arrays, j, w_ref.at[slot], sems.at[slot], width):
        copy.wait()
    return slot


def near(rows, where, blocks):
    m = len(blocks)
    parts = [(4 * g + k, g, REL[k]) for g in range(3) for k in range(4)]

    def body(*refs):
        place, n_ref, o_ref, w_ref, sems = refs[m:]
        slot = fetch_block(parts, place, refs[:m], w_ref, sems, 896)
        acc = jnp.dot(n_ref[:, :1344], w_ref[slot, :1344], preferred_element_type=F32)
        for g in (1, 2):
            lhs = n_ref[:, GROUP * g:GROUP * g + 1344]
            acc += jnp.dot(lhs, w_ref[slot, 1344 * g:1344 * g + 1344], preferred_element_type=F32)
        o_ref[...] = acc

    return pl.pallas_call(
        body,
        out_shape=jax.ShapeDtypeStruct((TOK, 2688), F32),
        grid=(3,),
        in_specs=[HB] * m + [SM, pl.BlockSpec((TOK, 3 * GROUP), lambda j: (0, 0))],
        out_specs=pl.BlockSpec((TOK, 896), lambda j: (0, j)),
        scratch_shapes=[pltpu.VMEM((2, 3 * 1344, 896), BF), pltpu.SemaphoreType.DMA((2, len(parts)))],
        compiler_params=params(56),
        cost_estimate=cost(0, 1000),
        name="near",
    )(*blocks, where, rows)


def far(rows, where, blocks, sums):
    m = len(blocks)
    parts = [(k, 0, REL[k]) for k in range(4)]

    def body(*refs):
        place, n_ref, s_ref, o_ref, w_ref, acc_ref, sems = refs[m:]
        j = pl.program_id(0)
        slot = lax.rem(j, 2)

        @pl.when(j == 0)
        def _():
            for copy in weight_copies(parts, place, refs[:m], 0, w_ref.at[0], sems.at[0]):
                copy.start()

        @pl.when(j + 1 < 7)
        def _():
            for copy in weight_copies(parts, place, refs[:m], j + 1, w_ref.at[1 - slot], sems.at[1 - slot]):
                copy.start()

        @pl.when(j < 7)
        def _():
            for copy in weight_copies(parts, place, refs[:m], j, w_ref.at[slot], sems.at[slot]):
                copy.wait()

        acc = acc_ref[1 - slot]
        last = acc[:, 256:]
        g = jnp.concatenate([acc[:, :128], last], axis=1)
        u = jnp.concatenate([acc[:, 128:256], pltpu.roll(last, 64, 1)], axis=1)
        o_ref[...] = (gelu(g) * u).T[:192].astype(BF)
        acc_ref[slot] = s_ref[...] + jnp.dot(n_ref[:, :1344], w_ref[slot], preferred_element_type=F32)

    return pl.pallas_call(
        body,
        out_shape=jax.ShapeDtypeStruct((1344, TOK), BF),
        grid=(8,),
        in_specs=[HB] * m
        + [
            SM,
            pl.BlockSpec((TOK, GROUP), lambda j: (0, 3)),
            pl.BlockSpec((TOK, 384), lambda j: (0, jnp.minimum(j, 6))),
        ],
        out_specs=pl.BlockSpec((192, TOK), lambda j: (jnp.maximum(j - 1, 0), 0)),
        scratch_shapes=[
            pltpu.VMEM((2, 1344, 384), BF),
            pltpu.VMEM((2, TOK, 384), F32),
            pltpu.SemaphoreType.DMA((2, len(parts))),
        ],
        compiler_params=params(56),
        cost_estimate=cost(2 * TOK * 1344 * 2688, 2 * 1344 * 2688 + 4 * TOK * 2688),
        name="far",
    )(*blocks, where, rows, sums)


def turn(value, by):
    return lax.dynamic_slice_in_dim(jnp.concatenate([value, value], axis=0), by % 4, 4, 0)


def swap(blocks, z, c):
    blocks = blocks.reshape(4, 2, *blocks.shape[1:])
    keep = jnp.where(c == 0, blocks[:, 0], blocks[:, 1])
    give = jnp.where(c == 0, blocks[:, 1], blocks[:, 0])
    take = shift(give, "c", 1)
    both = turn(jnp.stack([jnp.where(c == 0, keep, take), jnp.where(c == 0, take, keep)], axis=1), z)
    return [both[0], shift(both[3], "z", 3), shift(both[2], "z", 2), shift(both[1], "z", 1)]


def gather(got, z):
    got = jnp.stack(got)
    return turn(got, 4 - z).reshape(8, *got.shape[2:])


def per_device(queries, keys, values, doc_ids, out_weight, residual, post_gain, pre_gain, gate_weight, up_weight):
    y, x, z, c = (lax.axis_index(a) for a in ("y", "x", "z", "c"))
    where = jnp.stack([z, c, y, x]).astype(jnp.int32)

    kv0 = pair(keys, values)
    kv1 = behind(kv0)
    gate_weight, kv0 = lax.optimization_barrier((gate_weight, kv0))
    w = pack(gate_weight, up_weight)
    p = ring(w, -1, 0)
    kv1, w = lax.optimization_barrier((kv1, w))
    kv2 = behind(kv1)
    kv2, w_late, p = lax.optimization_barrier((kv2, w, p))
    m = ring(w_late, 1, 0)
    b = ring(p, -1, 0)
    prev, following = [ring(w_late, 1, 1)], [ring(w, -1, 1)]

    gains = jnp.stack([post_gain, pre_gain])
    high = gains.astype(BF)
    low = (gains - high.astype(F32)).astype(BF)
    extra = jnp.stack([high[0], low[0], high[1], low[1]])
    extra = jnp.concatenate([extra, jnp.zeros((12, 672), BF)], axis=0)
    sent = jnp.concatenate([residual.reshape(8, PER, 672), jnp.broadcast_to(extra[None], (8, 16, 672))], axis=1)
    mine = gather(swap(sent, z, c), z)

    start = (4 * y + x) * TOK
    padded = jnp.concatenate([jnp.full((2 * TOK,), -1, jnp.int32), doc_ids])
    kid = lax.dynamic_slice_in_dim(padded, start, 3 * TOK, 0)[None, :]
    qid = lax.dynamic_slice_in_dim(doc_ids, start, TOK, 0)[:, None]

    queries, mine, p, following[0] = lax.optimization_barrier((queries, mine, p, following[0]))
    mix = attend(where, queries, kv2, kv1, kv0, qid, kid)
    other_weight = shift(out_weight, "c", 1)
    own, other = mix[0].reshape(256, 512), shift(mix[1].reshape(256, 512), "c", 1)
    other, m = lax.optimization_barrier((other, m))
    p0, p1t, p1b, p2t, p2b, p3t, p3b = project(own, other, out_weight, other_weight)

    up_t = shift(p2t, "z", 1)
    dn_b = shift(p2b, "z", -1)
    a_b = shift(p1b, "z", 1)
    b_t = shift(p3t, "z", -1)
    up_t, dn_b, m, b, prev, following = lax.optimization_barrier((up_t, dn_b, m, b, prev, following))
    prev += [ring(v, 1, 1) for v in (m, p, b)]
    following += [ring(v, -1, 1) for v in (m, p, b)]
    add = lambda p, q: (p.astype(F32) + q.astype(F32)).astype(BF)
    a_t = shift(add(p1t, up_t), "z", 1)
    b_b = shift(add(p3b, dn_b), "z", -1)
    p0, prev[2], following[2] = lax.optimization_barrier((p0, prev[2], following[2]))
    new, nrm = norm(p0, a_t, a_b, b_t, b_b, mine)

    n_m, n_p = shift(nrm, "z", 1), shift(nrm, "z", -1)
    n_m, n_p, prev[1], following[1] = lax.optimization_barrier((n_m, n_p, prev[1], following[1]))
    pieces = [nrm, n_m, n_p, shift(n_m[:32], "z", 1), shift(n_p[32:], "z", -1)]
    places = [(0, None), (3, None), (1, None), (2, 0), (2, 1)]
    pieces += [shift(piece, "c", 1) for piece in pieces]
    tokens_at = [(dz, dc, part) for dc in range(2) for dz, part in places]
    pieces, prev[3], following[3] = lax.optimization_barrier((pieces, prev[3], following[3]))
    rows = order(pieces, tokens_at, where)

    last = [ring(prev[0], 1, 1), ring(prev[1], 1, 1), ring(following[2], -1, 1), ring(following[3], -1, 1)]
    new, rows = lax.optimization_barrier((new, rows))
    sent_back = swap(new, z, c)
    sums = near(rows, where, [w, m, p, b, *prev, *following])
    act = far(rows, where, last, sums)
    sent_back, act = lax.optimization_barrier((sent_back, act))
    new_residual = gather(sent_back, z).reshape(TOK, 672)
    return new_residual, act.T


def solution(mesh):
    fine = Mesh(mesh.devices.reshape(4, 4, 4, 2), ("y", "x", "z", "c"))
    t, f = ("y", "x"), ("z", "c")
    in_specs = (P(t, f), P(t, f), P(t, f), P(), P(f, None), P(t, f), P(f), P(f), P(t, f), P(t, f))
    return jax.shard_map(per_device, mesh=fine, in_specs=in_specs, out_specs=(P(t, f), P(t, f)), check_vma=False)
```

```python
import jax
import jax.numpy as jnp
from jax import lax
from jax.experimental import pallas as pl
from jax.experimental.pallas import tpu as pltpu
from jax.sharding import Mesh, PartitionSpec as P

D = 5376
HD = 128
WINDOW = 1024
EPS = 1e-06
LOG2E = 1.4426950408889634
SCALE = float(168) ** -0.5
TOK = 512
PER = 64
BF = jnp.bfloat16
F32 = jnp.float32
VM = pl.BlockSpec(memory_space=pltpu.VMEM)
SM = pl.BlockSpec(memory_space=pltpu.SMEM)
HB = pl.BlockSpec(memory_space=pltpu.HBM)
MB = 1 << 20


def params(mb):
    return pltpu.CompilerParams(vmem_limit_bytes=mb * MB)


def cost(flops, nbytes, trans=0):
    return pl.CostEstimate(flops=int(flops), bytes_accessed=int(nbytes), transcendentals=int(trans))


def shift(value, axis, by):
    n = lax.axis_size(axis)
    return lax.ppermute(value, axis, [(i, (i + by) % n) for i in range(n)])


def behind(value):
    n = 16
    return lax.ppermute(value, ("y", "x"), [(i, i + 1) for i in range(n - 1)])


def pair_kernel(k_ref, v_ref, kv_ref):
    for h in range(2):
        kv_ref[:, 256 * h:256 * h + 128] = k_ref[:, 128 * h:128 * h + 128]
        kv_ref[:, 256 * h + 128:256 * h + 256] = v_ref[:, 128 * h:128 * h + 128]


def pair(keys, values):
    return pl.pallas_call(
        pair_kernel,
        out_shape=jax.ShapeDtypeStruct((TOK, 512), BF),
        in_specs=[VM] * 2,
        out_specs=VM,
        compiler_params=params(16),
        cost_estimate=cost(0, 1000),
        name="pair",
    )(keys, values)


def pack_kernel(g_ref, u_ref, o_ref):
    g, u = g_ref[...], u_ref[...]
    for j in range(10):
        o_ref[:, 256 * j:256 * j + 128] = g[:, 128 * j:128 * j + 128]
        o_ref[:, 256 * j + 128:256 * j + 256] = u[:, 128 * j:128 * j + 128]
    o_ref[:, 2560:] = jnp.concatenate([g[:, 1280:], u[:, 1280:]], axis=1)


def pack(gate, up):
    return pl.pallas_call(
        pack_kernel,
        out_shape=jax.ShapeDtypeStruct((336, 2688), BF),
        in_specs=[VM, VM],
        out_specs=VM,
        compiler_params=params(24),
        cost_estimate=cost(0, 1000),
        name="pack",
    )(gate, up)


def attend_kernel(at_ref, q_ref, kv2_ref, kv1_ref, kv0_ref, qid_ref, kid_ref, o_ref):
    z, c = at_ref[0], at_ref[1]
    for b in range(2):
        lo = 256 * b
        qid = qid_ref[lo:lo + 256, :]
        kid = kid_ref[:, lo:lo + 1280]
        row = lax.broadcasted_iota(jnp.int32, (256, 1280), 0)
        col = lax.broadcasted_iota(jnp.int32, (256, 1280), 1)
        allowed = (qid == kid) & (col > row) & (col <= row + 1024)
        outs = []
        for h in range(4):
            kc = slice(256 * (h // 2), 256 * (h // 2) + HD)
            vc = slice(256 * (h // 2) + HD, 256 * (h // 2) + 2 * HD)
            near = slice(0, 512 if b else 256)
            k = jnp.concatenate([kv2_ref[lo:, kc], kv1_ref[:, kc], kv0_ref[near, kc]], axis=0)
            v = jnp.concatenate([kv2_ref[lo:, vc], kv1_ref[:, vc], kv0_ref[near, vc]], axis=0)
            q = q_ref[lo:lo + 256, HD * h:HD * h + HD]
            s = lax.dot_general(q, k, (((1,), (1,)), ((), ())), preferred_element_type=F32)
            s = jnp.where(allowed, s * (SCALE * LOG2E), -1e30)
            top = jnp.max(s, axis=1, keepdims=True)
            e = jnp.exp2(s - top)
            total = jnp.sum(e, axis=1, keepdims=True)
            outs.append(jnp.dot(e.astype(BF), v, preferred_element_type=F32) / total)
        out = jnp.concatenate(outs, axis=1).astype(BF)
        for i in range(4):
            zz, cc = 2 * b + i // 2, i % 2
            o_ref[(cc + c) % 2, (zz - z + 4) % 4] = out[PER * i:PER * i + PER]


def attend(at, q, kv2, kv1, kv0, qid, kid):
    return pl.pallas_call(
        attend_kernel,
        out_shape=jax.ShapeDtypeStruct((2, 4, PER, 512), BF),
        in_specs=[SM] + [VM] * 6,
        out_specs=VM,
        compiler_params=params(32),
        cost_estimate=cost(0, 1000),
        name="attend",
    )(at, q, kv2, kv1, kv0, qid, kid)


def project_kernel(a, s, w_ref, ws_ref, p0, p1t, p1b, p2t, p2b, p3t, p3b):
    acc = jnp.dot(a[...], w_ref[...], preferred_element_type=F32)
    acc += jnp.dot(s[...], ws_ref[...], preferred_element_type=F32)
    out = acc.astype(BF)
    p0[...] = out[:64]
    for i, ref in enumerate((p1t, p1b, p2t, p2b, p3t, p3b)):
        ref[...] = out[64 + 32 * i:96 + 32 * i]


def project(a, s, w, ws):
    width = 768
    row = lambda r: pl.BlockSpec((r, width), lambda j: (0, j))
    full = pl.BlockSpec((256, 512), lambda j: (0, 0))
    return pl.pallas_call(
        project_kernel,
        out_shape=[jax.ShapeDtypeStruct((64, D), BF)] + [jax.ShapeDtypeStruct((32, D), BF)] * 6,
        grid=(D // width,),
        in_specs=[full] * 2 + [row(512)] * 2,
        out_specs=[row(64)] + [row(32)] * 6,
        compiler_params=params(24),
        cost_estimate=cost(0, 1000),
        name="project",
    )(a, s, w, ws)


def norm_kernel(p0, at_ref, ab_ref, bt_ref, bb_ref, res_ref, new_ref, nrm_ref):
    gain = jnp.concatenate([res_ref[j, 64:80].astype(F32) for j in range(8)], axis=1)
    post, pre = gain[0:1] + gain[1:2], gain[2:3] + gain[3:4]
    for half, (a, b) in enumerate(((at_ref, bt_ref), (ab_ref, bb_ref))):
        rows = slice(32 * half, 32 * half + 32)
        owned = p0[rows].astype(F32) + a[...].astype(F32) + b[...].astype(F32)
        factor = lax.rsqrt(jnp.mean(owned * owned, axis=1, keepdims=True) + EPS)
        res = jnp.concatenate([res_ref[j, rows].astype(F32) for j in range(8)], axis=1)
        new = (res + owned * factor * post).astype(BF)
        stream = new.astype(F32)
        for j in range(8):
            new_ref[j, rows] = stream[:, 672 * j:672 * j + 672].astype(BF)
        second = lax.rsqrt(jnp.mean(stream * stream, axis=1, keepdims=True) + EPS)
        nrm_ref[rows] = (stream * second * pre).astype(BF)


def norm(*args):
    return pl.pallas_call(
        norm_kernel,
        out_shape=[jax.ShapeDtypeStruct((8, PER, 672), BF), jax.ShapeDtypeStruct((PER, D), BF)],
        in_specs=[VM] * 6,
        out_specs=[VM] * 2,
        compiler_params=params(16),
        cost_estimate=cost(0, 1000),
        name="norm",
    )(*args)


def token_copies(where, pieces, tokens_at, n_ref, sems):
    z, c = where[0], where[1]
    copies = []
    for i, (ref, (dz, dc, part)) in enumerate(zip(pieces, tokens_at)):
        base, rows = 64 * (2 * ((z + dz) % 4) + (c + dc) % 2), 64
        if part is not None:
            base, rows = base + 32 * part, 32
        copies.append(pltpu.make_async_copy(ref, n_ref.at[pl.ds(pl.multiple_of(base, 32), rows)], sems.at[i]))
    return copies


def gelu(g):
    return 0.5 * g * (1 + jnp.tanh(0.7978845608028654 * (g + 0.044715 * (g * g * g))))


REL = (0, 3, 1, 2)


def gated(pieces, tokens_at, where, w):
    n = len(pieces)

    def body(*refs):
        place, w_ref, o_ref, n_ref, sems = refs[n:]
        j = pl.program_id(0)

        @pl.when(j == 0)
        def _():
            copies = token_copies(place, refs[:n], tokens_at, n_ref, sems)
            for copy in copies:
                copy.start()
            for copy in copies:
                copy.wait()

        @pl.when(j < 10)
        def _():
            acc = jnp.dot(n_ref[...], w_ref[...], preferred_element_type=F32)
            o_ref[...] = (gelu(acc[:, :128]) * acc[:, 128:]).T.astype(BF)

        @pl.when(j == 10)
        def _():
            acc = jnp.dot(n_ref[...], w_ref[:, :128], preferred_element_type=F32)
            o_ref[...] = (gelu(acc) * pltpu.roll(acc, 64, 1)).T.astype(BF)

    return pl.pallas_call(
        body,
        out_shape=jax.ShapeDtypeStruct((1344, TOK), BF),
        grid=(11,),
        in_specs=[HB] * n + [SM, pl.BlockSpec((D, 256), lambda j: (0, j))],
        out_specs=pl.BlockSpec((128, TOK), lambda j: (j, 0)),
        scratch_shapes=[pltpu.VMEM((TOK, D), BF), pltpu.SemaphoreType.DMA((n,))],
        compiler_params=params(56),
        cost_estimate=cost(2 * TOK * D * 2688, 2 * D * 2688 + 2 * TOK * D),
        name="gated",
    )(*pieces, where, w)


def turn(value, by):
    return lax.dynamic_slice_in_dim(jnp.concatenate([value, value], axis=0), by % 4, 4, 0)


def swap(blocks, z, c):
    blocks = blocks.reshape(4, 2, *blocks.shape[1:])
    keep = jnp.where(c == 0, blocks[:, 0], blocks[:, 1])
    give = jnp.where(c == 0, blocks[:, 1], blocks[:, 0])
    take = shift(give, "c", 1)
    both = turn(jnp.stack([jnp.where(c == 0, keep, take), jnp.where(c == 0, take, keep)], axis=1), z)
    return [both[0], shift(both[3], "z", 3), shift(both[2], "z", 2), shift(both[1], "z", 1)]


def gather(got, z):
    got = jnp.stack(got)
    return turn(got, 4 - z).reshape(8, *got.shape[2:])


def per_device(queries, keys, values, doc_ids, out_weight, residual, post_gain, pre_gain, gate_weight, up_weight):
    y, x, z, c = (lax.axis_index(a) for a in ("y", "x", "z", "c"))
    where = jnp.stack([z, c, y, x]).astype(jnp.int32)

    w = pack(gate_weight, up_weight)
    w_all = lax.all_gather(w, ("y", "x"), axis=0, tiled=True)
    kv0 = pair(keys, values)
    kv1 = behind(kv0)
    kv2 = behind(kv1)

    gains = jnp.stack([post_gain, pre_gain])
    high = gains.astype(BF)
    low = (gains - high.astype(F32)).astype(BF)
    extra = jnp.stack([high[0], low[0], high[1], low[1]])
    extra = jnp.concatenate([extra, jnp.zeros((12, 672), BF)], axis=0)
    sent = jnp.concatenate([residual.reshape(8, PER, 672), jnp.broadcast_to(extra[None], (8, 16, 672))], axis=1)
    mine = gather(swap(sent, z, c), z)

    start = (4 * y + x) * TOK
    padded = jnp.concatenate([jnp.full((2 * TOK,), -1, jnp.int32), doc_ids])
    kid = lax.dynamic_slice_in_dim(padded, start, 3 * TOK, 0)[None, :]
    qid = lax.dynamic_slice_in_dim(doc_ids, start, TOK, 0)[:, None]

    queries, mine = lax.optimization_barrier((queries, mine))
    mix = attend(where, queries, kv2, kv1, kv0, qid, kid)
    other_weight = shift(out_weight, "c", 1)
    own, other = mix[0].reshape(256, 512), shift(mix[1].reshape(256, 512), "c", 1)
    p0, p1t, p1b, p2t, p2b, p3t, p3b = project(own, other, out_weight, other_weight)

    up_t = shift(p2t, "z", 1)
    dn_b = shift(p2b, "z", -1)
    a_b = shift(p1b, "z", 1)
    b_t = shift(p3t, "z", -1)
    add = lambda p, q: (p.astype(F32) + q.astype(F32)).astype(BF)
    a_t = shift(add(p1t, up_t), "z", 1)
    b_b = shift(add(p3b, dn_b), "z", -1)
    new, nrm = norm(p0, a_t, a_b, b_t, b_b, mine)

    n_m, n_p = shift(nrm, "z", 1), shift(nrm, "z", -1)
    pieces = [nrm, n_m, n_p, shift(n_m[:32], "z", 1), shift(n_p[32:], "z", -1)]
    places = [(0, None), (3, None), (1, None), (2, 0), (2, 1)]
    pieces += [shift(piece, "c", 1) for piece in pieces]
    tokens_at = [(dz, dc, part) for dc in range(2) for dz, part in places]
    new, pieces = lax.optimization_barrier((new, pieces))
    new_residual = gather(swap(new, z, c), z).reshape(TOK, 672)
    new_residual, pieces = lax.optimization_barrier((new_residual, pieces))
    return new_residual, gated(pieces, tokens_at, where, w_all).T


def solution(mesh):
    fine = Mesh(mesh.devices.reshape(4, 4, 4, 2), ("y", "x", "z", "c"))
    t, f = ("y", "x"), ("z", "c")
    in_specs = (P(t, f), P(t, f), P(t, f), P(), P(f, None), P(t, f), P(f), P(f), P(t, f), P(t, f))
    return jax.shard_map(per_device, mesh=fine, in_specs=in_specs, out_specs=(P(t, f), P(t, f)), check_vma=False)
```

```python
import jax
import jax.numpy as jnp
from jax import lax
from jax.experimental import pallas as pl
from jax.experimental.pallas import tpu as pltpu
from jax.sharding import Mesh, PartitionSpec as P

D = 5376
HD = 128
WINDOW = 1024
EPS = 1e-06
LOG2E = 1.4426950408889634
SCALE = float(168) ** -0.5
TOK = 512
PER = 64
BF = jnp.bfloat16
F32 = jnp.float32
VM = pl.BlockSpec(memory_space=pltpu.VMEM)
SM = pl.BlockSpec(memory_space=pltpu.SMEM)
HB = pl.BlockSpec(memory_space=pltpu.HBM)
MB = 1 << 20


def params(mb):
    return pltpu.CompilerParams(vmem_limit_bytes=mb * MB)


def cost(flops, nbytes, trans=0):
    return pl.CostEstimate(flops=int(flops), bytes_accessed=int(nbytes), transcendentals=int(trans))


def shift(value, axis, by):
    n = lax.axis_size(axis)
    return lax.ppermute(value, axis, [(i, (i + by) % n) for i in range(n)])


def behind(value):
    n = 16
    return lax.ppermute(value, ("y", "x"), [(i, i + 1) for i in range(n - 1)])


def pair_kernel(k_ref, v_ref, kv_ref):
    for h in range(2):
        kv_ref[:, 256 * h:256 * h + 128] = k_ref[:, 128 * h:128 * h + 128]
        kv_ref[:, 256 * h + 128:256 * h + 256] = v_ref[:, 128 * h:128 * h + 128]


def pair(keys, values):
    return pl.pallas_call(
        pair_kernel,
        out_shape=jax.ShapeDtypeStruct((TOK, 512), BF),
        in_specs=[VM] * 2,
        out_specs=VM,
        compiler_params=params(16),
        cost_estimate=cost(0, 1000),
        name="pair",
    )(keys, values)


def pack_kernel(g_ref, u_ref, o_ref):
    g, u = g_ref[...], u_ref[...]
    for j in range(7):
        lo = 192 * j
        o_ref[:, 384 * j:384 * j + 384] = jnp.concatenate(
            [g[:, lo:lo + 128], u[:, lo:lo + 128], g[:, lo + 128:lo + 192], u[:, lo + 128:lo + 192]], axis=1
        )


def pack(gate, up):
    return pl.pallas_call(
        pack_kernel,
        out_shape=jax.ShapeDtypeStruct((336, 2688), BF),
        in_specs=[VM, VM],
        out_specs=VM,
        compiler_params=params(24),
        cost_estimate=cost(0, 1000),
        name="pack",
    )(gate, up)


def ring(value, by, phase):
    pairs = []
    for y in range(4):
        for x in range(4):
            for z in range(4):
                for c in range(2):
                    along_x = (c == 0) == (phase == 0)
                    yy, xx = (y, (x + by) % 4) if along_x else ((y + by) % 4, x)
                    pairs.append((((y * 4 + x) * 4 + z) * 2 + c, ((yy * 4 + xx) * 4 + z) * 2 + c))
    return lax.ppermute(value, ("y", "x", "z", "c"), pairs)


def attend_kernel(at_ref, q_ref, kv2_ref, kv1_ref, kv0_ref, qid_ref, kid_ref, o_ref):
    z, c = at_ref[0], at_ref[1]
    for b in range(2):
        lo = 256 * b
        qid = qid_ref[lo:lo + 256, :]
        kid = kid_ref[:, lo:lo + 1280]
        row = lax.broadcasted_iota(jnp.int32, (256, 1280), 0)
        col = lax.broadcasted_iota(jnp.int32, (256, 1280), 1)
        allowed = (qid == kid) & (col > row) & (col <= row + 1024)
        outs = []
        for h in range(4):
            kc = slice(256 * (h // 2), 256 * (h // 2) + HD)
            vc = slice(256 * (h // 2) + HD, 256 * (h // 2) + 2 * HD)
            near = slice(0, 512 if b else 256)
            k = jnp.concatenate([kv2_ref[lo:, kc], kv1_ref[:, kc], kv0_ref[near, kc]], axis=0)
            v = jnp.concatenate([kv2_ref[lo:, vc], kv1_ref[:, vc], kv0_ref[near, vc]], axis=0)
            q = q_ref[lo:lo + 256, HD * h:HD * h + HD]
            s = lax.dot_general(q, k, (((1,), (1,)), ((), ())), preferred_element_type=F32)
            s = jnp.where(allowed, s * (SCALE * LOG2E), -1e30)
            top = jnp.max(s, axis=1, keepdims=True)
            e = jnp.exp2(s - top)
            total = jnp.sum(e, axis=1, keepdims=True)
            outs.append(jnp.dot(e.astype(BF), v, preferred_element_type=F32) / total)
        out = jnp.concatenate(outs, axis=1).astype(BF)
        for i in range(4):
            zz, cc = 2 * b + i // 2, i % 2
            o_ref[(cc + c) % 2, (zz - z + 4) % 4] = out[PER * i:PER * i + PER]


def attend(at, q, kv2, kv1, kv0, qid, kid):
    return pl.pallas_call(
        attend_kernel,
        out_shape=jax.ShapeDtypeStruct((2, 4, PER, 512), BF),
        in_specs=[SM] + [VM] * 6,
        out_specs=VM,
        compiler_params=params(32),
        cost_estimate=cost(0, 1000),
        name="attend",
    )(at, q, kv2, kv1, kv0, qid, kid)


def project_kernel(a, s, w_ref, ws_ref, p0, p1t, p1b, p2t, p2b, p3t, p3b):
    acc = jnp.dot(a[...], w_ref[...], preferred_element_type=F32)
    acc += jnp.dot(s[...], ws_ref[...], preferred_element_type=F32)
    out = acc.astype(BF)
    p0[...] = out[:64]
    for i, ref in enumerate((p1t, p1b, p2t, p2b, p3t, p3b)):
        ref[...] = out[64 + 32 * i:96 + 32 * i]


def project(a, s, w, ws):
    width = 768
    row = lambda r: pl.BlockSpec((r, width), lambda j: (0, j))
    full = pl.BlockSpec((256, 512), lambda j: (0, 0))
    return pl.pallas_call(
        project_kernel,
        out_shape=[jax.ShapeDtypeStruct((64, D), BF)] + [jax.ShapeDtypeStruct((32, D), BF)] * 6,
        grid=(D // width,),
        in_specs=[full] * 2 + [row(512)] * 2,
        out_specs=[row(64)] + [row(32)] * 6,
        compiler_params=params(24),
        cost_estimate=cost(0, 1000),
        name="project",
    )(a, s, w, ws)


def norm_kernel(p0, at_ref, ab_ref, bt_ref, bb_ref, res_ref, new_ref, nrm_ref):
    gain = jnp.concatenate([res_ref[j, 64:80].astype(F32) for j in range(8)], axis=1)
    post, pre = gain[0:1] + gain[1:2], gain[2:3] + gain[3:4]
    for half, (a, b) in enumerate(((at_ref, bt_ref), (ab_ref, bb_ref))):
        rows = slice(32 * half, 32 * half + 32)
        owned = p0[rows].astype(F32) + a[...].astype(F32) + b[...].astype(F32)
        factor = lax.rsqrt(jnp.mean(owned * owned, axis=1, keepdims=True) + EPS)
        res = jnp.concatenate([res_ref[j, rows].astype(F32) for j in range(8)], axis=1)
        new = (res + owned * factor * post).astype(BF)
        stream = new.astype(F32)
        for j in range(8):
            new_ref[j, rows] = stream[:, 672 * j:672 * j + 672].astype(BF)
        second = lax.rsqrt(jnp.mean(stream * stream, axis=1, keepdims=True) + EPS)
        nrm_ref[rows] = (stream * second * pre).astype(BF)


def norm(*args):
    return pl.pallas_call(
        norm_kernel,
        out_shape=[jax.ShapeDtypeStruct((8, PER, 672), BF), jax.ShapeDtypeStruct((PER, D), BF)],
        in_specs=[VM] * 6,
        out_specs=[VM] * 2,
        compiler_params=params(16),
        cost_estimate=cost(0, 1000),
        name="norm",
    )(*args)


def token_copies(where, pieces, tokens_at, n_ref, sems):
    z, c = where[0], where[1]
    copies = []
    for i, (ref, (dz, dc, part)) in enumerate(zip(pieces, tokens_at)):
        base, rows = 64 * (2 * ((z + dz) % 4) + (c + dc) % 2), 64
        if part is not None:
            base, rows = base + 32 * part, 32
        copies.append(pltpu.make_async_copy(ref, n_ref.at[pl.ds(pl.multiple_of(base, 32), rows)], sems.at[i]))
    return copies


def gelu(g):
    return 0.5 * g * (1 + jnp.tanh(0.7978845608028654 * (g + 0.044715 * (g * g * g))))


REL = (0, 3, 1, 2)


REL = (0, 3, 1, 2)
GROUP = 1408


def order(pieces, tokens_at, where):
    n = len(pieces)

    def body(*refs):
        place, o_ref, n_ref, sems = refs[n:]
        copies = token_copies(place, refs[:n], tokens_at, n_ref, sems)
        for copy in copies:
            copy.start()
        for copy in copies:
            copy.wait()
        c, y, x = place[1], place[2], place[3]

        def put(i, me, value, rows):
            rel = (i - me + 4) % 4
            slot = jnp.where(rel == 0, 0, jnp.where(rel == 3, 1, rel + 1))
            o_ref[rows, pl.ds(pl.multiple_of(GROUP * slot, 128), 1344)] = value

        @pl.loop(0, 8)
        def _(r):
            rows = pl.ds(pl.multiple_of(64 * r, 64), 64)

            @pl.when(c == 0)
            def _():
                for i in range(4):
                    put(i, y, n_ref[rows, 1344 * i:1344 * i + 1344], rows)

            @pl.when(c == 1)
            def _():
                for i in range(4):
                    cols = [1344 * k + 336 * i for k in range(4)]
                    put(i, x, jnp.concatenate([n_ref[rows, lo:lo + 336] for lo in cols], axis=1), rows)

    return pl.pallas_call(
        body,
        out_shape=jax.ShapeDtypeStruct((TOK, 4 * GROUP), BF),
        in_specs=[HB] * n + [SM],
        out_specs=VM,
        scratch_shapes=[pltpu.VMEM((TOK, D), BF), pltpu.SemaphoreType.DMA((n,))],
        compiler_params=params(40),
        cost_estimate=cost(0, 1000),
        name="order",
    )(*pieces, where)


def weight_copies(parts, where, arrays, block, w_ref, sems, width=384):
    c, y, x = where[1], where[2], where[3]
    first = jnp.where(c == 0, x, y)
    cols = pl.ds(pl.multiple_of(width * block, 128), width)
    copies = []
    for i, (array, slot, rel) in enumerate(parts):
        row = pl.multiple_of(1344 * slot + 336 * ((first + rel) % 4), 16)
        copies.append(
            pltpu.make_async_copy(arrays[array].at[:, cols], w_ref.at[pl.ds(row, 336)], sems.at[i])
        )
    return copies


def fetch_block(parts, place, arrays, w_ref, sems, width):
    j = pl.program_id(0)
    slot = lax.rem(j, 2)

    @pl.when(j == 0)
    def _():
        for copy in weight_copies(parts, place, arrays, 0, w_ref.at[0], sems.at[0], width):
            copy.start()

    @pl.when(j + 1 < 2688 // width)
    def _():
        for copy in weight_copies(parts, place, arrays, j + 1, w_ref.at[1 - slot], sems.at[1 - slot], width):
            copy.start()

    for copy in weight_copies(parts, place, arrays, j, w_ref.at[slot], sems.at[slot], width):
        copy.wait()
    return slot


def near(rows, where, blocks):
    m = len(blocks)
    parts = [(4 * g + k, g, REL[k]) for g in range(3) for k in range(4)]

    def body(*refs):
        place, n_ref, o_ref, w_ref, sems = refs[m:]
        slot = fetch_block(parts, place, refs[:m], w_ref, sems, 896)
        acc = jnp.dot(n_ref[:, :1344], w_ref[slot, :1344], preferred_element_type=F32)
        for g in (1, 2):
            lhs = n_ref[:, GROUP * g:GROUP * g + 1344]
            acc += jnp.dot(lhs, w_ref[slot, 1344 * g:1344 * g + 1344], preferred_element_type=F32)
        o_ref[...] = acc

    return pl.pallas_call(
        body,
        out_shape=jax.ShapeDtypeStruct((TOK, 2688), F32),
        grid=(3,),
        in_specs=[HB] * m + [SM, pl.BlockSpec((TOK, 3 * GROUP), lambda j: (0, 0))],
        out_specs=pl.BlockSpec((TOK, 896), lambda j: (0, j)),
        scratch_shapes=[pltpu.VMEM((2, 3 * 1344, 896), BF), pltpu.SemaphoreType.DMA((2, len(parts)))],
        compiler_params=params(56),
        cost_estimate=cost(0, 1000),
        name="near",
    )(*blocks, where, rows)


def far(rows, where, blocks, sums):
    m = len(blocks)
    parts = [(k, 0, REL[k]) for k in range(4)]

    def body(*refs):
        place, n_ref, s_ref, o_ref, w_ref, acc_ref, sems = refs[m:]
        j = pl.program_id(0)
        slot = lax.rem(j, 2)

        @pl.when(j == 0)
        def _():
            for copy in weight_copies(parts, place, refs[:m], 0, w_ref.at[0], sems.at[0]):
                copy.start()

        @pl.when(j + 1 < 7)
        def _():
            for copy in weight_copies(parts, place, refs[:m], j + 1, w_ref.at[1 - slot], sems.at[1 - slot]):
                copy.start()

        @pl.when(j < 7)
        def _():
            for copy in weight_copies(parts, place, refs[:m], j, w_ref.at[slot], sems.at[slot]):
                copy.wait()

        acc = acc_ref[1 - slot]
        last = acc[:, 256:]
        g = jnp.concatenate([acc[:, :128], last], axis=1)
        u = jnp.concatenate([acc[:, 128:256], pltpu.roll(last, 64, 1)], axis=1)
        o_ref[...] = (gelu(g) * u).T[:192].astype(BF)
        acc_ref[slot] = s_ref[...] + jnp.dot(n_ref[:, :1344], w_ref[slot], preferred_element_type=F32)

    return pl.pallas_call(
        body,
        out_shape=jax.ShapeDtypeStruct((1344, TOK), BF),
        grid=(8,),
        in_specs=[HB] * m
        + [
            SM,
            pl.BlockSpec((TOK, GROUP), lambda j: (0, 3)),
            pl.BlockSpec((TOK, 384), lambda j: (0, jnp.minimum(j, 6))),
        ],
        out_specs=pl.BlockSpec((192, TOK), lambda j: (jnp.maximum(j - 1, 0), 0)),
        scratch_shapes=[
            pltpu.VMEM((2, 1344, 384), BF),
            pltpu.VMEM((2, TOK, 384), F32),
            pltpu.SemaphoreType.DMA((2, len(parts))),
        ],
        compiler_params=params(56),
        cost_estimate=cost(2 * TOK * 1344 * 2688, 2 * 1344 * 2688 + 4 * TOK * 2688),
        name="far",
    )(*blocks, where, rows, sums)


def turn(value, by):
    return lax.dynamic_slice_in_dim(jnp.concatenate([value, value], axis=0), by % 4, 4, 0)


def swap(blocks, z, c):
    blocks = blocks.reshape(4, 2, *blocks.shape[1:])
    keep = jnp.where(c == 0, blocks[:, 0], blocks[:, 1])
    give = jnp.where(c == 0, blocks[:, 1], blocks[:, 0])
    take = shift(give, "c", 1)
    both = turn(jnp.stack([jnp.where(c == 0, keep, take), jnp.where(c == 0, take, keep)], axis=1), z)
    return [both[0], shift(both[3], "z", 3), shift(both[2], "z", 2), shift(both[1], "z", 1)]


def gather(got, z):
    got = jnp.stack(got)
    return turn(got, 4 - z).reshape(8, *got.shape[2:])


def per_device(queries, keys, values, doc_ids, out_weight, residual, post_gain, pre_gain, gate_weight, up_weight):
    y, x, z, c = (lax.axis_index(a) for a in ("y", "x", "z", "c"))
    where = jnp.stack([z, c, y, x]).astype(jnp.int32)

    kv0 = pair(keys, values)
    kv1 = behind(kv0)
    gate_weight, kv0 = lax.optimization_barrier((gate_weight, kv0))
    w = pack(gate_weight, up_weight)
    p = ring(w, -1, 0)
    kv1, w = lax.optimization_barrier((kv1, w))
    kv2 = behind(kv1)
    kv2, w_late, p = lax.optimization_barrier((kv2, w, p))
    m = ring(w_late, 1, 0)
    b = ring(p, -1, 0)
    prev, following = [ring(w_late, 1, 1)], [ring(w, -1, 1)]

    gains = jnp.stack([post_gain, pre_gain])
    high = gains.astype(BF)
    low = (gains - high.astype(F32)).astype(BF)
    extra = jnp.stack([high[0], low[0], high[1], low[1]])
    extra = jnp.concatenate([extra, jnp.zeros((12, 672), BF)], axis=0)
    sent = jnp.concatenate([residual.reshape(8, PER, 672), jnp.broadcast_to(extra[None], (8, 16, 672))], axis=1)
    mine = gather(swap(sent, z, c), z)

    start = (4 * y + x) * TOK
    padded = jnp.concatenate([jnp.full((2 * TOK,), -1, jnp.int32), doc_ids])
    kid = lax.dynamic_slice_in_dim(padded, start, 3 * TOK, 0)[None, :]
    qid = lax.dynamic_slice_in_dim(doc_ids, start, TOK, 0)[:, None]

    queries, mine, p, following[0] = lax.optimization_barrier((queries, mine, p, following[0]))
    mix = attend(where, queries, kv2, kv1, kv0, qid, kid)
    other_weight = shift(out_weight, "c", 1)
    own, other = mix[0].reshape(256, 512), shift(mix[1].reshape(256, 512), "c", 1)
    p0, p1t, p1b, p2t, p2b, p3t, p3b = project(own, other, out_weight, other_weight)

    up_t = shift(p2t, "z", 1)
    dn_b = shift(p2b, "z", -1)
    a_b = shift(p1b, "z", 1)
    b_t = shift(p3t, "z", -1)
    up_t, dn_b, m, b, prev, following = lax.optimization_barrier((up_t, dn_b, m, b, prev, following))
    prev += [ring(v, 1, 1) for v in (m, p, b)]
    following += [ring(v, -1, 1) for v in (m, p, b)]
    add = lambda p, q: (p.astype(F32) + q.astype(F32)).astype(BF)
    a_t = shift(add(p1t, up_t), "z", 1)
    b_b = shift(add(p3b, dn_b), "z", -1)
    p0, prev[2], following[2] = lax.optimization_barrier((p0, prev[2], following[2]))
    new, nrm = norm(p0, a_t, a_b, b_t, b_b, mine)

    n_m, n_p = shift(nrm, "z", 1), shift(nrm, "z", -1)
    n_m, n_p, prev[1], following[1] = lax.optimization_barrier((n_m, n_p, prev[1], following[1]))
    pieces = [nrm, n_m, n_p, shift(n_m[:32], "z", 1), shift(n_p[32:], "z", -1)]
    places = [(0, None), (3, None), (1, None), (2, 0), (2, 1)]
    pieces += [shift(piece, "c", 1) for piece in pieces]
    tokens_at = [(dz, dc, part) for dc in range(2) for dz, part in places]
    early = [ring(prev[0], 1, 1), ring(following[2], -1, 1)]
    rows = order(pieces, tokens_at, where)
    rows, prev[3], following[3], early = lax.optimization_barrier((rows, prev[3], following[3], early))

    last = [early[0], ring(prev[1], 1, 1), early[1], ring(following[3], -1, 1)]
    new, rows = lax.optimization_barrier((new, rows))
    sent_back = swap(new, z, c)
    sums = near(rows, where, [w, m, p, b, *prev, *following])
    act = far(rows, where, last, sums)
    sent_back, act = lax.optimization_barrier((sent_back, act))
    new_residual = gather(sent_back, z).reshape(TOK, 672)
    return new_residual, act.T


def solution(mesh):
    fine = Mesh(mesh.devices.reshape(4, 4, 4, 2), ("y", "x", "z", "c"))
    t, f = ("y", "x"), ("z", "c")
    in_specs = (P(t, f), P(t, f), P(t, f), P(), P(f, None), P(t, f), P(f), P(f), P(t, f), P(t, f))
    return jax.shard_map(per_device, mesh=fine, in_specs=in_specs, out_specs=(P(t, f), P(t, f)), check_vma=False)
```

```python
import jax
import jax.numpy as jnp
from jax import lax
from jax.experimental import pallas as pl
from jax.experimental.pallas import tpu as pltpu
from jax.sharding import Mesh, PartitionSpec as P

D = 5376
HD = 128
WINDOW = 1024
EPS = 1e-06
LOG2E = 1.4426950408889634
SCALE = float(168) ** -0.5
TOK = 512
PER = 64
BF = jnp.bfloat16
F32 = jnp.float32
VM = pl.BlockSpec(memory_space=pltpu.VMEM)
SM = pl.BlockSpec(memory_space=pltpu.SMEM)
HB = pl.BlockSpec(memory_space=pltpu.HBM)
MB = 1 << 20


def params(mb):
    return pltpu.CompilerParams(vmem_limit_bytes=mb * MB)


def cost(flops, nbytes, trans=0):
    return pl.CostEstimate(flops=int(flops), bytes_accessed=int(nbytes), transcendentals=int(trans))


def shift(value, axis, by):
    n = lax.axis_size(axis)
    return lax.ppermute(value, axis, [(i, (i + by) % n) for i in range(n)])


def behind(value):
    n = 16
    return lax.ppermute(value, ("y", "x"), [(i, i + 1) for i in range(n - 1)])


def pair_kernel(k_ref, v_ref, kv_ref):
    for h in range(2):
        kv_ref[:, 256 * h:256 * h + 128] = k_ref[:, 128 * h:128 * h + 128]
        kv_ref[:, 256 * h + 128:256 * h + 256] = v_ref[:, 128 * h:128 * h + 128]


def pair(keys, values):
    return pl.pallas_call(
        pair_kernel,
        out_shape=jax.ShapeDtypeStruct((TOK, 512), BF),
        in_specs=[VM] * 2,
        out_specs=VM,
        compiler_params=params(16),
        cost_estimate=cost(0, 1000),
        name="pair",
    )(keys, values)


def pack_kernel(g_ref, u_ref, o_ref):
    g, u = g_ref[...], u_ref[...]
    for j in range(7):
        lo = 192 * j
        o_ref[:, 384 * j:384 * j + 384] = jnp.concatenate(
            [g[:, lo:lo + 128], u[:, lo:lo + 128], g[:, lo + 128:lo + 192], u[:, lo + 128:lo + 192]], axis=1
        )


def pack(gate, up):
    return pl.pallas_call(
        pack_kernel,
        out_shape=jax.ShapeDtypeStruct((336, 2688), BF),
        in_specs=[VM, VM],
        out_specs=VM,
        compiler_params=params(24),
        cost_estimate=cost(0, 1000),
        name="pack",
    )(gate, up)


def ring(value, by, phase):
    pairs = []
    for y in range(4):
        for x in range(4):
            for z in range(4):
                for c in range(2):
                    along_x = (c == 0) == (phase == 0)
                    yy, xx = (y, (x + by) % 4) if along_x else ((y + by) % 4, x)
                    pairs.append((((y * 4 + x) * 4 + z) * 2 + c, ((yy * 4 + xx) * 4 + z) * 2 + c))
    return lax.ppermute(value, ("y", "x", "z", "c"), pairs)


def attend_kernel(at_ref, q_ref, kv2_ref, kv1_ref, kv0_ref, qid_ref, kid_ref, o_ref):
    z, c = at_ref[0], at_ref[1]
    for b in range(2):
        lo = 256 * b
        qid = qid_ref[lo:lo + 256, :]
        kid = kid_ref[:, lo:lo + 1280]
        row = lax.broadcasted_iota(jnp.int32, (256, 1280), 0)
        col = lax.broadcasted_iota(jnp.int32, (256, 1280), 1)
        allowed = (qid == kid) & (col > row) & (col <= row + 1024)
        outs = []
        for h in range(4):
            kc = slice(256 * (h // 2), 256 * (h // 2) + HD)
            vc = slice(256 * (h // 2) + HD, 256 * (h // 2) + 2 * HD)
            near = slice(0, 512 if b else 256)
            k = jnp.concatenate([kv2_ref[lo:, kc], kv1_ref[:, kc], kv0_ref[near, kc]], axis=0)
            v = jnp.concatenate([kv2_ref[lo:, vc], kv1_ref[:, vc], kv0_ref[near, vc]], axis=0)
            q = q_ref[lo:lo + 256, HD * h:HD * h + HD]
            s = lax.dot_general(q, k, (((1,), (1,)), ((), ())), preferred_element_type=F32)
            s = jnp.where(allowed, s * (SCALE * LOG2E), -1e30)
            top = jnp.max(s, axis=1, keepdims=True)
            e = jnp.exp2(s - top)
            total = jnp.sum(e, axis=1, keepdims=True)
            outs.append(jnp.dot(e.astype(BF), v, preferred_element_type=F32) / total)
        out = jnp.concatenate(outs, axis=1).astype(BF)
        for i in range(4):
            zz, cc = 2 * b + i // 2, i % 2
            o_ref[(cc + c) % 2, (zz - z + 4) % 4] = out[PER * i:PER * i + PER]


def attend(at, q, kv2, kv1, kv0, qid, kid):
    return pl.pallas_call(
        attend_kernel,
        out_shape=jax.ShapeDtypeStruct((2, 4, PER, 512), BF),
        in_specs=[SM] + [VM] * 6,
        out_specs=VM,
        compiler_params=params(32),
        cost_estimate=cost(0, 1000),
        name="attend",
    )(at, q, kv2, kv1, kv0, qid, kid)


def project_kernel(a, s, w_ref, ws_ref, p0, p1t, p1b, p2t, p2b, p3t, p3b):
    acc = jnp.dot(a[...], w_ref[...], preferred_element_type=F32)
    acc += jnp.dot(s[...], ws_ref[...], preferred_element_type=F32)
    out = acc.astype(BF)
    p0[...] = out[:64]
    for i, ref in enumerate((p1t, p1b, p2t, p2b, p3t, p3b)):
        ref[...] = out[64 + 32 * i:96 + 32 * i]


def project(a, s, w, ws):
    width = 768
    row = lambda r: pl.BlockSpec((r, width), lambda j: (0, j))
    full = pl.BlockSpec((256, 512), lambda j: (0, 0))
    return pl.pallas_call(
        project_kernel,
        out_shape=[jax.ShapeDtypeStruct((64, D), BF)] + [jax.ShapeDtypeStruct((32, D), BF)] * 6,
        grid=(D // width,),
        in_specs=[full] * 2 + [row(512)] * 2,
        out_specs=[row(64)] + [row(32)] * 6,
        compiler_params=params(24),
        cost_estimate=cost(0, 1000),
        name="project",
    )(a, s, w, ws)


def norm_kernel(p0, at_ref, ab_ref, bt_ref, bb_ref, res_ref, new_ref, nrm_ref):
    gain = jnp.concatenate([res_ref[j, 64:80].astype(F32) for j in range(8)], axis=1)
    post, pre = gain[0:1] + gain[1:2], gain[2:3] + gain[3:4]
    for half, (a, b) in enumerate(((at_ref, bt_ref), (ab_ref, bb_ref))):
        rows = slice(32 * half, 32 * half + 32)
        owned = p0[rows].astype(F32) + a[...].astype(F32) + b[...].astype(F32)
        factor = lax.rsqrt(jnp.mean(owned * owned, axis=1, keepdims=True) + EPS)
        res = jnp.concatenate([res_ref[j, rows].astype(F32) for j in range(8)], axis=1)
        new = (res + owned * factor * post).astype(BF)
        stream = new.astype(F32)
        for j in range(8):
            new_ref[j, rows] = stream[:, 672 * j:672 * j + 672].astype(BF)
        second = lax.rsqrt(jnp.mean(stream * stream, axis=1, keepdims=True) + EPS)
        nrm_ref[rows] = (stream * second * pre).astype(BF)


def norm(*args):
    return pl.pallas_call(
        norm_kernel,
        out_shape=[jax.ShapeDtypeStruct((8, PER, 672), BF), jax.ShapeDtypeStruct((PER, D), BF)],
        in_specs=[VM] * 6,
        out_specs=[VM] * 2,
        compiler_params=params(16),
        cost_estimate=cost(0, 1000),
        name="norm",
    )(*args)


def token_copies(where, pieces, tokens_at, n_ref, sems):
    z, c = where[0], where[1]
    copies = []
    for i, (ref, (dz, dc, part)) in enumerate(zip(pieces, tokens_at)):
        base, rows = 64 * (2 * ((z + dz) % 4) + (c + dc) % 2), 64
        if part is not None:
            base, rows = base + 32 * part, 32
        copies.append(pltpu.make_async_copy(ref, n_ref.at[pl.ds(pl.multiple_of(base, 32), rows)], sems.at[i]))
    return copies


def gelu(g):
    return 0.5 * g * (1 + jnp.tanh(0.7978845608028654 * (g + 0.044715 * (g * g * g))))


REL = (0, 3, 1, 2)


REL = (0, 3, 1, 2)
GROUP = 1408


def order(pieces, tokens_at, where):
    n = len(pieces)

    def body(*refs):
        place, o_ref, n_ref, sems = refs[n:]
        copies = token_copies(place, refs[:n], tokens_at, n_ref, sems)
        for copy in copies:
            copy.start()
        for copy in copies:
            copy.wait()
        c, y, x = place[1], place[2], place[3]

        def put(i, me, value, rows):
            rel = (i - me + 4) % 4
            slot = jnp.where(rel == 0, 0, jnp.where(rel == 3, 1, rel + 1))
            o_ref[rows, pl.ds(pl.multiple_of(GROUP * slot, 128), 1344)] = value

        @pl.loop(0, 8)
        def _(r):
            rows = pl.ds(pl.multiple_of(64 * r, 64), 64)

            @pl.when(c == 0)
            def _():
                for i in range(4):
                    put(i, y, n_ref[rows, 1344 * i:1344 * i + 1344], rows)

            @pl.when(c == 1)
            def _():
                for i in range(4):
                    cols = [1344 * k + 336 * i for k in range(4)]
                    put(i, x, jnp.concatenate([n_ref[rows, lo:lo + 336] for lo in cols], axis=1), rows)

    return pl.pallas_call(
        body,
        out_shape=jax.ShapeDtypeStruct((TOK, 4 * GROUP), BF),
        in_specs=[HB] * n + [SM],
        out_specs=VM,
        scratch_shapes=[pltpu.VMEM((TOK, D), BF), pltpu.SemaphoreType.DMA((n,))],
        compiler_params=params(40),
        cost_estimate=cost(0, 1000),
        name="order",
    )(*pieces, where)


def weight_copies(parts, where, arrays, block, w_ref, sems, width=384):
    c, y, x = where[1], where[2], where[3]
    first = jnp.where(c == 0, x, y)
    cols = pl.ds(pl.multiple_of(width * block, 128), width)
    copies = []
    for i, (array, slot, rel) in enumerate(parts):
        row = pl.multiple_of(1344 * slot + 336 * ((first + rel) % 4), 16)
        copies.append(
            pltpu.make_async_copy(arrays[array].at[:, cols], w_ref.at[pl.ds(row, 336)], sems.at[i])
        )
    return copies


def fetch_block(parts, place, arrays, w_ref, sems, width):
    j = pl.program_id(0)
    slot = lax.rem(j, 2)

    @pl.when(j == 0)
    def _():
        for copy in weight_copies(parts, place, arrays, 0, w_ref.at[0], sems.at[0], width):
            copy.start()

    @pl.when(j + 1 < 2688 // width)
    def _():
        for copy in weight_copies(parts, place, arrays, j + 1, w_ref.at[1 - slot], sems.at[1 - slot], width):
            copy.start()

    for copy in weight_copies(parts, place, arrays, j, w_ref.at[slot], sems.at[slot], width):
        copy.wait()
    return slot


def near(rows, where, blocks):
    m = len(blocks)
    parts = [(4 * g + k, g, REL[k]) for g in range(3) for k in range(4)]

    def body(*refs):
        place, n_ref, o_ref, w_ref, sems = refs[m:]
        slot = fetch_block(parts, place, refs[:m], w_ref, sems, 896)
        acc = jnp.dot(n_ref[:, :1344], w_ref[slot, :1344], preferred_element_type=F32)
        for g in (1, 2):
            lhs = n_ref[:, GROUP * g:GROUP * g + 1344]
            acc += jnp.dot(lhs, w_ref[slot, 1344 * g:1344 * g + 1344], preferred_element_type=F32)
        o_ref[...] = acc

    return pl.pallas_call(
        body,
        out_shape=jax.ShapeDtypeStruct((TOK, 2688), F32),
        grid=(3,),
        in_specs=[HB] * m + [SM, pl.BlockSpec((TOK, 3 * GROUP), lambda j: (0, 0))],
        out_specs=pl.BlockSpec((TOK, 896), lambda j: (0, j)),
        scratch_shapes=[pltpu.VMEM((2, 3 * 1344, 896), BF), pltpu.SemaphoreType.DMA((2, len(parts)))],
        compiler_params=params(56),
        cost_estimate=cost(0, 1000),
        name="near",
    )(*blocks, where, rows)


def far(rows, where, blocks, sums):
    m = len(blocks)
    parts = [(k, 0, REL[k]) for k in range(4)]

    def body(*refs):
        place, n_ref, s_ref, o_ref, w_ref, acc_ref, sems = refs[m:]
        j = pl.program_id(0)
        slot = lax.rem(j, 2)

        @pl.when(j == 0)
        def _():
            for copy in weight_copies(parts, place, refs[:m], 0, w_ref.at[0], sems.at[0]):
                copy.start()

        @pl.when(j + 1 < 7)
        def _():
            for copy in weight_copies(parts, place, refs[:m], j + 1, w_ref.at[1 - slot], sems.at[1 - slot]):
                copy.start()

        @pl.when(j < 7)
        def _():
            for copy in weight_copies(parts, place, refs[:m], j, w_ref.at[slot], sems.at[slot]):
                copy.wait()

        acc = acc_ref[1 - slot]
        last = acc[:, 256:]
        g = jnp.concatenate([acc[:, :128], last], axis=1)
        u = jnp.concatenate([acc[:, 128:256], pltpu.roll(last, 64, 1)], axis=1)
        o_ref[...] = (gelu(g) * u).T[:192].astype(BF)
        acc_ref[slot] = s_ref[...] + jnp.dot(n_ref[:, :1344], w_ref[slot], preferred_element_type=F32)

    return pl.pallas_call(
        body,
        out_shape=jax.ShapeDtypeStruct((1344, TOK), BF),
        grid=(8,),
        in_specs=[HB] * m
        + [
            SM,
            pl.BlockSpec((TOK, GROUP), lambda j: (0, 3)),
            pl.BlockSpec((TOK, 384), lambda j: (0, jnp.minimum(j, 6))),
        ],
        out_specs=pl.BlockSpec((192, TOK), lambda j: (jnp.maximum(j - 1, 0), 0)),
        scratch_shapes=[
            pltpu.VMEM((2, 1344, 384), BF),
            pltpu.VMEM((2, TOK, 384), F32),
            pltpu.SemaphoreType.DMA((2, len(parts))),
        ],
        compiler_params=params(56),
        cost_estimate=cost(2 * TOK * 1344 * 2688, 2 * 1344 * 2688 + 4 * TOK * 2688),
        name="far",
    )(*blocks, where, rows, sums)


def turn(value, by):
    return lax.dynamic_slice_in_dim(jnp.concatenate([value, value], axis=0), by % 4, 4, 0)


def swap(blocks, z, c):
    blocks = blocks.reshape(4, 2, *blocks.shape[1:])
    keep = jnp.where(c == 0, blocks[:, 0], blocks[:, 1])
    give = jnp.where(c == 0, blocks[:, 1], blocks[:, 0])
    take = shift(give, "c", 1)
    both = turn(jnp.stack([jnp.where(c == 0, keep, take), jnp.where(c == 0, take, keep)], axis=1), z)
    return [both[0], shift(both[3], "z", 3), shift(both[2], "z", 2), shift(both[1], "z", 1)]


def gather(got, z):
    got = jnp.stack(got)
    return turn(got, 4 - z).reshape(8, *got.shape[2:])


def per_device(queries, keys, values, doc_ids, out_weight, residual, post_gain, pre_gain, gate_weight, up_weight):
    y, x, z, c = (lax.axis_index(a) for a in ("y", "x", "z", "c"))
    where = jnp.stack([z, c, y, x]).astype(jnp.int32)

    kv0 = pair(keys, values)
    kv1 = behind(kv0)
    w = pack(gate_weight, up_weight)
    p = ring(w, -1, 0)
    kv1, w_late = lax.optimization_barrier((kv1, w))
    kv2 = behind(kv1)
    m = ring(w_late, 1, 0)
    b = ring(p, -1, 0)
    w_late, kv2 = lax.optimization_barrier((w_late, kv2))
    prev, following = [ring(w_late, 1, 1)], [ring(w_late, -1, 1)]

    gains = jnp.stack([post_gain, pre_gain])
    high = gains.astype(BF)
    low = (gains - high.astype(F32)).astype(BF)
    extra = jnp.stack([high[0], low[0], high[1], low[1]])
    extra = jnp.concatenate([extra, jnp.zeros((12, 672), BF)], axis=0)
    sent = jnp.concatenate([residual.reshape(8, PER, 672), jnp.broadcast_to(extra[None], (8, 16, 672))], axis=1)
    mine = gather(swap(sent, z, c), z)

    start = (4 * y + x) * TOK
    padded = jnp.concatenate([jnp.full((2 * TOK,), -1, jnp.int32), doc_ids])
    kid = lax.dynamic_slice_in_dim(padded, start, 3 * TOK, 0)[None, :]
    qid = lax.dynamic_slice_in_dim(doc_ids, start, TOK, 0)[:, None]

    queries, mine, p = lax.optimization_barrier((queries, mine, p))
    mix = attend(where, queries, kv2, kv1, kv0, qid, kid)
    other_weight = shift(out_weight, "c", 1)
    own, other = mix[0].reshape(256, 512), shift(mix[1].reshape(256, 512), "c", 1)
    other, m, following[0] = lax.optimization_barrier((other, m, following[0]))
    prev += [ring(v, 1, 1) for v in (m, p)]
    following += [ring(v, -1, 1) for v in (m, p)]
    p0, p1t, p1b, p2t, p2b, p3t, p3b = project(own, other, out_weight, other_weight)

    up_t = shift(p2t, "z", 1)
    dn_b = shift(p2b, "z", -1)
    a_b = shift(p1b, "z", 1)
    b_t = shift(p3t, "z", -1)
    up_t, dn_b, b, prev[0] = lax.optimization_barrier((up_t, dn_b, b, prev[0]))
    prev += [ring(b, 1, 1)]
    following += [ring(b, -1, 1)]
    add = lambda p, q: (p.astype(F32) + q.astype(F32)).astype(BF)
    a_t = shift(add(p1t, up_t), "z", 1)
    b_b = shift(add(p3b, dn_b), "z", -1)
    p0, prev[2], following[2] = lax.optimization_barrier((p0, prev[2], following[2]))
    new, nrm = norm(p0, a_t, a_b, b_t, b_b, mine)

    n_m, n_p = shift(nrm, "z", 1), shift(nrm, "z", -1)
    n_m, n_p, prev[1], following[1] = lax.optimization_barrier((n_m, n_p, prev[1], following[1]))
    pieces = [nrm, n_m, n_p, shift(n_m[:32], "z", 1), shift(n_p[32:], "z", -1)]
    places = [(0, None), (3, None), (1, None), (2, 0), (2, 1)]
    pieces += [shift(piece, "c", 1) for piece in pieces]
    tokens_at = [(dz, dc, part) for dc in range(2) for dz, part in places]
    pieces, prev[3], following[3] = lax.optimization_barrier((pieces, prev[3], following[3]))
    rows = order(pieces, tokens_at, where)

    last = [ring(prev[0], 1, 1), ring(prev[1], 1, 1), ring(following[2], -1, 1), ring(following[3], -1, 1)]
    new, rows = lax.optimization_barrier((new, rows))
    sent_back = swap(new, z, c)
    sums = near(rows, where, [w, m, p, b, *prev, *following])
    act = far(rows, where, last, sums)
    sent_back, act = lax.optimization_barrier((sent_back, act))
    new_residual = gather(sent_back, z).reshape(TOK, 672)
    return new_residual, act.T


def solution(mesh):
    fine = Mesh(mesh.devices.reshape(4, 4, 4, 2), ("y", "x", "z", "c"))
    t, f = ("y", "x"), ("z", "c")
    in_specs = (P(t, f), P(t, f), P(t, f), P(), P(f, None), P(t, f), P(f), P(f), P(t, f), P(t, f))
    return jax.shard_map(per_device, mesh=fine, in_specs=in_specs, out_specs=(P(t, f), P(t, f)), check_vma=False)
```

```python
import jax
import jax.numpy as jnp
from jax import lax
from jax.experimental import pallas as pl
from jax.experimental.pallas import tpu as pltpu
from jax.sharding import Mesh, PartitionSpec as P

D = 5376
HD = 128
WINDOW = 1024
EPS = 1e-06
LOG2E = 1.4426950408889634
SCALE = float(168) ** -0.5
TOK = 512
PER = 64
BF = jnp.bfloat16
F32 = jnp.float32
VM = pl.BlockSpec(memory_space=pltpu.VMEM)
SM = pl.BlockSpec(memory_space=pltpu.SMEM)
HB = pl.BlockSpec(memory_space=pltpu.HBM)
MB = 1 << 20


def params(mb):
    return pltpu.CompilerParams(vmem_limit_bytes=mb * MB)


def cost(flops, nbytes, trans=0):
    return pl.CostEstimate(flops=int(flops), bytes_accessed=int(nbytes), transcendentals=int(trans))


def shift(value, axis, by):
    n = lax.axis_size(axis)
    return lax.ppermute(value, axis, [(i, (i + by) % n) for i in range(n)])


def behind(value):
    n = 16
    return lax.ppermute(value, ("y", "x"), [(i, i + 1) for i in range(n - 1)])


def pair_kernel(k_ref, v_ref, kv_ref):
    for h in range(2):
        kv_ref[:, 256 * h:256 * h + 128] = k_ref[:, 128 * h:128 * h + 128]
        kv_ref[:, 256 * h + 128:256 * h + 256] = v_ref[:, 128 * h:128 * h + 128]


def pair(keys, values):
    return pl.pallas_call(
        pair_kernel,
        out_shape=jax.ShapeDtypeStruct((TOK, 512), BF),
        in_specs=[VM] * 2,
        out_specs=VM,
        compiler_params=params(16),
        cost_estimate=cost(0, 1000),
        name="pair",
    )(keys, values)


def pack_kernel(g_ref, u_ref, o_ref):
    g, u = g_ref[...], u_ref[...]
    for j in range(7):
        lo = 192 * j
        o_ref[:, 384 * j:384 * j + 384] = jnp.concatenate(
            [g[:, lo:lo + 128], u[:, lo:lo + 128], g[:, lo + 128:lo + 192], u[:, lo + 128:lo + 192]], axis=1
        )


def pack(gate, up):
    return pl.pallas_call(
        pack_kernel,
        out_shape=jax.ShapeDtypeStruct((336, 2688), BF),
        in_specs=[VM, VM],
        out_specs=VM,
        compiler_params=params(24),
        cost_estimate=cost(0, 1000),
        name="pack",
    )(gate, up)


def ring(value, by, phase):
    pairs = []
    for y in range(4):
        for x in range(4):
            for z in range(4):
                for c in range(2):
                    along_x = (c == 0) == (phase == 0)
                    yy, xx = (y, (x + by) % 4) if along_x else ((y + by) % 4, x)
                    pairs.append((((y * 4 + x) * 4 + z) * 2 + c, ((yy * 4 + xx) * 4 + z) * 2 + c))
    return lax.ppermute(value, ("y", "x", "z", "c"), pairs)


def attend_kernel(at_ref, q_ref, kv2_ref, kv1_ref, kv0_ref, qid_ref, kid_ref, o_ref):
    z, c = at_ref[0], at_ref[1]
    for b in range(2):
        lo = 256 * b
        qid = qid_ref[lo:lo + 256, :]
        kid = kid_ref[:, lo:lo + 1280]
        row = lax.broadcasted_iota(jnp.int32, (256, 1280), 0)
        col = lax.broadcasted_iota(jnp.int32, (256, 1280), 1)
        allowed = (qid == kid) & (col > row) & (col <= row + 1024)
        outs = []
        for h in range(4):
            kc = slice(256 * (h // 2), 256 * (h // 2) + HD)
            vc = slice(256 * (h // 2) + HD, 256 * (h // 2) + 2 * HD)
            near = slice(0, 512 if b else 256)
            k = jnp.concatenate([kv2_ref[lo:, kc], kv1_ref[:, kc], kv0_ref[near, kc]], axis=0)
            v = jnp.concatenate([kv2_ref[lo:, vc], kv1_ref[:, vc], kv0_ref[near, vc]], axis=0)
            q = q_ref[lo:lo + 256, HD * h:HD * h + HD]
            s = lax.dot_general(q, k, (((1,), (1,)), ((), ())), preferred_element_type=F32)
            s = jnp.where(allowed, s * (SCALE * LOG2E), -1e30)
            top = jnp.max(s, axis=1, keepdims=True)
            e = jnp.exp2(s - top)
            total = jnp.sum(e, axis=1, keepdims=True)
            outs.append(jnp.dot(e.astype(BF), v, preferred_element_type=F32) / total)
        out = jnp.concatenate(outs, axis=1).astype(BF)
        for i in range(4):
            zz, cc = 2 * b + i // 2, i % 2
            o_ref[(cc + c) % 2, (zz - z + 4) % 4] = out[PER * i:PER * i + PER]


def attend(at, q, kv2, kv1, kv0, qid, kid):
    return pl.pallas_call(
        attend_kernel,
        out_shape=jax.ShapeDtypeStruct((2, 4, PER, 512), BF),
        in_specs=[SM] + [VM] * 6,
        out_specs=VM,
        compiler_params=params(32),
        cost_estimate=cost(0, 1000),
        name="attend",
    )(at, q, kv2, kv1, kv0, qid, kid)


def project_kernel(a, s, w_ref, ws_ref, p0, p1t, p1b, p2t, p2b, p3t, p3b):
    acc = jnp.dot(a[...], w_ref[...], preferred_element_type=F32)
    acc += jnp.dot(s[...], ws_ref[...], preferred_element_type=F32)
    out = acc.astype(BF)
    p0[...] = out[:64]
    for i, ref in enumerate((p1t, p1b, p2t, p2b, p3t, p3b)):
        ref[...] = out[64 + 32 * i:96 + 32 * i]


def project(a, s, w, ws):
    width = 768
    row = lambda r: pl.BlockSpec((r, width), lambda j: (0, j))
    full = pl.BlockSpec((256, 512), lambda j: (0, 0))
    return pl.pallas_call(
        project_kernel,
        out_shape=[jax.ShapeDtypeStruct((64, D), BF)] + [jax.ShapeDtypeStruct((32, D), BF)] * 6,
        grid=(D // width,),
        in_specs=[full] * 2 + [row(512)] * 2,
        out_specs=[row(64)] + [row(32)] * 6,
        compiler_params=params(24),
        cost_estimate=cost(0, 1000),
        name="project",
    )(a, s, w, ws)


def norm_kernel(p0, at_ref, ab_ref, bt_ref, bb_ref, res_ref, new_ref, nrm_ref):
    gain = jnp.concatenate([res_ref[j, 64:80].astype(F32) for j in range(8)], axis=1)
    post, pre = gain[0:1] + gain[1:2], gain[2:3] + gain[3:4]
    for half, (a, b) in enumerate(((at_ref, bt_ref), (ab_ref, bb_ref))):
        rows = slice(32 * half, 32 * half + 32)
        owned = p0[rows].astype(F32) + a[...].astype(F32) + b[...].astype(F32)
        factor = lax.rsqrt(jnp.mean(owned * owned, axis=1, keepdims=True) + EPS)
        res = jnp.concatenate([res_ref[j, rows].astype(F32) for j in range(8)], axis=1)
        new = (res + owned * factor * post).astype(BF)
        stream = new.astype(F32)
        for j in range(8):
            new_ref[j, rows] = stream[:, 672 * j:672 * j + 672].astype(BF)
        second = lax.rsqrt(jnp.mean(stream * stream, axis=1, keepdims=True) + EPS)
        nrm_ref[rows] = (stream * second * pre).astype(BF)


def norm(*args):
    return pl.pallas_call(
        norm_kernel,
        out_shape=[jax.ShapeDtypeStruct((8, PER, 672), BF), jax.ShapeDtypeStruct((PER, D), BF)],
        in_specs=[VM] * 6,
        out_specs=[VM] * 2,
        compiler_params=params(16),
        cost_estimate=cost(0, 1000),
        name="norm",
    )(*args)


def token_copies(where, pieces, tokens_at, n_ref, sems):
    z, c = where[0], where[1]
    copies = []
    for i, (ref, (dz, dc, part)) in enumerate(zip(pieces, tokens_at)):
        base, rows = 64 * (2 * ((z + dz) % 4) + (c + dc) % 2), 64
        if part is not None:
            base, rows = base + 32 * part, 32
        copies.append(pltpu.make_async_copy(ref, n_ref.at[pl.ds(pl.multiple_of(base, 32), rows)], sems.at[i]))
    return copies


def gelu(g):
    return 0.5 * g * (1 + jnp.tanh(0.7978845608028654 * (g + 0.044715 * (g * g * g))))


REL = (0, 3, 1, 2)


REL = (0, 3, 1, 2)
GROUP = 1408


def order(pieces, tokens_at, where):
    n = len(pieces)

    def body(*refs):
        place, o_ref, n_ref, sems = refs[n:]
        copies = token_copies(place, refs[:n], tokens_at, n_ref, sems)
        for copy in copies:
            copy.start()
        for copy in copies:
            copy.wait()
        c, y, x = place[1], place[2], place[3]

        def put(i, me, value, rows):
            rel = (i - me + 4) % 4
            slot = jnp.where(rel == 0, 0, jnp.where(rel == 3, 1, rel + 1))
            o_ref[rows, pl.ds(pl.multiple_of(GROUP * slot, 128), 1344)] = value

        @pl.loop(0, 8)
        def _(r):
            rows = pl.ds(pl.multiple_of(64 * r, 64), 64)

            @pl.when(c == 0)
            def _():
                for i in range(4):
                    put(i, y, n_ref[rows, 1344 * i:1344 * i + 1344], rows)

            @pl.when(c == 1)
            def _():
                for i in range(4):
                    cols = [1344 * k + 336 * i for k in range(4)]
                    put(i, x, jnp.concatenate([n_ref[rows, lo:lo + 336] for lo in cols], axis=1), rows)

    return pl.pallas_call(
        body,
        out_shape=jax.ShapeDtypeStruct((TOK, 4 * GROUP), BF),
        in_specs=[HB] * n + [SM],
        out_specs=VM,
        scratch_shapes=[pltpu.VMEM((TOK, D), BF), pltpu.SemaphoreType.DMA((n,))],
        compiler_params=params(40),
        cost_estimate=cost(0, 1000),
        name="order",
    )(*pieces, where)


def weight_copies(parts, where, arrays, block, w_ref, sems, width=384):
    c, y, x = where[1], where[2], where[3]
    first = jnp.where(c == 0, x, y)
    cols = pl.ds(pl.multiple_of(width * block, 128), width)
    copies = []
    for i, (array, slot, rel) in enumerate(parts):
        row = pl.multiple_of(1344 * slot + 336 * ((first + rel) % 4), 16)
        copies.append(
            pltpu.make_async_copy(arrays[array].at[:, cols], w_ref.at[pl.ds(row, 336)], sems.at[i])
        )
    return copies


def fetch_block(parts, place, arrays, w_ref, sems, width):
    j = pl.program_id(0)
    slot = lax.rem(j, 2)

    @pl.when(j == 0)
    def _():
        for copy in weight_copies(parts, place, arrays, 0, w_ref.at[0], sems.at[0], width):
            copy.start()

    @pl.when(j + 1 < 2688 // width)
    def _():
        for copy in weight_copies(parts, place, arrays, j + 1, w_ref.at[1 - slot], sems.at[1 - slot], width):
            copy.start()

    for copy in weight_copies(parts, place, arrays, j, w_ref.at[slot], sems.at[slot], width):
        copy.wait()
    return slot


def near(rows, where, blocks):
    m = len(blocks)
    parts = [(4 * g + k, g, REL[k]) for g in range(3) for k in range(4)]

    def body(*refs):
        place, n_ref, o_ref, w_ref, sems = refs[m:]
        slot = fetch_block(parts, place, refs[:m], w_ref, sems, 896)
        acc = jnp.dot(n_ref[:, :1344], w_ref[slot, :1344], preferred_element_type=F32)
        for g in (1, 2):
            lhs = n_ref[:, GROUP * g:GROUP * g + 1344]
            acc += jnp.dot(lhs, w_ref[slot, 1344 * g:1344 * g + 1344], preferred_element_type=F32)
        o_ref[...] = acc

    return pl.pallas_call(
        body,
        out_shape=jax.ShapeDtypeStruct((TOK, 2688), F32),
        grid=(3,),
        in_specs=[HB] * m + [SM, pl.BlockSpec((TOK, 3 * GROUP), lambda j: (0, 0))],
        out_specs=pl.BlockSpec((TOK, 896), lambda j: (0, j)),
        scratch_shapes=[pltpu.VMEM((2, 3 * 1344, 896), BF), pltpu.SemaphoreType.DMA((2, len(parts)))],
        compiler_params=params(56),
        cost_estimate=cost(0, 1000),
        name="near",
    )(*blocks, where, rows)


def far(rows, where, blocks, sums):
    m = len(blocks)
    parts = [(k, 0, REL[k]) for k in range(4)]

    def body(*refs):
        place, n_ref, s_ref, o_ref, w_ref, acc_ref, sems = refs[m:]
        j = pl.program_id(0)
        slot = lax.rem(j, 2)

        @pl.when(j == 0)
        def _():
            for copy in weight_copies(parts, place, refs[:m], 0, w_ref.at[0], sems.at[0]):
                copy.start()

        @pl.when(j + 1 < 7)
        def _():
            for copy in weight_copies(parts, place, refs[:m], j + 1, w_ref.at[1 - slot], sems.at[1 - slot]):
                copy.start()

        @pl.when(j < 7)
        def _():
            for copy in weight_copies(parts, place, refs[:m], j, w_ref.at[slot], sems.at[slot]):
                copy.wait()

        acc = acc_ref[1 - slot]
        last = acc[:, 256:]
        g = jnp.concatenate([acc[:, :128], last], axis=1)
        u = jnp.concatenate([acc[:, 128:256], pltpu.roll(last, 64, 1)], axis=1)
        o_ref[...] = (gelu(g) * u).T[:192].astype(BF)
        acc_ref[slot] = s_ref[...] + jnp.dot(n_ref[:, :1344], w_ref[slot], preferred_element_type=F32)

    return pl.pallas_call(
        body,
        out_shape=jax.ShapeDtypeStruct((1344, TOK), BF),
        grid=(8,),
        in_specs=[HB] * m
        + [
            SM,
            pl.BlockSpec((TOK, GROUP), lambda j: (0, 3)),
            pl.BlockSpec((TOK, 384), lambda j: (0, jnp.minimum(j, 6))),
        ],
        out_specs=pl.BlockSpec((192, TOK), lambda j: (jnp.maximum(j - 1, 0), 0)),
        scratch_shapes=[
            pltpu.VMEM((2, 1344, 384), BF),
            pltpu.VMEM((2, TOK, 384), F32),
            pltpu.SemaphoreType.DMA((2, len(parts))),
        ],
        compiler_params=params(56),
        cost_estimate=cost(2 * TOK * 1344 * 2688, 2 * 1344 * 2688 + 4 * TOK * 2688),
        name="far",
    )(*blocks, where, rows, sums)


def turn(value, by):
    return lax.dynamic_slice_in_dim(jnp.concatenate([value, value], axis=0), by % 4, 4, 0)


def swap(blocks, z, c):
    blocks = blocks.reshape(4, 2, *blocks.shape[1:])
    keep = jnp.where(c == 0, blocks[:, 0], blocks[:, 1])
    give = jnp.where(c == 0, blocks[:, 1], blocks[:, 0])
    take = shift(give, "c", 1)
    both = turn(jnp.stack([jnp.where(c == 0, keep, take), jnp.where(c == 0, take, keep)], axis=1), z)
    return [both[0], shift(both[3], "z", 3), shift(both[2], "z", 2), shift(both[1], "z", 1)]


def gather(got, z):
    got = jnp.stack(got)
    return turn(got, 4 - z).reshape(8, *got.shape[2:])


def per_device(queries, keys, values, doc_ids, out_weight, residual, post_gain, pre_gain, gate_weight, up_weight):
    y, x, z, c = (lax.axis_index(a) for a in ("y", "x", "z", "c"))
    where = jnp.stack([z, c, y, x]).astype(jnp.int32)

    kv0 = pair(keys, values)
    kv1 = behind(kv0)
    w = pack(gate_weight, up_weight)
    p = ring(w, -1, 0)
    kv1, w_late = lax.optimization_barrier((kv1, w))
    kv2 = behind(kv1)
    m = ring(w_late, 1, 0)
    b = ring(p, -1, 0)
    w_late, kv2 = lax.optimization_barrier((w_late, kv2))
    prev, following = [ring(w_late, 1, 1)], [ring(w, -1, 1)]

    gains = jnp.stack([post_gain, pre_gain])
    high = gains.astype(BF)
    low = (gains - high.astype(F32)).astype(BF)
    extra = jnp.stack([high[0], low[0], high[1], low[1]])
    extra = jnp.concatenate([extra, jnp.zeros((12, 672), BF)], axis=0)
    sent = jnp.concatenate([residual.reshape(8, PER, 672), jnp.broadcast_to(extra[None], (8, 16, 672))], axis=1)
    mine = gather(swap(sent, z, c), z)

    start = (4 * y + x) * TOK
    padded = jnp.concatenate([jnp.full((2 * TOK,), -1, jnp.int32), doc_ids])
    kid = lax.dynamic_slice_in_dim(padded, start, 3 * TOK, 0)[None, :]
    qid = lax.dynamic_slice_in_dim(doc_ids, start, TOK, 0)[:, None]

    queries, mine, p = lax.optimization_barrier((queries, mine, p))
    mix = attend(where, queries, kv2, kv1, kv0, qid, kid)
    other_weight = shift(out_weight, "c", 1)
    own, other = mix[0].reshape(256, 512), shift(mix[1].reshape(256, 512), "c", 1)
    other, m, following[0] = lax.optimization_barrier((other, m, following[0]))
    prev += [ring(v, 1, 1) for v in (m, p)]
    following += [ring(v, -1, 1) for v in (m, p)]
    p0, p1t, p1b, p2t, p2b, p3t, p3b = project(own, other, out_weight, other_weight)

    up_t = shift(p2t, "z", 1)
    dn_b = shift(p2b, "z", -1)
    a_b = shift(p1b, "z", 1)
    b_t = shift(p3t, "z", -1)
    up_t, dn_b, b, prev[0] = lax.optimization_barrier((up_t, dn_b, b, prev[0]))
    prev += [ring(b, 1, 1)]
    following += [ring(b, -1, 1)]
    add = lambda p, q: (p.astype(F32) + q.astype(F32)).astype(BF)
    a_t = shift(add(p1t, up_t), "z", 1)
    b_b = shift(add(p3b, dn_b), "z", -1)
    p0, prev[2], following[2] = lax.optimization_barrier((p0, prev[2], following[2]))
    new, nrm = norm(p0, a_t, a_b, b_t, b_b, mine)

    n_m, n_p = shift(nrm, "z", 1), shift(nrm, "z", -1)
    n_m, n_p, prev[1], following[1] = lax.optimization_barrier((n_m, n_p, prev[1], following[1]))
    pieces = [nrm, n_m, n_p, shift(n_m[:32], "z", 1), shift(n_p[32:], "z", -1)]
    places = [(0, None), (3, None), (1, None), (2, 0), (2, 1)]
    pieces += [shift(piece, "c", 1) for piece in pieces]
    tokens_at = [(dz, dc, part) for dc in range(2) for dz, part in places]
    pieces, prev[3], following[3] = lax.optimization_barrier((pieces, prev[3], following[3]))
    rows = order(pieces, tokens_at, where)

    last = [ring(prev[0], 1, 1), ring(prev[1], 1, 1), ring(following[2], -1, 1), ring(following[3], -1, 1)]
    new, rows = lax.optimization_barrier((new, rows))
    sent_back = swap(new, z, c)
    sums = near(rows, where, [w, m, p, b, *prev, *following])
    act = far(rows, where, last, sums)
    sent_back, act = lax.optimization_barrier((sent_back, act))
    new_residual = gather(sent_back, z).reshape(TOK, 672)
    return new_residual, act.T


def solution(mesh):
    fine = Mesh(mesh.devices.reshape(4, 4, 4, 2), ("y", "x", "z", "c"))
    t, f = ("y", "x"), ("z", "c")
    in_specs = (P(t, f), P(t, f), P(t, f), P(), P(f, None), P(t, f), P(f), P(f), P(t, f), P(t, f))
    return jax.shard_map(per_device, mesh=fine, in_specs=in_specs, out_specs=(P(t, f), P(t, f)), check_vma=False)
```
